32 devices in a mesh: groups: 2 (over y), lat: 8 (over z, x), lon: 2 (over core).
Axes of the slice: x: 2, y: 2, z: 4, core: 2. Of those that a mesh axis runs over, the one named last changes fastest.
Arguments:
- tokens: bfloat16 [16, 256, 768], P(('groups', 'lat'), 'lon'), parts along dimension 0, may hold values from -5 to 5
- gain_attn: float32 [768], replicated, may hold values from 0.25 to 1.75
- w_qkv: bfloat16 [768, 2304], P('lat'), may hold values from -0.048353085 to 0.048353085
- key_bias: bfloat16 [8, 12, 256], P('lat', None, 'lon'), may hold values from -3 to 250
- w_out: bfloat16 [768, 768], P('lat'), may hold values from -0.21875 to 0.21875
- gain_conv: float32 [768], replicated, may hold values from 0.25 to 1.75
- w_conv: bfloat16 [2, 768, 64], replicated, may hold values from -0.75 to 0.75
- lat_taps: float32 [16, 2], replicated, may hold values from -2 to 2
- lon_half: int32 [8], P('lat'), may hold values from 1 to 128, as said below
- lat_half: int32 [8], P('lat'), may hold values from 0 to 1, as said below
- quad_off: int32 [8], P('lat'), may hold values from 0 to 13
Outputs:
- updated: bfloat16 [16, 256, 768], P(('groups', 'lat'), 'lon'), parts along dimension 0
The draws below stay inside these ranges and needn't reach their ends.
There are 2 independent parts, one for each index of `groups`. The reference program is written for one: setup_inputs(seed, part) draws one part's arguments, and reference() takes and returns one part's arrays. A program takes and returns all parts, laid end to end along the dimension named above; an argument that names none is the same for every part. Nothing has to cross between parts.
Inputs may be any that keep to these rules, and one draw needn't show every extreme that they name: `lon_half`: the bands at either pole reach 128. `lat_half`: both polar bands have 1.
All inputs are finite; a program needn't handle non-finite values.
Results may differ from the reference program's by a relative error of at most 0.008.
Values may be sent and summed in bfloat16 or wider, within the bound.
No kernel may reach another device: no remote copies, remote signals or barrier semaphores. Data moves between devices by JAX's collectives and lax.ppermute only.
A program may use at most 64 MiB of HBM per device.

```python
import math
import jax
import jax.numpy as jnp
from jax import lax

D = 768
H = 12
DH = 64
GW = 64
KB = 2
TAPS = 16
NLON = 256
NLAT = 8


def draw_tokens(key, part):
    col_key, main_key, base_key, wave_key = jax.random.split(key, 4)
    lon_angle = 2.0 * math.pi / NLON * jnp.arange(NLON, dtype=jnp.float32)
    first_cos = jnp.cos(lon_angle)[None, :, None]
    first_sin = jnp.sin(lon_angle)[None, :, None]
    wave_coef = jax.random.normal(wave_key, (4, NLAT, 1, D), jnp.float32)
    col_scale = jnp.exp(jax.random.uniform(col_key, (D,), jnp.float32, math.log(0.2), math.log(2.0)))
    rough_part = jnp.clip(jax.random.normal(main_key, (NLAT, NLON, D), jnp.float32), -3.0, 3.0) * col_scale
    base_part = 0.9 * jax.random.normal(base_key, (NLAT, 1, D), jnp.float32)
    smooth_part = 0.4 * (wave_coef[0] * first_cos + wave_coef[1] * first_sin)
    values = rough_part + base_part + smooth_part
    return jnp.clip(values, -5.0, 5.0).astype(jnp.bfloat16)


def draw_w_qkv(key, part):
    sign_key, size_key = jax.random.split(jax.random.fold_in(key, 23), 2)
    sign_flip = 2.0 * jax.random.randint(sign_key, (D, 3 * D), 0, 2).astype(jnp.float32) - 1.0
    jitter = jax.random.uniform(size_key, (D, 3 * D), jnp.float32, 1.1, 1.3)
    return (sign_flip * jitter * float(D) ** (-0.5)).astype(jnp.bfloat16)


def draw_key_bias(key, part):
    base_key = jax.random.fold_in(key, 0)
    values = jnp.clip(0.6 * jax.random.normal(base_key, (NLAT, H, NLON), jnp.float32), -3.0, 3.0)
    return values.astype(jnp.bfloat16)


def draw_lat_taps(key, part):
    sign_key, size_key = jax.random.split(key)
    sign_flip = 2.0 * jax.random.randint(sign_key, (TAPS, KB), 0, 2).astype(jnp.float32) - 1.0
    magnitude = jax.random.uniform(size_key, (TAPS, KB), jnp.float32, 0.8, 2.0)
    return sign_flip * magnitude


def draw_lon_half(key, part):
    factor = jax.random.randint(key, (NLAT,), 4, 8)
    band_ids = jnp.arange(NLAT, dtype=jnp.int32)
    from_pole = jnp.minimum(band_ids, NLAT - 1 - band_ids)
    widths = factor * NLON * NLAT // (128 * (2 * from_pole + 1))
    widths = jnp.where(from_pole == 0, NLON // 2, widths)
    return jnp.clip(widths, 1, NLON // 2)


def draw_lat_half(key, part):
    pick_key, zero_key = jax.random.split(jax.random.fold_in(key, 11))
    picked = jax.random.randint(pick_key, (NLAT,), 0, 2)
    band_ids = jnp.arange(NLAT, dtype=jnp.int32)
    centre = NLAT // 2
    near_centre = jnp.abs(band_ids - centre) <= 1
    zero_band = jax.random.randint(zero_key, (), 1, NLAT - 4)
    zero_band = jnp.where(zero_band >= centre - 1, zero_band + 3, zero_band)
    picked = jnp.where(near_centre, 1, picked)
    picked = jnp.where(band_ids == zero_band, 0, picked)
    at_pole = (band_ids == 0) | (band_ids == NLAT - 1)
    return jnp.where(at_pole, 1, picked)


def set_ends(values, rng, least, top_value):
    longest = values.shape.index(max(values.shape))
    spots = []
    for shift in (0, 1):
        where = [jax.random.randint(jax.random.fold_in(rng, axis), (), 0, length) for axis, length in enumerate(values.shape)]
        where[longest] = (where[longest] + shift) % values.shape[longest]
        spots.append(tuple(where))
    return values.at[spots[0]].set(least).at[spots[1]].set(top_value)


def level_of(own_key, dims, pieces, least, high):
    def one(dim, blocks):
        draws = jax.random.uniform(jax.random.fold_in(jax.random.fold_in(own_key, 6), dim), (blocks,), jnp.float32, least / len(pieces), high / len(pieces))
        return jnp.repeat(jnp.exp(draws), dims[dim] // blocks).reshape((-1,) + (1,) * (len(dims) - dim - 1))

    loudness = one(*pieces[0])
    for cut in pieces[1:]:
        loudness = loudness * one(*cut)
    return loudness


def normal_values(stream_key, shape, width, most, cuts=(), held_as=jnp.bfloat16):
    level = level_of(stream_key, shape, cuts, -0.22, 0.18) if cuts else 1.0
    drawn = jax.random.normal(stream_key, shape, jnp.float32) * width * level
    return jnp.minimum(jnp.maximum(drawn, -most), most).astype(held_as)


def setup_inputs(seed: int = 0, part: int = 0) -> dict:
    arg_keys = jax.random.split(jax.random.key(seed), 12)
    part_keys = jax.random.split(jax.random.fold_in(arg_keys[11], part), 12)
    tokens = draw_tokens(jax.random.fold_in(jax.random.fold_in(arg_keys[11], part), 71), part)
    gain_attn = jnp.clip(1.0 + 0.15 * jax.random.normal(arg_keys[1], (D,), jnp.float32), 0.25, 1.75)
    w_qkv = draw_w_qkv(jax.random.fold_in(arg_keys[11], 71), part)
    key_bias = draw_key_bias(jax.random.fold_in(arg_keys[11], 71), part)
    w_out = normal_values(arg_keys[4], (D, D), D ** -0.5, 0.21875, ((0, 8),))
    gain_conv = jnp.clip(1.0 + 0.15 * jax.random.normal(arg_keys[5], (D,), jnp.float32), 0.25, 1.75)
    w_conv = normal_values(arg_keys[6], (KB, D, GW), GW ** -0.5, 0.75)
    lat_taps = draw_lat_taps(jax.random.fold_in(arg_keys[11], 71), part)
    lon_half = draw_lon_half(jax.random.fold_in(arg_keys[11], 71), part)
    lat_half = draw_lat_half(jax.random.fold_in(arg_keys[11], 71), part)
    quad_off = set_ends(jax.random.randint(arg_keys[10], (NLAT,), 0, TAPS - 2), jax.random.fold_in(arg_keys[10], 1), 0, (TAPS - 2) - 1).astype(jnp.int32)
    return dict(tokens=tokens, gain_attn=gain_attn, w_qkv=w_qkv, key_bias=key_bias, w_out=w_out, gain_conv=gain_conv, w_conv=w_conv, lat_taps=lat_taps, lon_half=lon_half, lat_half=lat_half, quad_off=quad_off)


def layer_norm(inputs, gain):
    values = inputs.astype(jnp.float32)
    average = lax.optimization_barrier(jnp.mean(values, axis=-1, keepdims=True))
    centered = values - average
    variance = lax.optimization_barrier(jnp.mean(centered * centered, axis=-1, keepdims=True))
    return centered * lax.rsqrt(variance + 1e-05) * gain

def group_mix(inputs, w_conv):
    basis, length, channels = inputs.shape
    group_width = w_conv.shape[2]
    groups = channels // group_width
    mixed_rows = jnp.einsum('kjgc,kgce->kjge', inputs.reshape(basis, length, groups, group_width).astype(jnp.float32), w_conv.reshape(basis, groups, group_width, group_width).astype(jnp.float32))
    return mixed_rows.reshape(basis, length, channels).astype(jnp.bfloat16)

def lon_weights(row_ids, col_ids, half_width, lon_total):
    offset_lon = jnp.mod(col_ids[None, :] - row_ids[:, None] + lon_total // 2, lon_total) - lon_total // 2
    distance = jnp.abs(offset_lon).astype(jnp.float32)
    span_plus = (half_width + 1).astype(jnp.float32)
    tent_weight = jnp.where(distance <= half_width.astype(jnp.float32), (1.0 - distance / span_plus) / span_plus, 0.0)
    odd_weight = tent_weight * offset_lon.astype(jnp.float32) / span_plus
    return jnp.stack([tent_weight, odd_weight]).astype(jnp.bfloat16)

def reference(tokens, gain_attn, w_qkv, key_bias, w_out, gain_conv, w_conv, lat_taps, lon_half, lat_half, quad_off):
    score_scale = DH ** (-0.5)

    def attend_row(inputs):
        band_tokens, band_bias = inputs
        normed = layer_norm(band_tokens, gain_attn).astype(jnp.bfloat16)
        projected = jnp.dot(normed, w_qkv, preferred_element_type=jnp.float32).astype(jnp.bfloat16)
        queries = projected[:, :D].reshape(NLON, H, DH).astype(jnp.float32)
        key_rows = projected[:, D:2 * D].reshape(NLON, H, DH).astype(jnp.float32)
        value_rows = projected[:, 2 * D:].reshape(NLON, H, DH).astype(jnp.float32)
        scores = jnp.einsum('qhd,khd->hqk', queries, key_rows) * score_scale + band_bias.astype(jnp.float32)[:, None, :]
        exp_scores = jnp.exp(scores - lax.optimization_barrier(jnp.max(scores, axis=-1, keepdims=True)))
        totals = lax.optimization_barrier(jnp.sum(exp_scores, axis=-1))
        weighted = jnp.einsum('hqk,khd->qhd', exp_scores.astype(jnp.bfloat16).astype(jnp.float32), value_rows)
        attended = (weighted / totals.T[:, :, None]).reshape(NLON, D).astype(jnp.bfloat16)
        return (band_tokens.astype(jnp.float32) + jnp.dot(attended, w_out, preferred_element_type=jnp.float32)).astype(jnp.bfloat16)
    middle = lax.map(attend_row, (tokens, key_bias))
    conv_in = lax.map(lambda band_rows: layer_norm(band_rows, gain_conv).astype(jnp.bfloat16), middle)
    zero_row = jnp.zeros((1, NLON, D), jnp.bfloat16)
    padded = jnp.concatenate([zero_row, conv_in, zero_row], axis=0)
    offsets = jnp.arange(3, dtype=jnp.int32) - 1
    lon_ids = jnp.arange(NLON, dtype=jnp.int32)

    def conv_row(band_index):
        stacked = lax.dynamic_slice_in_dim(padded, band_index, 3, 0)
        tap_vals = lat_taps[quad_off[band_index] + offsets + 1]
        tap_vals = jnp.where((jnp.abs(offsets) <= lat_half[band_index])[:, None], tap_vals, 0.0)
        summed = jnp.einsum('rk,rjd->kjd', tap_vals, stacked.astype(jnp.float32), precision=lax.Precision.HIGHEST).astype(jnp.bfloat16)
        own_row = lax.dynamic_index_in_dim(conv_in, band_index, 0, keepdims=False)
        pole_gain = jnp.where(band_index == 0, tap_vals[0], 0.0) + jnp.where(band_index == NLAT - 1, tap_vals[2], 0.0)
        pole_rows = (pole_gain[:, None, None] * own_row.astype(jnp.float32)[None]).astype(jnp.bfloat16)
        mixed_rows = group_mix(summed, w_conv)
        pole_mixed = group_mix(pole_rows, w_conv)
        blended = (mixed_rows.astype(jnp.float32) + jnp.roll(pole_mixed, -(NLON // 2), axis=1).astype(jnp.float32)).astype(jnp.bfloat16)
        coeffs = lon_weights(lon_ids, lon_ids, lon_half[band_index], NLON)
        conv_out = jnp.einsum('kjc,kcd->jd', coeffs.astype(jnp.float32), blended.astype(jnp.float32))
        own_mid = lax.dynamic_index_in_dim(middle, band_index, 0, keepdims=False)
        return (own_mid.astype(jnp.float32) + conv_out).astype(jnp.bfloat16)
    return lax.map(conv_row, jnp.arange(NLAT, dtype=jnp.int32))
```

```python
import jax
import jax.numpy as jnp
from jax import lax
from jax.sharding import PartitionSpec as P


def padded(cells, sides, width):
    for axis, dim in sides:
        count = lax.axis_size(axis)
        ends = count - 1
        head = lax.slice_in_dim(cells, 0, width, axis=dim)
        tail = lax.slice_in_dim(cells, cells.shape[dim] - width, cells.shape[dim], axis=dim)
        cells = jnp.concatenate(
            [
                lax.ppermute(tail, axis, [(i, (i + 1) % count) for i in range(ends)]),
                cells,
                lax.ppermute(head, axis, [((i + 1) % count, i) for i in range(ends)]),
            ],
            axis=dim,
        )
    return cells


def layer_norm(inputs, gain):
    values = inputs.astype(jnp.float32)
    average = jnp.mean(values, axis=-1, keepdims=True)
    centered = values - average
    variance = jnp.mean(centered * centered, axis=-1, keepdims=True)
    return centered * lax.rsqrt(variance + 1e-05) * gain


def group_mix(inputs, w_conv):
    basis, length, channels = inputs.shape
    group_width = w_conv.shape[2]
    groups = channels // group_width
    mixed_rows = jnp.einsum(
        "kjgc,kgce->kjge",
        inputs.reshape(basis, length, groups, group_width),
        w_conv.reshape(basis, groups, group_width, group_width),
        preferred_element_type=jnp.float32,
    )
    return mixed_rows.reshape(basis, length, channels).astype(jnp.bfloat16)


def lon_weights(row_ids, col_ids, half_width, lon_total):
    offset_lon = (
        jnp.mod(col_ids[None, :] - row_ids[:, None] + lon_total // 2, lon_total) - lon_total // 2
    )
    distance = jnp.abs(offset_lon).astype(jnp.float32)
    span_plus = (half_width + 1).astype(jnp.float32)
    tent_weight = jnp.where(
        distance <= half_width.astype(jnp.float32), (1.0 - distance / span_plus) / span_plus, 0.0
    )
    odd_weight = tent_weight * offset_lon.astype(jnp.float32) / span_plus
    return jnp.stack([tent_weight, odd_weight]).astype(jnp.bfloat16)


def start_state(query_count, head_count, head_dim):
    running_max = jnp.full((head_count, query_count), -jnp.inf, jnp.float32)
    running_sum = jnp.zeros((head_count, query_count), jnp.float32)
    running_out = jnp.zeros((query_count, head_count, head_dim), jnp.float32)
    return (running_max, running_sum, running_out)


def attend_keys(carry_state, queries, key_rows, value_rows, bias_rows, score_scale):
    key_count = key_rows.shape[0]
    for offset in range(0, key_count, 128):
        running_max, running_sum, running_out = carry_state
        key_block = key_rows[offset : offset + 128]
        value_block = value_rows[offset : offset + 128]
        bias_block = bias_rows[offset : offset + 128]
        scores = (
            jnp.einsum("qhd,khd->hqk", queries, key_block, preferred_element_type=jnp.float32)
            * score_scale
        )
        scores = scores + bias_block.T.astype(jnp.float32)[:, None, :]
        new_max = jnp.maximum(running_max, jnp.max(scores, axis=-1))
        rescale = jnp.exp(running_max - new_max)
        exp_scores = jnp.exp(scores - new_max[:, :, None])
        running_sum = running_sum * rescale + jnp.sum(exp_scores, axis=-1)
        running_out = running_out * rescale.T[:, :, None] + jnp.einsum(
            "hqk,khd->qhd",
            exp_scores.astype(jnp.bfloat16),
            value_block,
            preferred_element_type=jnp.float32,
        )
        carry_state = (new_max, running_sum, running_out)
    return carry_state


def finish_state(carry_state):
    running_max, running_sum, running_out = carry_state
    finished = running_out / running_sum.T[:, :, None]
    return finished.reshape(finished.shape[0], -1).astype(jnp.bfloat16)


def lon_conv(blended, half_width, first_col, out_cols):
    lon_total = blended.shape[1]
    block_cols = min(128, lon_total)
    block_count = lon_total // block_cols
    first_block = jnp.floor_divide(first_col - half_width, block_cols)
    last_block = jnp.floor_divide(first_col + out_cols - 1 + half_width, block_cols)
    turn_count = jnp.minimum(block_count, last_block - first_block + 1)
    row_ids = first_col + jnp.arange(out_cols, dtype=jnp.int32)

    def add_block(turn_index, running_out):
        block_at = jnp.mod(first_block + turn_index, block_count)
        lon_block = lax.dynamic_slice_in_dim(blended, block_at * block_cols, block_cols, 1)
        col_ids = block_at * block_cols + jnp.arange(block_cols, dtype=jnp.int32)
        coeffs = lon_weights(row_ids, col_ids, half_width, lon_total)
        return running_out + jnp.einsum(
            "kjc,kcd->jd", coeffs, lon_block, preferred_element_type=jnp.float32
        )

    initial = jnp.zeros((out_cols, blended.shape[2]), jnp.float32)
    return lax.fori_loop(0, turn_count, add_block, initial)


def gather_weights(w_qkv, w_out, lon_place):
    lat_count = lax.axis_size("lat")
    rows = w_qkv.shape[0]
    half = rows // 2
    qkv_width = w_qkv.shape[1]
    both = jnp.concatenate([w_qkv, w_out], axis=1)
    mine = lax.dynamic_slice_in_dim(both, lon_place * half, half, 0)
    spread = jnp.broadcast_to(mine[None], (lat_count,) + mine.shape)
    got = lax.all_to_all(spread, "lat", 0, 0, tiled=False)
    pair = lax.all_gather(got, "lon", axis=1, tiled=True)
    full = pair.reshape(lat_count * rows, both.shape[1])
    return full[:, :qkv_width], full[:, qkv_width:]


def per_device(
    tokens,
    gain_attn,
    w_qkv,
    key_bias,
    w_out,
    gain_conv,
    w_conv,
    lat_taps,
    lon_half,
    lat_half,
    quad_off,
):
    own_tokens = tokens[0]
    count_lon, model_width = own_tokens.shape
    head_count = key_bias.shape[1]
    head_dim = model_width // head_count
    score_scale = head_dim ** (-0.5)
    lon_place = lax.axis_index("lon")
    normed = layer_norm(own_tokens, gain_attn).astype(jnp.bfloat16)
    bias_rows = key_bias[0].T
    full_qkv, full_out = gather_weights(w_qkv, w_out, lon_place)
    projected = jnp.dot(normed, full_qkv, preferred_element_type=jnp.float32).astype(jnp.bfloat16)
    queries = projected[:, :model_width].reshape(count_lon, head_count, head_dim)
    key_here = projected[:, model_width : 2 * model_width]
    value_here = projected[:, 2 * model_width :]
    key_piece = lax.all_gather(key_here, "lon", axis=0, tiled=True)
    value_piece = lax.all_gather(value_here, "lon", axis=0, tiled=True)
    bias_piece = lax.all_gather(bias_rows, "lon", axis=0, tiled=True)
    length = key_piece.shape[0]
    carry_state = attend_keys(
        start_state(count_lon, head_count, head_dim),
        queries,
        key_piece.reshape(length, head_count, head_dim),
        value_piece.reshape(length, head_count, head_dim),
        bias_piece,
        score_scale,
    )
    attended = finish_state(carry_state)
    branch_out = jnp.dot(attended, full_out, preferred_element_type=jnp.float32)
    middle = (own_tokens.astype(jnp.float32) + branch_out).astype(jnp.bfloat16)
    conv_in = layer_norm(middle, gain_conv).astype(jnp.bfloat16)
    stacked = padded(conv_in[None], (("lat", 0),), 1)
    lat_row = lax.axis_index("lat")
    last_band = lax.axis_size("lat") - 1
    offsets = jnp.arange(3, dtype=jnp.int32) - 1
    one_hot = (
        (quad_off[0] + offsets + 1)[:, None]
        == jnp.arange(lat_taps.shape[0], dtype=jnp.int32)[None, :]
    ).astype(jnp.float32)
    tap_vals = jnp.dot(one_hot, lat_taps, precision=lax.Precision.HIGHEST)
    tap_vals = jnp.where((jnp.abs(offsets) <= lat_half[0])[:, None], tap_vals, 0.0)
    summed = jnp.einsum(
        "rk,rjd->kjd", tap_vals, stacked.astype(jnp.float32), precision=lax.Precision.HIGHEST
    ).astype(jnp.bfloat16)
    pole_gain = jnp.where(lat_row == 0, tap_vals[0], 0.0) + jnp.where(
        lat_row == last_band, tap_vals[2], 0.0
    )
    first_col = lon_place * count_lon
    pole_rows = (pole_gain[:, None, None] * conv_in.astype(jnp.float32)[None]).astype(jnp.bfloat16)
    mixed_rows = group_mix(summed, w_conv)
    pole_mixed = group_mix(pole_rows, w_conv)
    circle_rows, pole_all = (
        lax.all_gather(mixed_rows, "lon", axis=1, tiled=True),
        lax.all_gather(pole_mixed, "lon", axis=1, tiled=True),
    )
    lon_total = circle_rows.shape[1]
    blended = (
        circle_rows.astype(jnp.float32)
        + jnp.roll(pole_all, -(lon_total // 2), axis=1).astype(jnp.float32)
    ).astype(jnp.bfloat16)
    conv_out = lon_conv(blended, lon_half[0], first_col, count_lon)
    return (middle.astype(jnp.float32) + conv_out).astype(jnp.bfloat16)[None]


def solution(mesh):
    return jax.shard_map(
        per_device,
        mesh=mesh,
        in_specs=(
            P(("groups", "lat"), "lon", None),
            P(),
            P("lat", None),
            P("lat", None, "lon"),
            P("lat", None),
            P(),
            P(),
            P(),
            P("lat"),
            P("lat"),
            P("lat"),
        ),
        out_specs=P(("groups", "lat"), "lon", None),
        check_vma=False,
    )
```

```python
import jax
import jax.numpy as jnp
from jax import lax
from jax.sharding import PartitionSpec as P

AXES = ("groups", "lat", "lon")


def layer_norm(values, gain):
    average = jnp.mean(values, axis=-1, keepdims=True)
    centered = values - average
    variance = jnp.mean(centered * centered, axis=-1, keepdims=True)
    return (centered * lax.rsqrt(variance + 1e-05) * gain).astype(jnp.bfloat16)


def device_pairs(target):
    lat_count = lax.axis_size("lat")
    pairs = []
    for group in range(2):
        for row in range(lat_count):
            for core in range(2):
                to = target(group, row, core)
                if 0 <= to[1] < lat_count:
                    source = (group * lat_count + row) * 2 + core
                    pairs.append((source, (to[0] * lat_count + to[1]) * 2 + to[2]))
    return pairs


def move(values, target):
    return lax.ppermute(values, AXES, device_pairs(target))


def slab_groups():
    lat_count = lax.axis_size("lat")
    return [
        [
            (group * lat_count + 2 * pair + side) * 2 + core
            for group in range(2)
            for side in range(2)
            for core in range(2)
        ]
        for pair in range(lat_count // 2)
    ]


def lon_weights(row_ids, col_ids, half_width, lon_total):
    offset_lon = (
        jnp.mod(col_ids[None, :] - row_ids[:, None] + lon_total // 2, lon_total) - lon_total // 2
    )
    distance = jnp.abs(offset_lon).astype(jnp.float32)
    span_plus = (half_width + 1).astype(jnp.float32)
    tent_weight = jnp.where(
        distance <= half_width.astype(jnp.float32), (1.0 - distance / span_plus) / span_plus, 0.0
    )
    odd_weight = tent_weight * offset_lon.astype(jnp.float32) / span_plus
    return tent_weight.astype(jnp.bfloat16), odd_weight.astype(jnp.bfloat16)


def per_device(
    tokens,
    gain_attn,
    w_qkv,
    key_bias,
    w_out,
    gain_conv,
    w_conv,
    lat_taps,
    lon_half,
    lat_half,
    quad_off,
):
    own_tokens = tokens[0]
    count_lon, width = own_tokens.shape
    head_count = key_bias.shape[1]
    head_dim = width // head_count
    lat_count = lax.axis_size("lat")
    group, lat_row, core = (lax.axis_index(name) for name in AXES)
    side = lax.rem(lat_row, 2)
    quarter = width // 4
    heads_here = head_count // 4
    rows = w_qkv.shape[0]
    half = rows // 2

    bias_rows = head_count * count_lon // width
    message = jnp.concatenate(
        [
            own_tokens,
            key_bias[0].reshape(bias_rows, width),
            jnp.zeros((16 - bias_rows, width), jnp.bfloat16),
        ]
    )
    blocks = {}
    for flip_core in range(2):
        for flip_group in range(2):
            blocks[flip_group, flip_core] = move(
                message,
                lambda g, l, c: (g ^ flip_group, l - l % 2 + (c ^ flip_core), l % 2),
            )

    w_half = lax.dynamic_slice_in_dim(w_qkv, core * half, half, 0)
    w_half = w_half.reshape(half, 3, 2, 2, quarter)
    w_half = lax.dynamic_index_in_dim(w_half, group, 3, keepdims=False)
    w_half = w_half.transpose(2, 0, 1, 3).reshape(2, half, 3 * quarter)
    spread = jnp.broadcast_to(w_half[None], (lat_count // 2, 2, half, 3 * quarter))
    spread = spread.reshape(lat_count, half, 3 * quarter)
    got = lax.all_to_all(spread, "lat", 0, 0, tiled=False)
    w_here = lax.all_gather(got, "lon", axis=1, tiled=True).reshape(width, 3 * quarter)

    out_half = lax.dynamic_slice_in_dim(w_out, core * half, half, 0)
    out_rows = lax.all_gather(out_half, "lat", axis=0)
    full_out = lax.all_gather(out_rows, "lon", axis=1).reshape(width, width)

    passed = move(blocks[0, 0][:count_lon], lambda g, l, c: (g, l if c != l % 2 else -1, 1 - c))
    other_tokens = jnp.where(core == side, passed, blocks[0, 1][:count_lon])

    order = [(0, 0), (0, 1), (1, 0), (1, 1)]
    stacked = jnp.concatenate([blocks[key][:count_lon] for key in order])
    normed = layer_norm(stacked.astype(jnp.float32), gain_attn)
    projected = jnp.dot(normed, w_here, preferred_element_type=jnp.float32).astype(jnp.bfloat16)
    projected = projected.reshape(2, 2 * count_lon, 3, heads_here, head_dim)
    head_first = (2 * side + group) * heads_here
    bias = jnp.concatenate(
        [
            lax.dynamic_slice_in_dim(
                blocks[0, flip][count_lon : count_lon + bias_rows].reshape(head_count, count_lon),
                head_first,
                heads_here,
                0,
            )
            for flip in range(2)
        ],
        axis=1,
    ).astype(jnp.float32)
    scores = jnp.einsum(
        "sqhd,skhd->shqk", projected[:, :, 0], projected[:, :, 1], preferred_element_type=jnp.float32
    ) * (head_dim ** (-0.5))
    scores = scores + bias[None, :, None, :]
    expd = jnp.exp(scores - jnp.max(scores, axis=-1, keepdims=True))
    totals = jnp.sum(expd, axis=-1)
    weighted = jnp.einsum(
        "shqk,skhd->sqhd",
        expd.astype(jnp.bfloat16),
        projected[:, :, 2],
        preferred_element_type=jnp.float32,
    )
    attended = weighted / totals.transpose(0, 2, 1)[..., None]
    attended = attended.astype(jnp.bfloat16).reshape(2, 2, count_lon, quarter)
    attended = jnp.where(group == 1, attended[::-1], attended)
    attended = jnp.where(side == 1, attended[:, ::-1], attended)
    pieces = jnp.broadcast_to(attended[:, None], (2, 2, 2, count_lon, quarter))
    pieces = pieces.reshape(8, count_lon, quarter)
    back = lax.all_to_all(pieces, AXES, 0, 0, axis_index_groups=slab_groups())
    back = back.reshape(2, 2, 2, count_lon, quarter).transpose(2, 3, 1, 0, 4)
    back = back.reshape(2 * count_lon, width)

    both_tokens = jnp.where(
        side == 0,
        jnp.concatenate([own_tokens, other_tokens]),
        jnp.concatenate([other_tokens, own_tokens]),
    )
    middle = (
        both_tokens.astype(jnp.float32)
        + jnp.dot(back, full_out, preferred_element_type=jnp.float32)
    ).astype(jnp.bfloat16)
    conv_in = layer_norm(middle.astype(jnp.float32), gain_conv).reshape(2, count_lon, width)
    first, second = conv_in[0], conv_in[1]
    own_in = jnp.where(side == 0, first, second)
    other_in = jnp.where(side == 0, second, first)
    own_middle = lax.dynamic_slice_in_dim(middle, side * count_lon, count_lon, 0)
    halo = move(other_in, lambda g, l, c: (g, l + 2 - 4 * (l % 2), c))

    offsets = jnp.arange(3, dtype=jnp.int32) - 1
    one_hot = (
        (quad_off[0] + offsets + 1)[:, None]
        == jnp.arange(lat_taps.shape[0], dtype=jnp.int32)[None, :]
    ).astype(jnp.float32)
    tap_vals = jnp.sum(one_hot[:, :, None] * lat_taps[None], axis=1)
    tap_vals = jnp.where((jnp.abs(offsets) <= lat_half[0])[:, None], tap_vals, 0.0)
    pole_gain = jnp.where(lat_row == 0, tap_vals[0], 0.0) + jnp.where(
        lat_row == lat_count - 1, tap_vals[2], 0.0
    )
    other_gain = jnp.where(side == 0, tap_vals[2], tap_vals[0])
    halo_gain = jnp.where(side == 0, tap_vals[0], tap_vals[2])
    own_f32 = own_in.astype(jnp.float32)
    group_width = w_conv.shape[2]
    groups = width // group_width
    lon_total = 2 * count_lon
    row_ids = jnp.arange(lon_total, dtype=jnp.int32)
    col_ids = core * count_lon + jnp.arange(count_lon, dtype=jnp.int32)
    coeffs = lon_weights(row_ids, col_ids, lon_half[0], lon_total)
    coeffs = coeffs + lon_weights(row_ids, col_ids + count_lon, lon_half[0], lon_total)
    lines = []
    for basis in range(2):
        lines.append(
            other_gain[basis] * other_in.astype(jnp.float32)
            + tap_vals[1, basis] * own_f32
            + halo_gain[basis] * halo.astype(jnp.float32)
        )
    for basis in range(2):
        lines.append(pole_gain[basis] * own_f32)
    lines = jnp.stack(lines).astype(jnp.bfloat16)
    weights = w_conv.reshape(1, 2, groups, group_width, group_width)
    mixed = jnp.einsum(
        "pkjgc,kgce->pkjge",
        lines.reshape(2, 2, count_lon, groups, group_width),
        weights[0],
        preferred_element_type=jnp.float32,
    ).astype(jnp.bfloat16)
    mixed = mixed.reshape(4 * count_lon, width)
    partial = jnp.dot(
        jnp.concatenate(coeffs, axis=1), mixed, preferred_element_type=jnp.float32
    ).reshape(2, count_lon, width)
    mine = lax.dynamic_index_in_dim(partial, core, 0, keepdims=False)
    yours = lax.dynamic_index_in_dim(partial, 1 - core, 0, keepdims=False).astype(jnp.bfloat16)
    received = lax.ppermute(yours, "lon", [(0, 1), (1, 0)])
    updated = own_middle.astype(jnp.float32) + mine + received.astype(jnp.float32)
    return updated.astype(jnp.bfloat16)[None]


def solution(mesh):
    return jax.shard_map(
        per_device,
        mesh=mesh,
        in_specs=(
            P(("groups", "lat"), "lon", None),
            P(),
            P("lat", None),
            P("lat", None, "lon"),
            P("lat", None),
            P(),
            P(),
            P(),
            P("lat"),
            P("lat"),
            P("lat"),
        ),
        out_specs=P(("groups", "lat"), "lon", None),
        check_vma=False,
    )
```

```python
import functools

import jax
import jax.numpy as jnp
from jax import lax
from jax.experimental import pallas as pl
from jax.experimental.pallas import tpu as pltpu
from jax.sharding import PartitionSpec as P

AXES = ("groups", "lat", "lon")
VMEM = pl.BlockSpec(memory_space=pltpu.VMEM)
SMEM = pl.BlockSpec(memory_space=pltpu.SMEM)
BF16 = jnp.bfloat16
F32 = jnp.float32


def call(body, outs, specs, args, flops, scratch=()):
    outs = tuple(jax.ShapeDtypeStruct(shape, dtype) for shape, dtype in outs)
    moved = sum(a.size * a.dtype.itemsize for a in args)
    return pl.pallas_call(
        body,
        out_shape=outs,
        in_specs=specs,
        out_specs=tuple(VMEM for _ in outs),
        scratch_shapes=list(scratch),
        compiler_params=pltpu.CompilerParams(vmem_limit_bytes=32 * 1024 * 1024),
        cost_estimate=pl.CostEstimate(flops=flops, bytes_accessed=moved, transcendentals=0),
    )(*args)


def device_pairs(target):
    lat_count = lax.axis_size("lat")
    pairs = []
    for group in range(2):
        for row in range(lat_count):
            for core in range(2):
                to = target(group, row, core)
                if 0 <= to[1] < lat_count:
                    source = (group * lat_count + row) * 2 + core
                    pairs.append((source, (to[0] * lat_count + to[1]) * 2 + to[2]))
    return pairs


def move(values, target):
    return lax.ppermute(values, AXES, device_pairs(target))


def swap_cores(values):
    return lax.ppermute(values, "lon", [(0, 1), (1, 0)])


def slab_groups():
    lat_count = lax.axis_size("lat")
    return [
        [
            (group * lat_count + 2 * pair + side) * 2 + core
            for group in range(2)
            for side in range(2)
            for core in range(2)
        ]
        for pair in range(lat_count // 2)
    ]


def norm_rows(values, gain):
    average = jnp.mean(values, axis=-1, keepdims=True)
    centered = values - average
    variance = jnp.mean(centered * centered, axis=-1, keepdims=True)
    return (centered * lax.rsqrt(variance + 1e-05) * gain).astype(BF16)


def pack_body(place, tokens, bias, w_qkv, w_out, message, qkv_pieces, out_pieces):
    count = tokens.shape[0]
    heads, bias_width = bias.shape
    message[:count, :] = tokens[...]
    message[count:, :] = jnp.zeros((16, tokens.shape[1]), BF16)
    message[count : count + heads, :bias_width] = bias[...]
    group, core = place[0], place[2]
    half = qkv_pieces.shape[1]
    width = w_out.shape[1]
    quarter = width // 4
    start = pl.multiple_of(core * half, half)
    rows = w_qkv[pl.ds(start, half), :]
    for side in range(2):
        parts = []
        for kind in range(3):
            first = kind * width + side * 2 * quarter
            parts.append(
                jnp.where(
                    group == 0,
                    rows[:, first : first + quarter],
                    rows[:, first + quarter : first + 2 * quarter],
                )
            )
        piece = jnp.concatenate(parts, axis=1)
        for pair in range(qkv_pieces.shape[0] // 2):
            qkv_pieces[2 * pair + side] = piece
    out_rows = w_out[pl.ds(start, half), :]
    for row in range(out_pieces.shape[0]):
        out_pieces[row] = out_rows


def join_halves(core, mine, other, joined):
    count, half, _ = mine.shape
    for row in range(count):
        joined[pl.ds(pl.multiple_of(row * 2 * half + core * half, half), half), :] = mine[row]
        joined[pl.ds(pl.multiple_of(row * 2 * half + (1 - core) * half, half), half), :] = other[row]


def attend_body(
    place, gain, near0, near1, far0, far1, mine, other, pieces, weights, bias_rows, normed
):
    group, lat_row, core = place[0], place[1], place[2]
    side = lax.rem(lat_row, 2)
    count, quarter = pieces.shape[3], pieces.shape[4]
    heads = 3
    head_dim = quarter // heads
    join_halves(core, mine, other, weights)
    gains = gain[...]
    for slot, block in enumerate((near0, near1, far0, far1)):
        normed[slot * count : (slot + 1) * count, :] = norm_rows(
            block[:count, :].astype(F32), gains
        )
    for slot, block in enumerate((near0, near1)):
        bias_rows[:, slot * count : (slot + 1) * count] = block[count:, :count].astype(F32)
    first_head = (2 * side + group) * heads
    for far in range(2):
        projected = jnp.dot(
            normed[far * 2 * count : (far + 1) * 2 * count, :],
            weights[...],
            preferred_element_type=F32,
        ).astype(BF16)
        outs = []
        for head in range(heads):
            low = head * head_dim
            queries = projected[:, low : low + head_dim]
            keys = projected[:, quarter + low : quarter + low + head_dim]
            values = projected[:, 2 * quarter + low : 2 * quarter + low + head_dim]
            scores = lax.dot_general(
                queries, keys, (((1,), (1,)), ((), ())), preferred_element_type=F32
            ) * (head_dim**-0.5)
            scores = scores + bias_rows[pl.ds(first_head + head, 1), :]
            expd = jnp.exp(scores - jnp.max(scores, axis=-1, keepdims=True))
            totals = jnp.sum(expd, axis=-1, keepdims=True)
            weighted = jnp.dot(expd.astype(BF16), values, preferred_element_type=F32)
            outs.append((weighted / totals).astype(BF16))
        attended = jnp.concatenate(outs, axis=1)
        sample = far + group - 2 * far * group
        for flip in range(2):
            lon_at = flip + side - 2 * flip * side
            part = attended[flip * count : (flip + 1) * count]
            for to_side in range(2):
                pieces[sample, to_side, lon_at] = part


def project_out(band, back, weights, tokens, gain):
    attended = jnp.concatenate(
        [back[part % 2, part // 2, band] for part in range(4)], axis=1
    )
    summed = tokens + jnp.dot(attended, weights[...], preferred_element_type=F32)
    middle = summed.astype(BF16)
    return middle, norm_rows(middle.astype(F32), gain)


def other_body(place, gain, back, mine, other, passed, near1, other_in, full_out):
    lat_row, core = place[1], place[2]
    side = lax.rem(lat_row, 2)
    count = other_in.shape[0]
    join_halves(core, mine, other, full_out)
    tokens = jnp.where(
        core == side, passed[:count, :].astype(F32), near1[:count, :].astype(F32)
    )
    other_in[...] = project_out(1 - side, back, full_out, tokens, gain[...])[1]


def diagonal_body(w_conv, blocks):
    size = w_conv.shape[2]
    blocks[...] = jnp.zeros(blocks.shape, BF16)
    per_block = blocks.shape[2] // size
    for basis in range(blocks.shape[0]):
        for tile in range(blocks.shape[1]):
            for at in range(per_block):
                first = (tile * per_block + at) * size
                low, high = at * size, (at + 1) * size
                blocks[basis, tile, low:high, low:high] = w_conv[basis, first : first + size, :]


def tent_pair(row_count, first_col, col_count, half_width):
    rows = lax.broadcasted_iota(jnp.int32, (row_count, col_count), 0)
    cols = lax.broadcasted_iota(jnp.int32, (row_count, col_count), 1) + first_col
    offset = ((cols - rows + row_count // 2) & (row_count - 1)) - row_count // 2
    distance = jnp.abs(offset).astype(F32)
    span_plus = (half_width + 1).astype(F32)
    tent = jnp.where(
        distance <= half_width.astype(F32), (1.0 - distance / span_plus) / span_plus, 0.0
    )
    odd = tent * offset.astype(F32) / span_plus
    return tent.astype(BF16), odd.astype(BF16)


def mix(lines, blocks, basis):
    size = blocks.shape[2]
    return jnp.concatenate(
        [
            jnp.dot(
                lines[:, tile * size : (tile + 1) * size],
                blocks[basis, tile],
                preferred_element_type=F32,
            ).astype(BF16)
            for tile in range(blocks.shape[1])
        ],
        axis=1,
    )


def tap_gain(taps, quad_off, lat_half, offset, basis):
    value = taps[quad_off[0] + offset + 1, basis]
    if offset == 0:
        return value
    return jnp.where(lat_half[0] >= 1, value, 0.0)


def own_body(
    lat_count,
    place,
    lon_half,
    lat_half,
    quad_off,
    taps,
    gain,
    back,
    mine,
    other,
    tokens,
    other_in,
    blocks,
    middle,
    partial,
    full_out,
):
    lat_row, core = place[1], place[2]
    side = lax.rem(lat_row, 2)
    count = tokens.shape[0]
    join_halves(core, mine, other, full_out)
    own_middle, own_in = project_out(side, back, full_out, tokens[...].astype(F32), gain[...])
    middle[...] = own_middle
    own = own_in.astype(F32)
    neighbour = other_in[...].astype(F32)
    rows = partial.shape[0]
    mixed, coeffs = [], []
    direct = tent_pair(rows, core * count, count, lon_half[0])
    rolled = tent_pair(rows, core * count + count, count, lon_half[0])
    for basis in range(2):
        below = tap_gain(taps, quad_off, lat_half, -1, basis)
        above = tap_gain(taps, quad_off, lat_half, 1, basis)
        centre = tap_gain(taps, quad_off, lat_half, 0, basis)
        other_gain = jnp.where(side == 0, above, below)
        pole_gain = jnp.where(lat_row == 0, below, 0.0) + jnp.where(
            lat_row == lat_count - 1, above, 0.0
        )
        lines = jnp.concatenate(
            [
                (other_gain * neighbour + centre * own).astype(BF16),
                (pole_gain * own).astype(BF16),
            ]
        )
        mixed.append(mix(lines, blocks, basis))
        coeffs += [direct[basis], rolled[basis]]
    partial[...] = jnp.dot(
        jnp.concatenate(coeffs, axis=1),
        jnp.concatenate(mixed, axis=0),
        preferred_element_type=F32,
    )


def halo_body(
    place, lon_half, lat_half, quad_off, taps, halo, blocks, middle, partial, kept, sent, total
):
    lat_row, core = place[1], place[2]
    side = lax.rem(lat_row, 2)
    count = halo.shape[0]
    rows = partial.shape[0]
    values = halo[...].astype(F32)
    mixed = []
    for basis in range(2):
        below = tap_gain(taps, quad_off, lat_half, -1, basis)
        above = tap_gain(taps, quad_off, lat_half, 1, basis)
        gain = jnp.where(side == 0, below, above)
        mixed.append(mix((gain * values).astype(BF16), blocks, basis))
    total[...] = partial[...] + jnp.dot(
        jnp.concatenate(tent_pair(rows, core * count, count, lon_half[0]), axis=1),
        jnp.concatenate(mixed, axis=0),
        preferred_element_type=F32,
    )
    here = pl.multiple_of(core * count, count)
    there = pl.multiple_of((1 - core) * count, count)
    kept[...] = middle[...].astype(F32) + total[pl.ds(here, count), :]
    sent[...] = total[pl.ds(there, count), :].astype(BF16)


def pack_plain(place, tokens, bias, w_qkv, w_out, lat_count):
    count, width = tokens.shape
    quarter = width // 4
    half = w_qkv.shape[0] // 2
    tail = jnp.zeros((16, width), BF16).at[: bias.shape[0], : bias.shape[1]].set(bias)
    rows = lax.dynamic_slice_in_dim(w_qkv, place[2] * half, half, 0)
    rows = rows.reshape(half, 3, 2, 2, quarter)
    rows = lax.dynamic_index_in_dim(rows, place[0], 3, keepdims=False)
    rows = rows.transpose(2, 0, 1, 3).reshape(2, half, 3 * quarter)
    qkv = jnp.broadcast_to(rows[None], (lat_count // 2, 2, half, 3 * quarter))
    out = lax.dynamic_slice_in_dim(w_out, place[2] * half, half, 0)
    return (
        jnp.concatenate([tokens, tail]),
        qkv.reshape(lat_count, half, 3 * quarter),
        jnp.broadcast_to(out[None], (lat_count, half, width)),
    )


def regroup(core, mine, other):
    both = jnp.where(core == 0, jnp.stack([mine, other], 1), jnp.stack([other, mine], 1))
    whole = both.reshape(8, 2, -1, mine.shape[2])
    pick = lambda index: lax.dynamic_index_in_dim(whole, index, 1, keepdims=False)
    return pick(core), pick(1 - core)


def per_device(
    tokens,
    gain_attn,
    w_qkv,
    key_bias,
    w_out,
    gain_conv,
    w_conv,
    lat_taps,
    lon_half,
    lat_half,
    quad_off,
):
    own_tokens = tokens[0]
    count, width = own_tokens.shape
    quarter = width // 4
    lat_count = lax.axis_size("lat")
    place = jnp.stack([lax.axis_index(name) for name in AXES]).astype(jnp.int32)
    core = place[2]
    half = w_qkv.shape[0] // 2
    gain_attn = gain_attn[None]
    gain_conv = gain_conv[None]

    if half % 16 == 0:
        message, qkv_pieces, out_pieces = call(
            pack_body,
            [
                ((count + 16, width), BF16),
                ((lat_count, half, 3 * quarter), BF16),
                ((lat_count, half, width), BF16),
            ],
            [SMEM] + [VMEM] * 4,
            (place, own_tokens, key_bias[0], w_qkv, w_out),
            0,
        )
    else:
        message, qkv_pieces, out_pieces = pack_plain(
            place, own_tokens, key_bias[0], w_qkv, w_out, lat_count
        )
    qkv_mine = lax.all_to_all(qkv_pieces, "lat", 0, 0)
    blocks = {}
    for flip_core in range(2):
        for flip_group in range(2):
            blocks[flip_group, flip_core] = move(
                message,
                lambda g, l, c: (g ^ flip_group, l - l % 2 + (c ^ flip_core), l % 2),
            )
    out_mine = lax.all_to_all(out_pieces, "lat", 0, 0)
    qkv_other = swap_cores(qkv_mine)
    out_other = swap_cores(out_mine)
    passed = move(blocks[0, 0], lambda g, l, c: (g, l if c != l % 2 else -1, 1 - c))
    if half % 16:
        qkv_mine, qkv_other = regroup(core, qkv_mine, qkv_other)
        out_mine, out_other = regroup(core, out_mine, out_other)

    size = 4 * w_conv.shape[2]
    (diagonal,) = call(
        diagonal_body, [((2, width // size, size, size), BF16)], [VMEM], (w_conv,), 0
    )

    (pieces,) = call(
        attend_body,
        [((2, 2, 2, count, quarter), BF16)],
        [SMEM] + [VMEM] * 7,
        (
            place,
            gain_attn,
            blocks[0, 0],
            blocks[0, 1],
            blocks[1, 0],
            blocks[1, 1],
            qkv_mine,
            qkv_other,
        ),
        2 * 512 * 768 * 576 + 4 * 6 * 256 * 256 * 64,
        [
            pltpu.VMEM((width, 3 * quarter), BF16),
            pltpu.VMEM((16, 2 * count), F32),
            pltpu.VMEM((4 * count, width), BF16),
        ],
    )
    back = lax.all_to_all(
        pieces.reshape(8, count, quarter), AXES, 0, 0, axis_index_groups=slab_groups()
    ).reshape(2, 2, 2, count, quarter)

    (other_in,) = call(
        other_body,
        [((count, width), BF16)],
        [SMEM] + [VMEM] * 6,
        (place, gain_conv, back, out_mine, out_other, passed, blocks[0, 1]),
        2 * count * width * width,
        [pltpu.VMEM((width, width), BF16)],
    )
    halo = move(other_in, lambda g, l, c: (g, l + 2 - 4 * (l % 2), c))
    middle, partial = call(
        functools.partial(own_body, lat_count),
        [((count, width), BF16), ((2 * count, width), F32)],
        [SMEM] * 5 + [VMEM] * 7,
        (
            place,
            lon_half,
            lat_half,
            quad_off,
            lat_taps,
            gain_conv,
            back,
            out_mine,
            out_other,
            own_tokens,
            other_in,
            diagonal,
        ),
        2 * count * width * width * 3,
        [pltpu.VMEM((width, width), BF16)],
    )
    kept, sent = call(
        halo_body,
        [((count, width), F32), ((count, width), BF16)],
        [SMEM] * 5 + [VMEM] * 4,
        (place, lon_half, lat_half, quad_off, lat_taps, halo, diagonal, middle, partial),
        2 * 256 * 256 * width,
        [pltpu.VMEM((2 * count, width), F32)],
    )
    received = swap_cores(sent)
    return (kept + received.astype(F32)).astype(BF16)[None]


def solution(mesh):
    return jax.shard_map(
        per_device,
        mesh=mesh,
        in_specs=(
            P(("groups", "lat"), "lon", None),
            P(),
            P("lat", None),
            P("lat", None, "lon"),
            P("lat", None),
            P(),
            P(),
            P(),
            P("lat"),
            P("lat"),
            P("lat"),
        ),
        out_specs=P(("groups", "lat"), "lon", None),
        check_vma=False,
    )
```

```python
import functools

import jax
import jax.numpy as jnp
from jax import lax
from jax.experimental import pallas as pl
from jax.experimental.pallas import tpu as pltpu
from jax.sharding import PartitionSpec as P

AXES = ("groups", "lat", "lon")
VMEM = pl.BlockSpec(memory_space=pltpu.VMEM)
ANY = pl.BlockSpec(memory_space=pl.ANY)
FLIPS = ((1, 0), (0, 1), (1, 1))
SMEM = pl.BlockSpec(memory_space=pltpu.SMEM)
BF16 = jnp.bfloat16
F32 = jnp.float32


def call(body, outs, specs, args, flops, scratch=()):
    outs = tuple(jax.ShapeDtypeStruct(shape, dtype) for shape, dtype in outs)
    moved = sum(a.size * a.dtype.itemsize for a in args)
    return pl.pallas_call(
        body,
        out_shape=outs,
        in_specs=specs,
        out_specs=tuple(VMEM for _ in outs),
        scratch_shapes=list(scratch),
        compiler_params=pltpu.CompilerParams(vmem_limit_bytes=32 * 1024 * 1024),
        cost_estimate=pl.CostEstimate(flops=flops, bytes_accessed=moved, transcendentals=0),
    )(*args)


def device_pairs(target):
    lat_count = lax.axis_size("lat")
    pairs = []
    for group in range(2):
        for row in range(lat_count):
            for core in range(2):
                to = target(group, row, core)
                if 0 <= to[1] < lat_count:
                    source = (group * lat_count + row) * 2 + core
                    pairs.append((source, (to[0] * lat_count + to[1]) * 2 + to[2]))
    return pairs


def move(values, target):
    return lax.ppermute(values, AXES, device_pairs(target))


def swap_cores(values):
    return lax.ppermute(values, "lon", [(0, 1), (1, 0)])


def flip_chips(values, flip, sample):
    return move(values, lambda g, l, c: (g ^ sample, l ^ flip, c))


def norm_rows(values, gain):
    average = jnp.mean(values, axis=-1, keepdims=True)
    centered = values - average
    variance = jnp.mean(centered * centered, axis=-1, keepdims=True)
    return (centered * lax.rsqrt(variance + 1e-05) * gain).astype(BF16)


def norm_body(tokens, bias, gain, message, raw, sems):
    count = tokens.shape[0]
    heads, bias_width = bias.shape
    fetch = pltpu.make_async_copy(tokens, raw, sems.at[0])
    fetch.start()
    message[count:, :] = jnp.zeros((16, tokens.shape[1]), BF16)
    message[count : count + heads, :bias_width] = bias[...]
    fetch.wait()
    message[:count, :] = norm_rows(raw[...].astype(F32), gain[...])


def pack_qkv_body(w_qkv, message, pieces, rows, sems):
    del message
    group, core = lax.axis_index("groups"), lax.axis_index("lon")
    half = pieces.shape[1]
    quarter = pieces.shape[2] // 3
    start = pl.multiple_of(core * half, half)
    fetch = pltpu.make_async_copy(w_qkv.at[pl.ds(start, half), :], rows, sems.at[0])
    fetch.start()
    fetch.wait()
    for side in range(2):
        parts = []
        for kind in range(3):
            first = (4 * kind + 2 * side) * quarter
            parts.append(
                jnp.where(
                    group == 0,
                    rows[:, first : first + quarter],
                    rows[:, first + quarter : first + 2 * quarter],
                )
            )
        piece = jnp.concatenate(parts, axis=1)
        for pair in range(pieces.shape[0] // 2):
            pieces[2 * pair + side] = piece


def pack_out_body(w_out, qkv_pieces, pieces, sems):
    del qkv_pieces
    core = lax.axis_index("lon")
    count, half, _ = pieces.shape
    start = pl.multiple_of(core * half, half)
    fetches = [
        pltpu.make_async_copy(w_out.at[pl.ds(start, half), :], pieces.at[row], sems.at[row])
        for row in range(count)
    ]
    for fetch in fetches:
        fetch.start()
    for fetch in fetches:
        fetch.wait()


def join_halves(mine, other, joined):
    core = lax.axis_index("lon")
    count, half, _ = mine.shape
    for row in range(count):
        joined[pl.ds(pl.multiple_of(row * 2 * half + core * half, half), half), :] = mine[row]
        joined[pl.ds(pl.multiple_of(row * 2 * half + (1 - core) * half, half), half), :] = other[row]


def attend_body(*refs):
    near, far, (mine, other) = refs[:4], refs[4:8], refs[8:10]
    pieces, (weights, bias_rows, near_rows, far_rows) = refs[10:14], refs[14:]
    group, side = lax.axis_index("groups"), lax.rem(lax.axis_index("lat"), 2)
    _, count, quarter = pieces[0].shape
    heads = 3
    head_dim = quarter // heads
    join_halves(mine, other, weights)
    for slot in range(4):
        near_rows[slot * count : (slot + 1) * count, :] = near[slot][:count, :]
        far_rows[slot * count : (slot + 1) * count, :] = far[slot][:count, :]
    for flip in range(2):
        for at, block in enumerate((near[flip], far[flip])):
            bias_rows[flip, :, at * count : (at + 1) * count] = block[count:, :count].astype(F32)
    first_head = (2 * side + group) * heads
    here = jnp.dot(near_rows[...], weights[...], preferred_element_type=F32).astype(BF16)
    there = jnp.dot(far_rows[...], weights[:, quarter:], preferred_element_type=F32).astype(BF16)
    for slot in range(4):
        flip, sample = slot % 2, slot // 2
        low_row, high_row = slot * count, (slot + 1) * count
        outs = []
        for head in range(heads):
            low = head * head_dim
            queries = here[low_row:high_row, low : low + head_dim]
            keys, values = (
                jnp.concatenate(
                    [
                        here[low_row:high_row, (kind + 1) * quarter + low :][:, :head_dim],
                        there[low_row:high_row, kind * quarter + low :][:, :head_dim],
                    ]
                )
                for kind in range(2)
            )
            scores = lax.dot_general(
                queries, keys, (((1,), (1,)), ((), ())), preferred_element_type=F32
            ) * (head_dim**-0.5)
            scores = scores + bias_rows[flip, pl.ds(first_head + head, 1), :]
            expd = jnp.exp(scores - jnp.max(scores, axis=-1, keepdims=True))
            totals = jnp.sum(expd, axis=-1, keepdims=True)
            weighted = jnp.dot(expd.astype(BF16), values, preferred_element_type=F32)
            outs.append((weighted / totals).astype(BF16))
        attended = jnp.concatenate(outs, axis=1)
        pieces[2 * sample + flip][0] = attended
        pieces[2 * sample + 1 - flip][1] = attended


def project_out(which, pieces, weights, tokens, gain):
    group, side = lax.axis_index("groups"), lax.rem(lax.axis_index("lat"), 2)
    summed = tokens.astype(F32)
    for slot, piece in enumerate(pieces):
        flip, sample = slot % 2, slot // 2
        quarter = piece.shape[2]
        owner = 2 * (side + flip - 2 * side * flip) + (group + sample - 2 * group * sample)
        rows = pl.ds(pl.multiple_of(owner * quarter, quarter), quarter)
        summed = summed + jnp.dot(piece[which], weights[rows, :], preferred_element_type=F32)
    middle = summed.astype(BF16)
    return middle, norm_rows(middle.astype(F32), gain)


def other_body(gain, piece0, piece1, piece2, piece3, weights, tokens, other_in):
    pieces = (piece0, piece1, piece2, piece3)
    other_in[...] = project_out(1, pieces, weights, tokens[...], gain[...])[1]


def diagonal_body(w_conv, blocks):
    size = w_conv.shape[2]
    blocks[...] = jnp.zeros(blocks.shape, BF16)
    per_block = blocks.shape[2] // size
    for basis in range(blocks.shape[0]):
        for tile in range(blocks.shape[1]):
            for at in range(per_block):
                first = (tile * per_block + at) * size
                low, high = at * size, (at + 1) * size
                blocks[basis, tile, low:high, low:high] = w_conv[basis, first : first + size, :]


def tent_pair(row_count, first_col, col_count, half_width):
    rows = lax.broadcasted_iota(jnp.int32, (row_count, col_count), 0)
    cols = lax.broadcasted_iota(jnp.int32, (row_count, col_count), 1) + first_col
    offset = ((cols - rows + row_count // 2) & (row_count - 1)) - row_count // 2
    distance = jnp.abs(offset).astype(F32)
    span_plus = (half_width + 1).astype(F32)
    tent = jnp.where(
        distance <= half_width.astype(F32), (1.0 - distance / span_plus) / span_plus, 0.0
    )
    odd = tent * offset.astype(F32) / span_plus
    return tent.astype(BF16), odd.astype(BF16)


def mix(lines, blocks, basis):
    size = blocks.shape[2]
    return jnp.concatenate(
        [
            jnp.dot(
                lines[:, tile * size : (tile + 1) * size],
                blocks[basis, tile],
                preferred_element_type=F32,
            ).astype(BF16)
            for tile in range(blocks.shape[1])
        ],
        axis=1,
    )


def tap_gain(taps, quad_off, lat_half, offset, basis):
    value = taps[quad_off[0] + offset + 1, basis]
    if offset == 0:
        return value
    return jnp.where(lat_half[0] >= 1, value, 0.0)


def own_body(
    lat_count,
    lon_half,
    lat_half,
    quad_off,
    taps,
    gain,
    piece0,
    piece1,
    piece2,
    piece3,
    weights,
    tokens,
    other_in,
    blocks,
    middle,
    partial,
):
    lat_row, core = lax.axis_index("lat"), lax.axis_index("lon")
    side = lax.rem(lat_row, 2)
    count = tokens.shape[0]
    pieces = (piece0, piece1, piece2, piece3)
    own_middle, own_in = project_out(0, pieces, weights, tokens[...], gain[...])
    middle[...] = own_middle
    own = own_in.astype(F32)
    neighbour = other_in[...].astype(F32)
    rows = partial.shape[0]
    mixed, coeffs = [], []
    direct = tent_pair(rows, core * count, count, lon_half[0])
    rolled = tent_pair(rows, core * count + count, count, lon_half[0])
    for basis in range(2):
        below = tap_gain(taps, quad_off, lat_half, -1, basis)
        above = tap_gain(taps, quad_off, lat_half, 1, basis)
        centre = tap_gain(taps, quad_off, lat_half, 0, basis)
        other_gain = jnp.where(side == 0, above, below)
        pole_gain = jnp.where(lat_row == 0, below, 0.0) + jnp.where(
            lat_row == lat_count - 1, above, 0.0
        )
        lines = jnp.concatenate(
            [
                (other_gain * neighbour + centre * own).astype(BF16),
                (pole_gain * own).astype(BF16),
            ]
        )
        mixed.append(mix(lines, blocks, basis))
        coeffs += [direct[basis], rolled[basis]]
    partial[...] = jnp.dot(
        jnp.concatenate(coeffs, axis=1),
        jnp.concatenate(mixed, axis=0),
        preferred_element_type=F32,
    )


def halo_body(
    lon_half, lat_half, quad_off, taps, halo, blocks, middle, partial, kept, sent, total
):
    lat_row, core = lax.axis_index("lat"), lax.axis_index("lon")
    side = lax.rem(lat_row, 2)
    count = halo.shape[0]
    rows = partial.shape[0]
    values = halo[...].astype(F32)
    mixed = []
    for basis in range(2):
        below = tap_gain(taps, quad_off, lat_half, -1, basis)
        above = tap_gain(taps, quad_off, lat_half, 1, basis)
        gain = jnp.where(side == 0, below, above)
        mixed.append(mix((gain * values).astype(BF16), blocks, basis))
    total[...] = partial[...] + jnp.dot(
        jnp.concatenate(tent_pair(rows, core * count, count, lon_half[0]), axis=1),
        jnp.concatenate(mixed, axis=0),
        preferred_element_type=F32,
    )
    here = pl.multiple_of(core * count, count)
    there = pl.multiple_of((1 - core) * count, count)
    kept[...] = middle[...].astype(F32) + total[pl.ds(here, count), :]
    sent[...] = total[pl.ds(there, count), :].astype(BF16)


def pack_plain(weights, columns):
    core, lat_count = lax.axis_index("lon"), lax.axis_size("lat")
    half, width = weights.shape[0] // 2, weights.shape[1]
    rows = lax.dynamic_slice_in_dim(weights, core * half, half, 0)
    if columns == width:
        return jnp.broadcast_to(rows[None], (lat_count, half, width))
    rows = rows.reshape(half, 3, 2, 2, columns // 3)
    rows = lax.dynamic_index_in_dim(rows, lax.axis_index("groups"), 3, keepdims=False)
    rows = rows.transpose(2, 0, 1, 3).reshape(2, half, columns)
    rows = jnp.broadcast_to(rows[None], (lat_count // 2, 2, half, columns))
    return rows.reshape(lat_count, half, columns)


def regroup(core, mine, other):
    both = jnp.where(core == 0, jnp.stack([mine, other], 1), jnp.stack([other, mine], 1))
    whole = both.reshape(8, 2, -1, mine.shape[2])
    pick = lambda index: lax.dynamic_index_in_dim(whole, index, 1, keepdims=False)
    return pick(core), pick(1 - core)


def per_device(
    tokens,
    gain_attn,
    w_qkv,
    key_bias,
    w_out,
    gain_conv,
    w_conv,
    lat_taps,
    lon_half,
    lat_half,
    quad_off,
):
    own_tokens = tokens[0]
    count, width = own_tokens.shape
    quarter = width // 4
    lat_count = lax.axis_size("lat")
    core = lax.axis_index("lon")
    half = w_qkv.shape[0] // 2
    gain_attn = gain_attn[None]
    gain_conv = gain_conv[None]

    (message,) = call(
        norm_body,
        [((count + 16, width), BF16)],
        [ANY, VMEM, VMEM],
        (own_tokens, key_bias[0], gain_attn),
        10 * count * width,
        [pltpu.VMEM((count, width), BF16), pltpu.SemaphoreType.DMA((1,))],
    )
    near = [message] + [flip_chips(message, flip, sample) for flip, sample in FLIPS]
    far = [swap_cores(block) for block in near]

    if half % 16 == 0:
        (qkv_pieces,) = call(
            pack_qkv_body,
            [((lat_count, half, 3 * quarter), BF16)],
            [ANY] * 2,
            (w_qkv, message),
            0,
            [pltpu.VMEM((half, 3 * width), BF16), pltpu.SemaphoreType.DMA((1,))],
        )
        (out_pieces,) = call(
            pack_out_body,
            [((lat_count, half, width), BF16)],
            [ANY] * 2,
            (w_out, qkv_pieces),
            0,
            [pltpu.SemaphoreType.DMA((lat_count,))],
        )
    else:
        qkv_pieces = pack_plain(w_qkv, 3 * quarter)
        out_pieces = pack_plain(w_out, width)
    qkv_mine = lax.all_to_all(qkv_pieces, "lat", 0, 0)
    qkv_other = swap_cores(qkv_mine)
    out_mine = lax.all_to_all(out_pieces, "lat", 0, 0)
    out_other = swap_cores(out_mine)
    if half % 16:
        qkv_mine, qkv_other = regroup(core, qkv_mine, qkv_other)
        out_mine, out_other = regroup(core, out_mine, out_other)
    other_tokens = flip_chips(own_tokens, 1, 0)

    size = 4 * w_conv.shape[2]
    (diagonal,) = call(
        diagonal_body, [((2, width // size, size, size), BF16)], [VMEM], (w_conv,), 0
    )

    pieces = call(
        attend_body,
        [((2, count, quarter), BF16)] * 4,
        [VMEM] * 10,
        (*near, *far, qkv_mine, qkv_other),
        2 * 1024 * width * 3 * quarter,
        [
            pltpu.VMEM((width, 3 * quarter), BF16),
            pltpu.VMEM((2, 16, 2 * count), F32),
            pltpu.VMEM((4 * count, width), BF16),
            pltpu.VMEM((4 * count, width), BF16),
        ],
    )
    back = [pieces[0]] + [
        flip_chips(piece, flip, sample) for piece, (flip, sample) in zip(pieces[1:], FLIPS)
    ]
    (full_out,) = call(
        join_halves, [((width, width), BF16)], [VMEM] * 2, (out_mine, out_other), 0
    )
    (other_in,) = call(
        other_body,
        [((count, width), BF16)],
        [VMEM] * 7,
        (gain_conv, *back, full_out, other_tokens),
        2 * count * width * width,
    )
    halo = move(other_in, lambda g, l, c: (g, l + 2 - 4 * (l % 2), c))
    middle, partial = call(
        functools.partial(own_body, lat_count),
        [((count, width), BF16), ((2 * count, width), F32)],
        [SMEM] * 4 + [VMEM] * 9,
        (
            lon_half,
            lat_half,
            quad_off,
            lat_taps,
            gain_conv,
            *back,
            full_out,
            own_tokens,
            other_in,
            diagonal,
        ),
        2 * count * width * width * 3,
    )
    kept, sent = call(
        halo_body,
        [((count, width), F32), ((count, width), BF16)],
        [SMEM] * 4 + [VMEM] * 4,
        (lon_half, lat_half, quad_off, lat_taps, halo, diagonal, middle, partial),
        2 * 256 * 256 * width,
        [pltpu.VMEM((2 * count, width), F32)],
    )
    received = swap_cores(sent)
    return (kept + received.astype(F32)).astype(BF16)[None]


def solution(mesh):
    return jax.shard_map(
        per_device,
        mesh=mesh,
        in_specs=(
            P(("groups", "lat"), "lon", None),
            P(),
            P("lat", None),
            P("lat", None, "lon"),
            P("lat", None),
            P(),
            P(),
            P(),
            P("lat"),
            P("lat"),
            P("lat"),
        ),
        out_specs=P(("groups", "lat"), "lon", None),
        check_vma=False,
    )
```

```python
import functools

import jax
import jax.numpy as jnp
from jax import lax
from jax.experimental import pallas as pl
from jax.experimental.pallas import tpu as pltpu
from jax.sharding import PartitionSpec as P

AXES = ("groups", "lat", "lon")
VMEM = pl.BlockSpec(memory_space=pltpu.VMEM)
ANY = pl.BlockSpec(memory_space=pl.ANY)
HBM = pl.BlockSpec(memory_space=pltpu.HBM)
FLIPS = ((1, 0), (0, 1), (1, 1))
SMEM = pl.BlockSpec(memory_space=pltpu.SMEM)
BF16 = jnp.bfloat16
F32 = jnp.float32


def call(body, outs, specs, args, flops, scratch=()):
    outs = tuple(jax.ShapeDtypeStruct(shape, dtype) for shape, dtype in outs)
    moved = sum(a.size * a.dtype.itemsize for a in args)
    return pl.pallas_call(
        body,
        out_shape=outs,
        in_specs=specs,
        out_specs=tuple(VMEM for _ in outs),
        scratch_shapes=list(scratch),
        compiler_params=pltpu.CompilerParams(vmem_limit_bytes=32 * 1024 * 1024),
        cost_estimate=pl.CostEstimate(flops=flops, bytes_accessed=moved, transcendentals=0),
    )(*args)


def untouched(*refs):
    del refs


def gate(value, *after):
    return pl.pallas_call(
        untouched,
        out_shape=jax.ShapeDtypeStruct(value.shape, value.dtype),
        in_specs=[ANY] * (1 + len(after)),
        out_specs=ANY,
        input_output_aliases={0: 0},
    )(value, *after)


def device_pairs(target):
    lat_count = lax.axis_size("lat")
    pairs = []
    for group in range(2):
        for row in range(lat_count):
            for core in range(2):
                to = target(group, row, core)
                if 0 <= to[1] < lat_count:
                    source = (group * lat_count + row) * 2 + core
                    pairs.append((source, (to[0] * lat_count + to[1]) * 2 + to[2]))
    return pairs


def move(values, target):
    return lax.ppermute(values, AXES, device_pairs(target))


def swap_cores(values):
    return lax.ppermute(values, "lon", [(0, 1), (1, 0)])


def flip_chips(values, flip, sample):
    return move(values, lambda g, l, c: (g ^ sample, l ^ flip, c))


def norm_rows(values, gain):
    average = jnp.mean(values, axis=-1, keepdims=True)
    centered = values - average
    variance = jnp.mean(centered * centered, axis=-1, keepdims=True)
    return (centered * lax.rsqrt(variance + 1e-05) * gain).astype(BF16)


def pack_body(tokens, bias, gain, w_out, message, raw, out_pieces, bias_here, gain_here, sems):
    count = tokens.shape[0]
    heads, bias_width = bias.shape
    group, core = lax.axis_index("groups"), lax.axis_index("lon")
    fetches = [
        pltpu.make_async_copy(source, target, sems.at[at])
        for at, (source, target) in enumerate(
            ((tokens, raw), (gain, gain_here), (bias, bias_here))
        )
    ]
    if out_pieces is not None:
        pieces, half, columns = out_pieces.shape
        rows = pl.ds(pl.multiple_of(core * half, half), half)
        lanes = pl.ds(pl.multiple_of(group * columns, columns), columns)
        fetches += [
            pltpu.make_async_copy(w_out.at[rows, lanes], out_pieces.at[row], sems.at[3 + row])
            for row in range(pieces)
        ]
    for fetch in fetches:
        fetch.start()
    message[count:, :] = jnp.zeros((16, tokens.shape[1]), BF16)
    for fetch in fetches[:3]:
        fetch.wait()
    message[count : count + heads, :bias_width] = bias_here[...]
    message[:count, :] = norm_rows(raw[...].astype(F32), gain_here[...])
    for fetch in fetches[3:]:
        fetch.wait()


def pack_norm_body(tokens, bias, gain, message, raw, bias_here, gain_here, sems):
    pack_body(tokens, bias, gain, None, message, raw, None, bias_here, gain_here, sems)


def pack_qkv_body(w_qkv, message, pieces, rows, sems):
    del message
    group, core = lax.axis_index("groups"), lax.axis_index("lon")
    half = pieces.shape[1]
    quarter = pieces.shape[2] // 3
    start = pl.multiple_of(core * half, half)
    fetch = pltpu.make_async_copy(w_qkv.at[pl.ds(start, half), :], rows, sems.at[0])
    fetch.start()
    fetch.wait()
    for side in range(2):
        parts = []
        for kind in range(3):
            first = (4 * kind + 2 * side) * quarter
            parts.append(
                jnp.where(
                    group == 0,
                    rows[:, first : first + quarter],
                    rows[:, first + quarter : first + 2 * quarter],
                )
            )
        piece = jnp.concatenate(parts, axis=1)
        for pair in range(pieces.shape[0] // 2):
            pieces[2 * pair + side] = piece


def join_halves(mine, other, joined):
    core = lax.axis_index("lon")
    count, half, _ = mine.shape
    for row in range(count):
        joined[pl.ds(pl.multiple_of(row * 2 * half + core * half, half), half), :] = mine[row]
        joined[pl.ds(pl.multiple_of(row * 2 * half + (1 - core) * half, half), half), :] = other[row]


def join_quarters(mine, other, mine_far, other_far, joined):
    group, core = lax.axis_index("groups"), lax.axis_index("lon")
    count, half, columns = mine.shape
    for at_group, at_core, block in (
        (group, core, mine),
        (1 - group, core, other),
        (group, 1 - core, mine_far),
        (1 - group, 1 - core, other_far),
    ):
        lanes = pl.ds(pl.multiple_of(at_group * columns, columns), columns)
        for row in range(count):
            first = row * 2 * half + at_core * half
            joined[pl.ds(pl.multiple_of(first, half), half), lanes] = block[row]


def attend_body(*refs):
    near, far, (mine, other) = refs[:4], refs[4:8], refs[8:10]
    pieces, (weights, bias_rows, near_rows, far_rows) = refs[10:14], refs[14:]
    group, side = lax.axis_index("groups"), lax.rem(lax.axis_index("lat"), 2)
    _, count, quarter = pieces[0].shape
    heads = 3
    head_dim = quarter // heads
    join_halves(mine, other, weights)
    for slot in range(4):
        near_rows[slot * count : (slot + 1) * count, :] = near[slot][:count, :]
        far_rows[slot * count : (slot + 1) * count, :] = far[slot][:count, :]
    for flip in range(2):
        for at, block in enumerate((near[flip], far[flip])):
            bias_rows[flip, :, at * count : (at + 1) * count] = block[count:, :count].astype(F32)
    first_head = (2 * side + group) * heads
    here = jnp.dot(near_rows[...], weights[...], preferred_element_type=F32).astype(BF16)
    there = jnp.dot(far_rows[...], weights[:, quarter:], preferred_element_type=F32).astype(BF16)
    for slot in range(4):
        flip, sample = slot % 2, slot // 2
        low_row, high_row = slot * count, (slot + 1) * count
        outs = []
        for head in range(heads):
            low = head * head_dim
            queries = here[low_row:high_row, low : low + head_dim]
            keys, values = (
                jnp.concatenate(
                    [
                        here[low_row:high_row, (kind + 1) * quarter + low :][:, :head_dim],
                        there[low_row:high_row, kind * quarter + low :][:, :head_dim],
                    ]
                )
                for kind in range(2)
            )
            scores = lax.dot_general(
                queries, keys, (((1,), (1,)), ((), ())), preferred_element_type=F32
            ) * (head_dim**-0.5)
            scores = scores + bias_rows[flip, pl.ds(first_head + head, 1), :]
            expd = jnp.exp(scores - jnp.max(scores, axis=-1, keepdims=True))
            totals = jnp.sum(expd, axis=-1, keepdims=True)
            weighted = jnp.dot(expd.astype(BF16), values, preferred_element_type=F32)
            outs.append((weighted / totals).astype(BF16))
        attended = jnp.concatenate(outs, axis=1)
        pieces[2 * sample + flip][0] = attended
        pieces[2 * sample + 1 - flip][1] = attended


def project_out(which, pieces, weights, tokens, gain):
    group, side = lax.axis_index("groups"), lax.rem(lax.axis_index("lat"), 2)
    summed = tokens.astype(F32)
    for slot, piece in enumerate(pieces):
        flip, sample = slot % 2, slot // 2
        quarter = piece.shape[2]
        owner = 2 * (side + flip - 2 * side * flip) + (group + sample - 2 * group * sample)
        rows = pl.ds(pl.multiple_of(owner * quarter, quarter), quarter)
        summed = summed + jnp.dot(piece[which], weights[rows, :], preferred_element_type=F32)
    middle = summed.astype(BF16)
    return middle, norm_rows(middle.astype(F32), gain)


def other_body(gain, piece0, piece1, piece2, piece3, weights, tokens, other_in):
    pieces = (piece0, piece1, piece2, piece3)
    other_in[...] = project_out(1, pieces, weights, tokens[...], gain[...])[1]


def tent_pair(row_count, first_col, col_count, half_width):
    rows = lax.broadcasted_iota(jnp.int32, (row_count, col_count), 0)
    cols = lax.broadcasted_iota(jnp.int32, (row_count, col_count), 1) + first_col
    offset = ((cols - rows + row_count // 2) & (row_count - 1)) - row_count // 2
    distance = jnp.abs(offset).astype(F32)
    span_plus = (half_width + 1).astype(F32)
    tent = jnp.where(
        distance <= half_width.astype(F32), (1.0 - distance / span_plus) / span_plus, 0.0
    )
    odd = tent * offset.astype(F32) / span_plus
    return tent.astype(BF16), odd.astype(BF16)


def mix(lines, blocks, basis):
    size = blocks.shape[2]
    return jnp.concatenate(
        [
            jnp.dot(
                lines[:, tile * size : (tile + 1) * size],
                blocks[basis, tile],
                preferred_element_type=F32,
            ).astype(BF16)
            for tile in range(blocks.shape[1])
        ],
        axis=1,
    )


def plan_body(
    lat_count, lon_half, lat_half, quad_off, taps, w_conv, message, blocks, coeffs, gains
):
    del message
    lat_row, core = lax.axis_index("lat"), lax.axis_index("lon")
    side = lax.rem(lat_row, 2)
    for basis in range(2):
        below, centre, above = (taps[quad_off[0] + row, basis] for row in range(3))
        below = jnp.where(lat_half[0] >= 1, below, 0.0)
        above = jnp.where(lat_half[0] >= 1, above, 0.0)
        other = jnp.where(side == 0, above, below)
        halo = jnp.where(side == 0, below, above)
        pole = jnp.where(lat_row == 0, below, 0.0) + jnp.where(
            lat_row == lat_count - 1, above, 0.0
        )
        for at, value in enumerate((other, centre, halo, pole)):
            gains[4 * basis + at : 4 * basis + at + 1, :] = jnp.full((1, 128), value, F32)
    rows, count = coeffs.shape[0], coeffs.shape[1] // 4
    direct = tent_pair(rows, core * count, count, lon_half[0])
    rolled = tent_pair(rows, core * count + count, count, lon_half[0])
    for at, part in enumerate((direct[0], direct[1], rolled[0], rolled[1])):
        coeffs[:, at * count : (at + 1) * count] = part
    size = w_conv.shape[2]
    blocks[...] = jnp.zeros(blocks.shape, BF16)
    per_block = blocks.shape[2] // size
    for basis in range(blocks.shape[0]):
        for tile in range(blocks.shape[1]):
            for at in range(per_block):
                first = (tile * per_block + at) * size
                low, high = at * size, (at + 1) * size
                blocks[basis, tile, low:high, low:high] = w_conv[basis, first : first + size, :]


def own_body(
    gains,
    gain,
    piece0,
    piece1,
    piece2,
    piece3,
    weights,
    tokens,
    other_in,
    blocks,
    coeffs,
    middle,
    partial,
):
    count = tokens.shape[0]
    pieces = (piece0, piece1, piece2, piece3)
    own_middle, own_in = project_out(0, pieces, weights, tokens[...], gain[...])
    middle[...] = own_middle
    own = own_in.astype(F32)
    neighbour = other_in[...].astype(F32)
    direct, rolled = [], []
    for basis in range(2):
        other, centre, _, pole = (gains[4 * basis + at : 4 * basis + at + 1, :1] for at in range(4))
        lines = jnp.concatenate(
            [(other * neighbour + centre * own).astype(BF16), (pole * own).astype(BF16)]
        )
        mixed = mix(lines, blocks, basis)
        direct.append(mixed[:count])
        rolled.append(mixed[count:])
    partial[...] = jnp.dot(
        coeffs[...], jnp.concatenate(direct + rolled), preferred_element_type=F32
    )


def halo_body(gains, halo, blocks, coeffs, middle, partial, kept, sent, total):
    core = lax.axis_index("lon")
    count = halo.shape[0]
    values = halo[...].astype(F32)
    mixed = [
        mix((gains[4 * basis + 2 : 4 * basis + 3, :1] * values).astype(BF16), blocks, basis)
        for basis in range(2)
    ]
    total[...] = partial[...] + jnp.dot(
        coeffs[:, : 2 * count], jnp.concatenate(mixed), preferred_element_type=F32
    )
    here = pl.multiple_of(core * count, count)
    there = pl.multiple_of((1 - core) * count, count)
    kept[...] = middle[...].astype(F32) + total[pl.ds(here, count), :]
    sent[...] = total[pl.ds(there, count), :].astype(BF16)


def pack_plain(weights, columns):
    core, lat_count = lax.axis_index("lon"), lax.axis_size("lat")
    half, width = weights.shape[0] // 2, weights.shape[1]
    rows = lax.dynamic_slice_in_dim(weights, core * half, half, 0)
    if columns == width // 2:
        rows = lax.dynamic_slice_in_dim(rows, lax.axis_index("groups") * columns, columns, 1)
        return jnp.broadcast_to(rows[None], (lat_count, half, columns))
    rows = rows.reshape(half, 3, 2, 2, columns // 3)
    rows = lax.dynamic_index_in_dim(rows, lax.axis_index("groups"), 3, keepdims=False)
    rows = rows.transpose(2, 0, 1, 3).reshape(2, half, columns)
    rows = jnp.broadcast_to(rows[None], (lat_count // 2, 2, half, columns))
    return rows.reshape(lat_count, half, columns)


def regroup(core, mine, other):
    both = jnp.where(core == 0, jnp.stack([mine, other], 1), jnp.stack([other, mine], 1))
    whole = both.reshape(8, 2, -1, mine.shape[2])
    pick = lambda index: lax.dynamic_index_in_dim(whole, index, 1, keepdims=False)
    return pick(core), pick(1 - core)


def per_device(
    tokens,
    gain_attn,
    w_qkv,
    key_bias,
    w_out,
    gain_conv,
    w_conv,
    lat_taps,
    lon_half,
    lat_half,
    quad_off,
):
    own_tokens = tokens[0]
    count, width = own_tokens.shape
    quarter = width // 4
    lat_count = lax.axis_size("lat")
    core = lax.axis_index("lon")
    half = w_qkv.shape[0] // 2
    gain_conv = gain_conv[None]

    aligned = half % 16 == 0
    outs = [((count + 16, width), BF16), ((count, width), BF16)]
    scratch = [
        pltpu.VMEM(key_bias.shape[1:], BF16),
        pltpu.VMEM((1, width), F32),
        pltpu.SemaphoreType.DMA((3 + lat_count,)),
    ]
    args = (own_tokens, key_bias[0], gain_attn[None])
    if aligned:
        message, raw_tokens, out_pieces = call(
            pack_body,
            outs + [((lat_count, half, width // 2), BF16)],
            [HBM] * 4,
            (*args, w_out),
            10 * count * width,
            scratch,
        )
    else:
        message, raw_tokens = call(
            pack_norm_body, outs, [HBM] * 3, args, 10 * count * width, scratch
        )
        out_pieces = pack_plain(w_out, width // 2)
    out_mine = lax.all_to_all(out_pieces, "lat", 0, 0)

    near = [message, flip_chips(message, 1, 0), flip_chips(message, 0, 1)]
    near.append(flip_chips(near[1], 0, 1))
    far = [swap_cores(block) for block in near]

    size = 4 * w_conv.shape[2]
    diagonal, coeffs, gains = call(
        functools.partial(plan_body, lat_count),
        [
            ((2, width // size, size, size), BF16),
            ((2 * count, 4 * count), BF16),
            ((8, 128), F32),
        ],
        [SMEM] * 4 + [VMEM, ANY],
        (lon_half, lat_half, quad_off, lat_taps, w_conv, message),
        0,
    )
    if aligned:
        (qkv_pieces,) = call(
            pack_qkv_body,
            [((lat_count, half, 3 * quarter), BF16)],
            [HBM, ANY],
            (w_qkv, message),
            0,
            [pltpu.VMEM((half, 3 * width), BF16), pltpu.SemaphoreType.DMA((1,))],
        )
    else:
        qkv_pieces = pack_plain(w_qkv, 3 * quarter)
    qkv_pieces = gate(qkv_pieces, near[1], near[2], out_mine, gains)
    qkv_mine = lax.all_to_all(qkv_pieces, "lat", 0, 0)
    qkv_other = swap_cores(qkv_mine)
    out_other = flip_chips(out_mine, 0, 1)
    out_far = [swap_cores(out_mine), swap_cores(out_other)]
    if not aligned:
        qkv_mine, qkv_other = regroup(core, qkv_mine, qkv_other)
        out_mine, out_far[0] = regroup(core, out_mine, out_far[0])
        out_other, out_far[1] = regroup(core, out_other, out_far[1])
    raw_tokens = gate(raw_tokens, qkv_mine)
    other_tokens = flip_chips(raw_tokens, 1, 0)

    pieces = call(
        attend_body,
        [((2, count, quarter), BF16)] * 4,
        [VMEM] * 10,
        (*near, *far, qkv_mine, qkv_other),
        2 * 1024 * width * 3 * quarter,
        [
            pltpu.VMEM((width, 3 * quarter), BF16),
            pltpu.VMEM((2, 16, 2 * count), F32),
            pltpu.VMEM((4 * count, width), BF16),
            pltpu.VMEM((4 * count, width), BF16),
        ],
    )
    back = [pieces[0]] + [
        flip_chips(piece, flip, sample) for piece, (flip, sample) in zip(pieces[1:], FLIPS)
    ]
    (full_out,) = call(
        join_quarters, [((width, width), BF16)], [VMEM] * 4, (out_mine, out_other, *out_far), 0
    )
    (other_in,) = call(
        other_body,
        [((count, width), BF16)],
        [VMEM] * 7,
        (gain_conv, *back, full_out, other_tokens),
        2 * count * width * width,
    )
    halo = move(other_in, lambda g, l, c: (g, l + 2 - 4 * (l % 2), c))
    middle, partial = call(
        own_body,
        [((count, width), BF16), ((2 * count, width), F32)],
        [VMEM] * 11,
        (gains, gain_conv, *back, full_out, raw_tokens, other_in, diagonal, coeffs),
        2 * count * width * width * 3,
    )
    kept, sent = call(
        halo_body,
        [((count, width), F32), ((count, width), BF16)],
        [VMEM] * 6,
        (gains, halo, diagonal, coeffs, middle, partial),
        2 * 256 * 256 * width,
        [pltpu.VMEM((2 * count, width), F32)],
    )
    received = swap_cores(sent)
    return (kept + received.astype(F32)).astype(BF16)[None]


def solution(mesh):
    return jax.shard_map(
        per_device,
        mesh=mesh,
        in_specs=(
            P(("groups", "lat"), "lon", None),
            P(),
            P("lat", None),
            P("lat", None, "lon"),
            P("lat", None),
            P(),
            P(),
            P(),
            P("lat"),
            P("lat"),
            P("lat"),
        ),
        out_specs=P(("groups", "lat"), "lon", None),
        check_vma=False,
    )
```

```python
import functools

import jax
import jax.numpy as jnp
from jax import lax
from jax.experimental import pallas as pl
from jax.experimental.pallas import tpu as pltpu
from jax.sharding import PartitionSpec as P

AXES = ("groups", "lat", "lon")
VMEM = pl.BlockSpec(memory_space=pltpu.VMEM)
ANY = pl.BlockSpec(memory_space=pl.ANY)
HBM = pl.BlockSpec(memory_space=pltpu.HBM)
FLIPS = ((1, 0), (0, 1), (1, 1))
SMEM = pl.BlockSpec(memory_space=pltpu.SMEM)
BF16 = jnp.bfloat16
F32 = jnp.float32


def call(body, outs, specs, args, flops, scratch=(), limit=32):
    outs = tuple(jax.ShapeDtypeStruct(shape, dtype) for shape, dtype in outs)
    moved = sum(a.size * a.dtype.itemsize for a in args)
    return pl.pallas_call(
        body,
        out_shape=outs,
        in_specs=specs,
        out_specs=tuple(VMEM for _ in outs),
        scratch_shapes=list(scratch),
        compiler_params=pltpu.CompilerParams(vmem_limit_bytes=limit * 1024 * 1024),
        cost_estimate=pl.CostEstimate(flops=flops, bytes_accessed=moved, transcendentals=0),
    )(*args)


def copy_body(*refs):
    refs[-1][...] = refs[0][...]


def gate(value, *after):
    specs = [VMEM] * (1 + len(after))
    return call(copy_body, [(value.shape, value.dtype)], specs, (value, *after), 0)[0]


def device_pairs(target):
    lat_count = lax.axis_size("lat")
    pairs = []
    for group in range(2):
        for row in range(lat_count):
            for core in range(2):
                to = target(group, row, core)
                if 0 <= to[1] < lat_count:
                    source = (group * lat_count + row) * 2 + core
                    pairs.append((source, (to[0] * lat_count + to[1]) * 2 + to[2]))
    return pairs


def move(values, target):
    return lax.ppermute(values, AXES, device_pairs(target))


def swap_cores(values):
    return lax.ppermute(values, "lon", [(0, 1), (1, 0)])


def flip_chips(values, flip, sample):
    return move(values, lambda g, l, c: (g ^ sample, l ^ flip, c))


def norm_rows(values, gain):
    average = jnp.mean(values, axis=-1, keepdims=True)
    centered = values - average
    variance = jnp.mean(centered * centered, axis=-1, keepdims=True)
    return (centered * lax.rsqrt(variance + 1e-05) * gain).astype(BF16)


def pack_body(*refs, weights):
    tokens, bias, gain, message, raw = *refs[:3], *refs[-9:-7]
    count = tokens.shape[0]
    heads, bias_width = bias.shape
    group, core = lax.axis_index("groups"), lax.axis_index("lon")
    side = lax.rem(lax.axis_index("lat"), 2)
    if weights:
        w_qkv, w_out = refs[3:5]
    qkv_own, qkv_cross, out_own, bias_here, gain_here, rows, sems = refs[-7:]
    half = rows.shape[0]
    quarter = qkv_own.shape[1] // 3
    copies = [(gain, gain_here), (bias, bias_here), (tokens, raw)]
    if weights:
        picked = pl.ds(pl.multiple_of(core * half, half), half)
        copies += [(w_qkv.at[picked, :], rows), (w_out.at[picked, :], out_own)]
    fetches = [
        pltpu.make_async_copy(source, target, sems.at[at])
        for at, (source, target) in enumerate(copies)
    ]
    for fetch in fetches:
        fetch.start()
    message[count:, :] = jnp.zeros((16, tokens.shape[1]), BF16)
    for fetch in fetches[:3]:
        fetch.wait()
    message[count : count + heads, :bias_width] = bias_here[...]
    message[:count, :] = norm_rows(raw[...].astype(F32), gain_here[...])
    for fetch in fetches[3:]:
        fetch.wait()
    if not weights:
        return
    for kind in range(3):
        low = 4 * kind * quarter
        block = [rows[:, low + at * quarter : low + (at + 1) * quarter] for at in range(4)]
        sides = [jnp.where(group == 0, block[2 * at], block[2 * at + 1]) for at in range(2)]
        columns = slice(kind * quarter, (kind + 1) * quarter)
        qkv_own[:, columns] = jnp.where(side == 0, sides[0], sides[1])
        qkv_cross[:, columns] = jnp.where(side == 0, sides[1], sides[0])


def bundle_body(own, cross, bundle):
    side = lax.rem(lax.axis_index("lat"), 2)
    bundle[side] = own[...]
    bundle[1 - side] = cross[...]


def join_bundles(mine, other, joined):
    core = lax.axis_index("lon")
    pair = lax.rem(lax.axis_index("lat") // 2, 4)
    for flip, blocks in enumerate(zip(mine, other)):
        away = (pair // 2 + flip // 2 - 2 * (pair // 2) * (flip // 2)) * 2
        away = away + (pair % 2 + flip % 2 - 2 * (pair % 2) * (flip % 2))
        for block, at in zip(blocks, (core, 1 - core)):
            half = block.shape[1]
            for row in range(2):
                first = pl.multiple_of(((away * 2 + row) * 2 + at) * half, half)
                joined[pl.ds(first, half), :] = block[row]


def join_body(*refs):
    join_bundles(refs[:4], refs[4:8], refs[8])


def attend_body(*refs):
    near, far, mine, other = refs[:4], refs[4:8], refs[8:12], refs[12:16]
    pieces, (weights, bias_rows, near_rows, far_rows) = refs[17:21], refs[21:]
    group, side = lax.axis_index("groups"), lax.rem(lax.axis_index("lat"), 2)
    _, count, quarter = pieces[0].shape
    heads = 3
    head_dim = quarter // heads
    join_bundles(mine, other, weights)
    for slot in range(4):
        near_rows[slot * count : (slot + 1) * count, :] = near[slot][:count, :]
        far_rows[slot * count : (slot + 1) * count, :] = far[slot][:count, :]
    for flip in range(2):
        for at, block in enumerate((near[flip], far[flip])):
            bias_rows[flip, :, at * count : (at + 1) * count] = block[count:, :count].astype(F32)
    first_head = (2 * side + group) * heads
    here = jnp.dot(near_rows[...], weights[...], preferred_element_type=F32).astype(BF16)
    there = jnp.dot(far_rows[...], weights[:, quarter:], preferred_element_type=F32).astype(BF16)
    for slot in range(4):
        flip, sample = slot % 2, slot // 2
        low_row, high_row = slot * count, (slot + 1) * count
        outs = []
        for head in range(heads):
            low = head * head_dim
            queries = here[low_row:high_row, low : low + head_dim]
            keys, values = (
                jnp.concatenate(
                    [
                        here[low_row:high_row, (kind + 1) * quarter + low :][:, :head_dim],
                        there[low_row:high_row, kind * quarter + low :][:, :head_dim],
                    ]
                )
                for kind in range(2)
            )
            scores = lax.dot_general(
                queries, keys, (((1,), (1,)), ((), ())), preferred_element_type=F32
            ) * (head_dim**-0.5)
            scores = scores + bias_rows[flip, pl.ds(first_head + head, 1), :]
            expd = jnp.exp(scores - jnp.max(scores, axis=-1, keepdims=True))
            totals = jnp.sum(expd, axis=-1, keepdims=True)
            weighted = jnp.dot(expd.astype(BF16), values, preferred_element_type=F32)
            outs.append((weighted / totals).astype(BF16))
        attended = jnp.concatenate(outs, axis=1)
        pieces[2 * sample + flip][0] = attended
        pieces[2 * sample + 1 - flip][1] = attended


def project_out(which, pieces, weights, tokens, gain):
    group, side = lax.axis_index("groups"), lax.rem(lax.axis_index("lat"), 2)
    summed = tokens.astype(F32)
    for slot, piece in enumerate(pieces):
        flip, sample = slot % 2, slot // 2
        quarter = piece.shape[2]
        owner = 2 * (side + flip - 2 * side * flip) + (group + sample - 2 * group * sample)
        rows = pl.ds(pl.multiple_of(owner * quarter, quarter), quarter)
        summed = summed + jnp.dot(piece[which], weights[rows, :], preferred_element_type=F32)
    middle = summed.astype(BF16)
    return middle, norm_rows(middle.astype(F32), gain)


def other_body(gain, piece0, piece1, piece2, piece3, weights, tokens, other_in):
    pieces = (piece0, piece1, piece2, piece3)
    other_in[...] = project_out(1, pieces, weights, tokens[...], gain[...])[1]


def tent_pair(row_count, first_col, col_count, half_width):
    rows = lax.broadcasted_iota(jnp.int32, (row_count, col_count), 0)
    cols = lax.broadcasted_iota(jnp.int32, (row_count, col_count), 1) + first_col
    offset = ((cols - rows + row_count // 2) & (row_count - 1)) - row_count // 2
    distance = jnp.abs(offset).astype(F32)
    span_plus = (half_width + 1).astype(F32)
    tent = jnp.where(
        distance <= half_width.astype(F32), (1.0 - distance / span_plus) / span_plus, 0.0
    )
    odd = tent * offset.astype(F32) / span_plus
    return tent.astype(BF16), odd.astype(BF16)


def mix(lines, blocks, basis):
    size = blocks.shape[2]
    return jnp.concatenate(
        [
            jnp.dot(
                lines[:, tile * size : (tile + 1) * size],
                blocks[basis, tile],
                preferred_element_type=F32,
            ).astype(BF16)
            for tile in range(blocks.shape[1])
        ],
        axis=1,
    )


def plan_body(
    lat_count, lon_half, lat_half, quad_off, taps, w_conv, message, blocks, coeffs, gains
):
    del message
    lat_row, core = lax.axis_index("lat"), lax.axis_index("lon")
    side = lax.rem(lat_row, 2)
    for basis in range(2):
        below, centre, above = (taps[quad_off[0] + row, basis] for row in range(3))
        below = jnp.where(lat_half[0] >= 1, below, 0.0)
        above = jnp.where(lat_half[0] >= 1, above, 0.0)
        other = jnp.where(side == 0, above, below)
        halo = jnp.where(side == 0, below, above)
        pole = jnp.where(lat_row == 0, below, 0.0) + jnp.where(
            lat_row == lat_count - 1, above, 0.0
        )
        for at, value in enumerate((other, centre, halo, pole)):
            gains[4 * basis + at : 4 * basis + at + 1, :] = jnp.full((1, 128), value, F32)
    rows, count = coeffs.shape[0], coeffs.shape[1] // 4
    direct = tent_pair(rows, core * count, count, lon_half[0])
    rolled = tent_pair(rows, core * count + count, count, lon_half[0])
    for at, part in enumerate((direct[0], direct[1], rolled[0], rolled[1])):
        coeffs[:, at * count : (at + 1) * count] = part
    size = w_conv.shape[2]
    blocks[...] = jnp.zeros(blocks.shape, BF16)
    per_block = blocks.shape[2] // size
    for basis in range(blocks.shape[0]):
        for tile in range(blocks.shape[1]):
            for at in range(per_block):
                first = (tile * per_block + at) * size
                low, high = at * size, (at + 1) * size
                blocks[basis, tile, low:high, low:high] = w_conv[basis, first : first + size, :]


def own_body(
    gains,
    gain,
    piece0,
    piece1,
    piece2,
    piece3,
    weights,
    tokens,
    other_in,
    blocks,
    coeffs,
    middle,
    partial,
):
    count = tokens.shape[0]
    pieces = (piece0, piece1, piece2, piece3)
    own_middle, own_in = project_out(0, pieces, weights, tokens[...], gain[...])
    middle[...] = own_middle
    own = own_in.astype(F32)
    neighbour = other_in[...].astype(F32)
    direct, rolled = [], []
    for basis in range(2):
        other, centre, _, pole = (gains[4 * basis + at : 4 * basis + at + 1, :1] for at in range(4))
        lines = jnp.concatenate(
            [(other * neighbour + centre * own).astype(BF16), (pole * own).astype(BF16)]
        )
        mixed = mix(lines, blocks, basis)
        direct.append(mixed[:count])
        rolled.append(mixed[count:])
    partial[...] = jnp.dot(
        coeffs[...], jnp.concatenate(direct + rolled), preferred_element_type=F32
    )


def halo_body(gains, halo, blocks, coeffs, middle, partial, kept, sent, total):
    core = lax.axis_index("lon")
    count = halo.shape[0]
    values = halo[...].astype(F32)
    mixed = [
        mix((gains[4 * basis + 2 : 4 * basis + 3, :1] * values).astype(BF16), blocks, basis)
        for basis in range(2)
    ]
    total[...] = partial[...] + jnp.dot(
        coeffs[:, : 2 * count], jnp.concatenate(mixed), preferred_element_type=F32
    )
    here = pl.multiple_of(core * count, count)
    there = pl.multiple_of((1 - core) * count, count)
    kept[...] = middle[...].astype(F32) + total[pl.ds(here, count), :]
    sent[...] = total[pl.ds(there, count), :].astype(BF16)


def pack_plain(weights, columns):
    core, lat_count = lax.axis_index("lon"), lax.axis_size("lat")
    half, width = weights.shape[0] // 2, weights.shape[1]
    rows = lax.dynamic_slice_in_dim(weights, core * half, half, 0)
    if columns == width:
        return jnp.broadcast_to(rows[None], (lat_count, half, columns))
    rows = rows.reshape(half, 3, 2, 2, columns // 3)
    rows = lax.dynamic_index_in_dim(rows, lax.axis_index("groups"), 3, keepdims=False)
    rows = rows.transpose(2, 0, 1, 3).reshape(2, half, columns)
    rows = jnp.broadcast_to(rows[None], (lat_count // 2, 2, half, columns))
    return rows.reshape(lat_count, half, columns)


def gather_plain(weights, columns):
    core = lax.axis_index("lon")
    mine = lax.all_to_all(pack_plain(weights, columns), "lat", 0, 0)
    other = swap_cores(mine)
    both = jnp.where(core == 0, jnp.stack([mine, other], 1), jnp.stack([other, mine], 1))
    whole = both.reshape(4, 2, 2, -1, columns)
    pair = lax.rem(lax.axis_index("lat") // 2, 4)
    return [
        [
            lax.dynamic_index_in_dim(
                lax.dynamic_index_in_dim(whole, pair ^ flip, 0, keepdims=False),
                at,
                1,
                keepdims=False,
            )
            for flip in range(4)
        ]
        for at in (core, 1 - core)
    ]


def bundled(own, cross):
    return call(
        bundle_body, [((2, *own.shape), BF16)], [VMEM] * 2, (own, flip_chips(cross, 1, 0)), 0
    )[0]


def flip_levels(bundle):
    return [move(bundle, lambda g, l, c: (g, l ^ (2 * flip), c)) for flip in (1, 2, 3)]


def per_device(
    tokens,
    gain_attn,
    w_qkv,
    key_bias,
    w_out,
    gain_conv,
    w_conv,
    lat_taps,
    lon_half,
    lat_half,
    quad_off,
):
    own_tokens = tokens[0]
    count, width = own_tokens.shape
    quarter = width // 4
    lat_count = lax.axis_size("lat")
    half = w_qkv.shape[0] // 2
    gain_conv = gain_conv[None]

    direct = half % 16 == 0 and lat_count == 8
    outs = [
        ((count + 16, width), BF16),
        ((count, width), BF16),
        ((half, 3 * quarter), BF16),
        ((half, 3 * quarter), BF16),
        ((half, width), BF16),
    ]
    scratch = [
        pltpu.VMEM(key_bias.shape[1:], BF16),
        pltpu.VMEM((1, width), F32),
        pltpu.VMEM((half, 3 * width), BF16),
        pltpu.SemaphoreType.DMA((5,)),
    ]
    args = (own_tokens, key_bias[0], gain_attn[None]) + ((w_qkv, w_out) if direct else ())
    message, raw_tokens, qkv_own, qkv_cross, out_own = call(
        functools.partial(pack_body, weights=direct),
        outs,
        [HBM] * len(args),
        args,
        10 * count * width,
        scratch,
        limit=56,
    )

    near = [message, flip_chips(message, 1, 0), flip_chips(message, 0, 1)]
    near.append(flip_chips(near[1], 0, 1))
    far = [swap_cores(block) for block in near]

    size = 4 * w_conv.shape[2]
    diagonal, coeffs, gains = call(
        functools.partial(plan_body, lat_count),
        [
            ((2, width // size, size, size), BF16),
            ((2 * count, 4 * count), BF16),
            ((8, 128), F32),
        ],
        [SMEM] * 4 + [VMEM, ANY],
        (lon_half, lat_half, quad_off, lat_taps, w_conv, message),
        0,
    )
    if direct:
        qkv_bundle = bundled(qkv_own, qkv_cross)
        out_bundle = bundled(out_own, out_own)
        qkv_mine = [qkv_bundle] + flip_levels(qkv_bundle)
        qkv_other = [swap_cores(block) for block in qkv_mine]
        out_bundle = gate(out_bundle, *qkv_mine[1:])
        out_mine = [out_bundle] + flip_levels(out_bundle)
    else:
        qkv_mine, qkv_other = gather_plain(w_qkv, 3 * quarter)
    raw_tokens = gate(raw_tokens, *qkv_mine[1:])
    other_tokens = flip_chips(raw_tokens, 1, 0)

    pieces = call(
        attend_body,
        [((2, count, quarter), BF16)] * 4,
        [VMEM] * 17,
        (*near, *far, *qkv_mine, *qkv_other, gains),
        2 * 1024 * width * 3 * quarter,
        [
            pltpu.VMEM((width, 3 * quarter), BF16),
            pltpu.VMEM((2, 16, 2 * count), F32),
            pltpu.VMEM((4 * count, width), BF16),
            pltpu.VMEM((4 * count, width), BF16),
        ],
    )
    back = [pieces[0]] + [
        flip_chips(piece, flip, sample) for piece, (flip, sample) in zip(pieces[1:], FLIPS)
    ]
    if direct:
        out_mine = [gate(block, back[1]) for block in out_mine]
        out_other = [swap_cores(block) for block in out_mine]
    else:
        out_mine, out_other = gather_plain(w_out, width)
    (full_out,) = call(
        join_body, [((width, width), BF16)], [VMEM] * 8, (*out_mine, *out_other), 0
    )
    (other_in,) = call(
        other_body,
        [((count, width), BF16)],
        [VMEM] * 7,
        (gain_conv, *back, full_out, other_tokens),
        2 * count * width * width,
    )
    halo = move(other_in, lambda g, l, c: (g, l + 2 - 4 * (l % 2), c))
    middle, partial = call(
        own_body,
        [((count, width), BF16), ((2 * count, width), F32)],
        [VMEM] * 11,
        (gains, gain_conv, *back, full_out, raw_tokens, other_in, diagonal, coeffs),
        2 * count * width * width * 3,
    )
    kept, sent = call(
        halo_body,
        [((count, width), F32), ((count, width), BF16)],
        [VMEM] * 6,
        (gains, halo, diagonal, coeffs, middle, partial),
        2 * 256 * 256 * width,
        [pltpu.VMEM((2 * count, width), F32)],
    )
    received = swap_cores(sent)
    return (kept + received.astype(F32)).astype(BF16)[None]


def solution(mesh):
    return jax.shard_map(
        per_device,
        mesh=mesh,
        in_specs=(
            P(("groups", "lat"), "lon", None),
            P(),
            P("lat", None),
            P("lat", None, "lon"),
            P("lat", None),
            P(),
            P(),
            P(),
            P("lat"),
            P("lat"),
            P("lat"),
        ),
        out_specs=P(("groups", "lat"), "lon", None),
        check_vma=False,
    )
```

```python
import functools

import jax
import jax.numpy as jnp
from jax import lax
from jax.experimental import pallas as pl
from jax.experimental.pallas import tpu as pltpu
from jax.sharding import PartitionSpec as P

AXES = ("groups", "lat", "lon")
VMEM = pl.BlockSpec(memory_space=pltpu.VMEM)
ANY = pl.BlockSpec(memory_space=pl.ANY)
HBM = pl.BlockSpec(memory_space=pltpu.HBM)
FLIPS = ((1, 0), (0, 1), (1, 1))
SMEM = pl.BlockSpec(memory_space=pltpu.SMEM)
BF16 = jnp.bfloat16
F32 = jnp.float32


def call(body, outs, specs, args, flops, scratch=(), limit=32):
    outs = tuple(jax.ShapeDtypeStruct(shape, dtype) for shape, dtype in outs)
    moved = sum(a.size * a.dtype.itemsize for a in args)
    return pl.pallas_call(
        body,
        out_shape=outs,
        in_specs=specs,
        out_specs=tuple(VMEM for _ in outs),
        scratch_shapes=list(scratch),
        compiler_params=pltpu.CompilerParams(vmem_limit_bytes=limit * 1024 * 1024),
        cost_estimate=pl.CostEstimate(flops=flops, bytes_accessed=moved, transcendentals=0),
    )(*args)


def copy_body(*refs):
    refs[-1][...] = refs[0][...]


def gate(value, *after):
    specs = [VMEM] * (1 + len(after))
    return call(copy_body, [(value.shape, value.dtype)], specs, (value, *after), 0)[0]


def device_pairs(target):
    lat_count = lax.axis_size("lat")
    pairs = []
    for group in range(2):
        for row in range(lat_count):
            for core in range(2):
                to = target(group, row, core)
                if 0 <= to[1] < lat_count:
                    source = (group * lat_count + row) * 2 + core
                    pairs.append((source, (to[0] * lat_count + to[1]) * 2 + to[2]))
    return pairs


def move(values, target):
    return lax.ppermute(values, AXES, device_pairs(target))


def swap_cores(values):
    return lax.ppermute(values, "lon", [(0, 1), (1, 0)])


def flip_chips(values, flip, sample):
    return move(values, lambda g, l, c: (g ^ sample, l ^ flip, c))


def norm_rows(values, gain):
    average = jnp.mean(values, axis=-1, keepdims=True)
    centered = values - average
    variance = jnp.mean(centered * centered, axis=-1, keepdims=True)
    return (centered * lax.rsqrt(variance + 1e-05) * gain).astype(BF16)


def pick_columns(rows, side, quarter):
    group = lax.axis_index("groups")
    parts = []
    for kind in range(3):
        low = 4 * kind * quarter
        block = [rows[:, low + at * quarter : low + (at + 1) * quarter] for at in range(4)]
        sides = [jnp.where(group == 0, block[2 * at], block[2 * at + 1]) for at in range(2)]
        parts.append(jnp.where(side == 0, sides[0], sides[1]))
    return jnp.concatenate(parts, axis=1)


def pack_body(*refs, weights):
    tokens, bias, gain = refs[:3]
    message, raw, out_own, bias_here, gain_here, rows, sems = refs[-7:]
    count = tokens.shape[0]
    heads, bias_width = bias.shape
    core = lax.axis_index("lon")
    half = rows.shape[0]
    copies = [(gain, gain_here), (bias, bias_here), (tokens, raw)]
    if weights:
        w_qkv, w_out = refs[3:5]
        picked = pl.ds(pl.multiple_of(core * half, half), half)
        copies += [(w_qkv.at[picked, :], rows), (w_out.at[picked, :], out_own)]
    fetches = [
        pltpu.make_async_copy(source, target, sems.at[at])
        for at, (source, target) in enumerate(copies)
    ]
    for fetch in fetches:
        fetch.start()
    message[count:, :] = jnp.zeros((message.shape[0] - count, tokens.shape[1]), BF16)
    for fetch in fetches[:3]:
        fetch.wait()
    message[count : count + heads, :bias_width] = bias_here[...]
    message[:count, :] = norm_rows(raw[...].astype(F32), gain_here[...][None])
    for fetch in fetches[3:]:
        fetch.wait()
    if weights:
        side = lax.rem(lax.axis_index("lat"), 2)
        cross = pick_columns(rows, 1 - side, tokens.shape[1] // 4)
        message[count + 16 :, : cross.shape[1]] = cross


def columns_body(w_qkv, gains, own):
    del gains
    half = own.shape[0]
    start = pl.multiple_of(lax.axis_index("lon") * half, half)
    rows = w_qkv[pl.ds(start, half), :]
    own[...] = pick_columns(rows, lax.rem(lax.axis_index("lat"), 2), own.shape[1] // 3)


def arrived_body(
    own, by_x, by_y, out_own, out1, out2, out3, gains, bundle, x_block, outs
):
    del by_y, gains
    side = lax.rem(lax.axis_index("lat"), 2)
    rows, width = x_block.shape[0], own.shape[1]
    bundle[side] = own[...]
    bundle[1 - side] = by_x[rows:, :width]
    x_block[...] = by_x[:rows, :]
    for at, block in enumerate((out_own, out1, out2, out3)):
        outs[at] = block[...]


def complete_body(
    bundle, level1, level2, level3, message, x_block, by_y, by_xy, outs, crossed, weights, near, both
):
    rows = x_block.shape[0]
    for at, block in enumerate((bundle, level1, level2, level3)):
        weights[at] = block[...]
    for at, block in enumerate((message, x_block, by_y, by_xy)):
        near[at] = block[:rows, :]
    both[0] = outs[...]
    both[1] = crossed[...]


def pair_away(flip):
    pair = lax.rem(lax.axis_index("lat") // 2, 4)
    high, low = pair // 2, pair % 2
    high = 1 - high if flip // 2 else high
    low = 1 - low if flip % 2 else low
    return 2 * high + low


def join_bundles(mine, other, joined):
    core = lax.axis_index("lon")
    half = mine.shape[2]
    for flip in range(4):
        for block, at in ((mine, core), (other, 1 - core)):
            for row in range(2):
                first = pl.multiple_of(((pair_away(flip) * 2 + row) * 2 + at) * half, half)
                joined[pl.ds(first, half), :] = block[flip, row]


def join_columns(mine, other, joined):
    core, side = lax.axis_index("lon"), lax.rem(lax.axis_index("lat"), 2)
    half = mine.shape[2]
    for flip in range(4):
        for block, at in ((mine, core), (other, 1 - core)):
            for cross, row in enumerate((side, 1 - side)):
                first = pl.multiple_of(((pair_away(flip) * 2 + row) * 2 + at) * half, half)
                joined[pl.ds(first, half), :] = block[cross, flip]


def attend_body(*refs):
    (near, far, mine, other), pieces = refs[:4], refs[4:8]
    weights, bias_rows, near_rows, far_rows = refs[8:]
    group, side = lax.axis_index("groups"), lax.rem(lax.axis_index("lat"), 2)
    _, count, quarter = pieces[0].shape
    heads = 3
    head_dim = quarter // heads
    join_bundles(mine, other, weights)
    for slot in range(4):
        near_rows[slot * count : (slot + 1) * count, :] = near[slot, :count, :]
        far_rows[slot * count : (slot + 1) * count, :] = far[slot, :count, :]
    for flip in range(2):
        for at, block in enumerate((near, far)):
            bias_rows[flip, :, at * count : (at + 1) * count] = block[flip, count:, :count].astype(
                F32
            )
    first_head = (2 * side + group) * heads
    here = jnp.dot(near_rows[...], weights[...], preferred_element_type=F32).astype(BF16)
    there = jnp.dot(far_rows[...], weights[:, quarter:], preferred_element_type=F32).astype(BF16)
    for slot in range(4):
        flip, sample = slot % 2, slot // 2
        low_row, high_row = slot * count, (slot + 1) * count
        outs = []
        for head in range(heads):
            low = head * head_dim
            queries = here[low_row:high_row, low : low + head_dim]
            keys, values = (
                jnp.concatenate(
                    [
                        here[low_row:high_row, (kind + 1) * quarter + low :][:, :head_dim],
                        there[low_row:high_row, kind * quarter + low :][:, :head_dim],
                    ]
                )
                for kind in range(2)
            )
            scores = lax.dot_general(
                queries, keys, (((1,), (1,)), ((), ())), preferred_element_type=F32
            ) * (head_dim**-0.5)
            scores = scores + bias_rows[flip, pl.ds(first_head + head, 1), :]
            expd = jnp.exp(scores - jnp.max(scores, axis=-1, keepdims=True))
            totals = jnp.sum(expd, axis=-1, keepdims=True)
            weighted = jnp.dot(expd.astype(BF16), values, preferred_element_type=F32)
            outs.append((weighted / totals).astype(BF16))
        attended = jnp.concatenate(outs, axis=1)
        pieces[2 * sample + flip][0] = attended
        pieces[2 * sample + 1 - flip][1] = attended


def project_out(which, pieces, weights, tokens, gain):
    group, side = lax.axis_index("groups"), lax.rem(lax.axis_index("lat"), 2)
    summed = tokens.astype(F32)
    for slot, piece in enumerate(pieces):
        flip, sample = slot % 2, slot // 2
        quarter = piece.shape[2]
        owner = 2 * (side + flip - 2 * side * flip) + (group + sample - 2 * group * sample)
        rows = pl.ds(pl.multiple_of(owner * quarter, quarter), quarter)
        summed = summed + jnp.dot(piece[which], weights[rows, :], preferred_element_type=F32)
    middle = summed.astype(BF16)
    return middle, norm_rows(middle.astype(F32), gain)


def other_body(gain, piece0, piece1, piece2, piece3, weights, tokens, other_in):
    pieces = (piece0, piece1, piece2, piece3)
    other_in[...] = project_out(1, pieces, weights, tokens[...], gain[...])[1]


def tent_pair(row_count, first_col, col_count, half_width):
    rows = lax.broadcasted_iota(jnp.int32, (row_count, col_count), 0)
    cols = lax.broadcasted_iota(jnp.int32, (row_count, col_count), 1) + first_col
    offset = ((cols - rows + row_count // 2) & (row_count - 1)) - row_count // 2
    distance = jnp.abs(offset).astype(F32)
    span_plus = (half_width + 1).astype(F32)
    tent = jnp.where(
        distance <= half_width.astype(F32), (1.0 - distance / span_plus) / span_plus, 0.0
    )
    odd = tent * offset.astype(F32) / span_plus
    return tent.astype(BF16), odd.astype(BF16)


def mix(lines, blocks, basis):
    size = blocks.shape[2]
    return jnp.concatenate(
        [
            jnp.dot(
                lines[:, tile * size : (tile + 1) * size],
                blocks[basis, tile],
                preferred_element_type=F32,
            ).astype(BF16)
            for tile in range(blocks.shape[1])
        ],
        axis=1,
    )


def plan_body(
    lat_count, lon_half, lat_half, quad_off, taps, w_conv, message, blocks, coeffs, gains
):
    del message
    lat_row, core = lax.axis_index("lat"), lax.axis_index("lon")
    side = lax.rem(lat_row, 2)
    for basis in range(2):
        below, centre, above = (taps[quad_off[0] + row, basis] for row in range(3))
        below = jnp.where(lat_half[0] >= 1, below, 0.0)
        above = jnp.where(lat_half[0] >= 1, above, 0.0)
        other = jnp.where(side == 0, above, below)
        halo = jnp.where(side == 0, below, above)
        pole = jnp.where(lat_row == 0, below, 0.0) + jnp.where(
            lat_row == lat_count - 1, above, 0.0
        )
        for at, value in enumerate((other, centre, halo, pole)):
            gains[4 * basis + at : 4 * basis + at + 1, :] = jnp.full((1, 128), value, F32)
    rows, count = coeffs.shape[0], coeffs.shape[1] // 4
    direct = tent_pair(rows, core * count, count, lon_half[0])
    rolled = tent_pair(rows, core * count + count, count, lon_half[0])
    for at, part in enumerate((direct[0], direct[1], rolled[0], rolled[1])):
        coeffs[:, at * count : (at + 1) * count] = part
    size = w_conv.shape[2]
    blocks[...] = jnp.zeros(blocks.shape, BF16)
    per_block = blocks.shape[2] // size
    for basis in range(blocks.shape[0]):
        for tile in range(blocks.shape[1]):
            for at in range(per_block):
                first = (tile * per_block + at) * size
                low, high = at * size, (at + 1) * size
                blocks[basis, tile, low:high, low:high] = w_conv[basis, first : first + size, :]


def own_body(
    gains,
    gain,
    piece0,
    piece1,
    piece2,
    piece3,
    weights,
    tokens,
    other_in,
    blocks,
    coeffs,
    middle,
    partial,
):
    count = tokens.shape[0]
    pieces = (piece0, piece1, piece2, piece3)
    own_middle, own_in = project_out(0, pieces, weights, tokens[...], gain[...])
    middle[...] = own_middle
    own = own_in.astype(F32)
    neighbour = other_in[...].astype(F32)
    direct, rolled = [], []
    for basis in range(2):
        other, centre, _, pole = (gains[4 * basis + at : 4 * basis + at + 1, :1] for at in range(4))
        lines = jnp.concatenate(
            [(other * neighbour + centre * own).astype(BF16), (pole * own).astype(BF16)]
        )
        mixed = mix(lines, blocks, basis)
        direct.append(mixed[:count])
        rolled.append(mixed[count:])
    partial[...] = jnp.dot(
        coeffs[...], jnp.concatenate(direct + rolled), preferred_element_type=F32
    )


def halo_body(gains, halo, blocks, coeffs, middle, partial, kept, sent, total):
    core = lax.axis_index("lon")
    count = halo.shape[0]
    values = halo[...].astype(F32)
    mixed = [
        mix((gains[4 * basis + 2 : 4 * basis + 3, :1] * values).astype(BF16), blocks, basis)
        for basis in range(2)
    ]
    total[...] = partial[...] + jnp.dot(
        coeffs[:, : 2 * count], jnp.concatenate(mixed), preferred_element_type=F32
    )
    here = pl.multiple_of(core * count, count)
    there = pl.multiple_of((1 - core) * count, count)
    kept[...] = middle[...].astype(F32) + total[pl.ds(here, count), :]
    sent[...] = total[pl.ds(there, count), :].astype(BF16)


def pack_plain(weights, columns):
    core, lat_count = lax.axis_index("lon"), lax.axis_size("lat")
    half, width = weights.shape[0] // 2, weights.shape[1]
    rows = lax.dynamic_slice_in_dim(weights, core * half, half, 0)
    if columns == width:
        return jnp.broadcast_to(rows[None], (lat_count, half, columns))
    rows = rows.reshape(half, 3, 2, 2, columns // 3)
    rows = lax.dynamic_index_in_dim(rows, lax.axis_index("groups"), 3, keepdims=False)
    rows = rows.transpose(2, 0, 1, 3).reshape(2, half, columns)
    rows = jnp.broadcast_to(rows[None], (lat_count // 2, 2, half, columns))
    return rows.reshape(lat_count, half, columns)


def gather_plain(weights, columns):
    core = lax.axis_index("lon")
    mine = lax.all_to_all(pack_plain(weights, columns), "lat", 0, 0)
    other = swap_cores(mine)
    both = jnp.where(core == 0, jnp.stack([mine, other], 1), jnp.stack([other, mine], 1))
    whole = both.reshape(4, 2, 2, -1, columns)
    pair = lax.rem(lax.axis_index("lat") // 2, 4)
    whole = jnp.stack(
        [lax.dynamic_index_in_dim(whole, pair ^ flip, 0, keepdims=False) for flip in range(4)]
    )
    return [
        lax.dynamic_index_in_dim(whole, at, 2, keepdims=False) for at in (core, 1 - core)
    ]


def flip_levels(bundle):
    return [move(bundle, lambda g, l, c: (g, l ^ (2 * flip), c)) for flip in (1, 2, 3)]


def per_device(
    tokens,
    gain_attn,
    w_qkv,
    key_bias,
    w_out,
    gain_conv,
    w_conv,
    lat_taps,
    lon_half,
    lat_half,
    quad_off,
):
    own_tokens = tokens[0]
    count, width = own_tokens.shape
    quarter = width // 4
    lat_count = lax.axis_size("lat")
    half = w_qkv.shape[0] // 2
    gain_conv = gain_conv[None]

    direct = half % 16 == 0 and lat_count == 8
    rows = count + 16
    message, raw_tokens, out_own = call(
        functools.partial(pack_body, weights=direct),
        [
            ((rows + (half if direct else 0), width), BF16),
            ((count, width), BF16),
            ((half, width), BF16),
        ],
        [HBM] * (5 if direct else 3),
        (own_tokens, key_bias[0], gain_attn) + ((w_qkv, w_out) if direct else ()),
        10 * count * width,
        [
            pltpu.VMEM(key_bias.shape[1:], BF16),
            pltpu.VMEM((width,), F32),
            pltpu.VMEM((half, 3 * width), BF16),
            pltpu.SemaphoreType.DMA((5,)),
        ],
        limit=56,
    )

    size = 4 * w_conv.shape[2]
    diagonal, coeffs, gains = call(
        functools.partial(plan_body, lat_count),
        [
            ((2, width // size, size, size), BF16),
            ((2 * count, 4 * count), BF16),
            ((8, 128), F32),
        ],
        [SMEM] * 4 + [VMEM, ANY],
        (lon_half, lat_half, quad_off, lat_taps, w_conv, message),
        0,
    )
    by_x, by_y = flip_chips(message, 1, 0), flip_chips(message, 0, 1)
    if direct:
        (qkv_own,) = call(
            columns_body, [((half, 3 * quarter), BF16)], [VMEM] * 2, (w_qkv, gains), 0
        )
        bundle, x_block, outs = call(
            arrived_body,
            [
                ((2, half, 3 * quarter), BF16),
                ((rows, width), BF16),
                ((4, half, width), BF16),
            ],
            [VMEM] * 8,
            (qkv_own, by_x, by_y, out_own, *flip_levels(out_own), gains),
            0,
        )
        qkv_mine, near, out_mine = call(
            complete_body,
            [
                ((4, 2, half, 3 * quarter), BF16),
                ((4, rows, width), BF16),
                ((2, 4, half, width), BF16),
            ],
            [VMEM] * 10,
            (
                bundle,
                *flip_levels(bundle),
                message,
                x_block,
                by_y,
                flip_chips(x_block, 0, 1),
                outs,
                flip_chips(outs, 1, 0),
            ),
            0,
        )
        qkv_other, out_other = swap_cores(qkv_mine), swap_cores(out_mine)
        join = join_columns
    else:
        near = jnp.stack([message, by_x, by_y, flip_chips(by_x, 0, 1)])
        qkv_mine, qkv_other = gather_plain(w_qkv, 3 * quarter)
        out_mine, out_other = gather_plain(w_out, width)
        join = join_bundles
    far = swap_cores(near)
    raw_tokens = gate(raw_tokens, qkv_mine)
    other_tokens = flip_chips(raw_tokens, 1, 0)

    pieces = call(
        attend_body,
        [((2, count, quarter), BF16)] * 4,
        [VMEM] * 4,
        (near, far, qkv_mine, qkv_other),
        2 * 1024 * width * 3 * quarter,
        [
            pltpu.VMEM((width, 3 * quarter), BF16),
            pltpu.VMEM((2, 16, 2 * count), F32),
            pltpu.VMEM((4 * count, width), BF16),
            pltpu.VMEM((4 * count, width), BF16),
        ],
    )
    back = [pieces[0]] + [
        flip_chips(piece, flip, sample) for piece, (flip, sample) in zip(pieces[1:], FLIPS)
    ]
    (full_out,) = call(
        join, [((width, width), BF16)], [VMEM] * 2, (out_mine, out_other), 0
    )
    (other_in,) = call(
        other_body,
        [((count, width), BF16)],
        [VMEM] * 7,
        (gain_conv, *back, full_out, other_tokens),
        2 * count * width * width,
    )
    halo = move(other_in, lambda g, l, c: (g, l + 2 - 4 * (l % 2), c))
    middle, partial = call(
        own_body,
        [((count, width), BF16), ((2 * count, width), F32)],
        [VMEM] * 11,
        (gains, gain_conv, *back, full_out, raw_tokens, other_in, diagonal, coeffs),
        2 * count * width * width * 3,
    )
    kept, sent = call(
        halo_body,
        [((count, width), F32), ((count, width), BF16)],
        [VMEM] * 6,
        (gains, halo, diagonal, coeffs, middle, partial),
        2 * 256 * 256 * width,
        [pltpu.VMEM((2 * count, width), F32)],
    )
    received = swap_cores(sent)
    return (kept + received.astype(F32)).astype(BF16)[None]


def solution(mesh):
    return jax.shard_map(
        per_device,
        mesh=mesh,
        in_specs=(
            P(("groups", "lat"), "lon", None),
            P(),
            P("lat", None),
            P("lat", None, "lon"),
            P("lat", None),
            P(),
            P(),
            P(),
            P("lat"),
            P("lat"),
            P("lat"),
        ),
        out_specs=P(("groups", "lat"), "lon", None),
        check_vma=False,
    )
```

```python
import functools

import jax
import jax.numpy as jnp
from jax import lax
from jax.experimental import pallas as pl
from jax.experimental.pallas import tpu as pltpu
from jax.sharding import PartitionSpec as P

AXES = ("groups", "lat", "lon")
VMEM = pl.BlockSpec(memory_space=pltpu.VMEM)
ANY = pl.BlockSpec(memory_space=pl.ANY)
HBM = pl.BlockSpec(memory_space=pltpu.HBM)
FLIPS = ((1, 0), (0, 1), (1, 1))
SMEM = pl.BlockSpec(memory_space=pltpu.SMEM)
BF16 = jnp.bfloat16
F32 = jnp.float32


def call(body, outs, specs, args, flops, scratch=(), limit=32):
    outs = tuple(jax.ShapeDtypeStruct(shape, dtype) for shape, dtype in outs)
    moved = sum(a.size * a.dtype.itemsize for a in args)
    return pl.pallas_call(
        body,
        out_shape=outs,
        in_specs=specs,
        out_specs=tuple(VMEM for _ in outs),
        scratch_shapes=list(scratch),
        compiler_params=pltpu.CompilerParams(vmem_limit_bytes=limit * 1024 * 1024),
        cost_estimate=pl.CostEstimate(flops=flops, bytes_accessed=moved, transcendentals=0),
    )(*args)


def device_pairs(target):
    lat_count = lax.axis_size("lat")
    pairs = []
    for group in range(2):
        for row in range(lat_count):
            for core in range(2):
                to = target(group, row, core)
                if 0 <= to[1] < lat_count:
                    source = (group * lat_count + row) * 2 + core
                    pairs.append((source, (to[0] * lat_count + to[1]) * 2 + to[2]))
    return pairs


def move(values, target):
    return lax.ppermute(values, AXES, device_pairs(target))


def swap_cores(values):
    return lax.ppermute(values, "lon", [(0, 1), (1, 0)])


def flip_chips(values, flip, sample):
    return move(values, lambda g, l, c: (g ^ sample, l ^ flip, c))


def norm_rows(values, gain):
    average = jnp.mean(values, axis=-1, keepdims=True)
    centered = values - average
    variance = jnp.mean(centered * centered, axis=-1, keepdims=True)
    return (centered * lax.rsqrt(variance + 1e-05) * gain).astype(BF16)


def pick_columns(rows, side, quarter):
    group = lax.axis_index("groups")
    parts = []
    for kind in range(3):
        low = 4 * kind * quarter
        block = [rows[:, low + at * quarter : low + (at + 1) * quarter] for at in range(4)]
        sides = [jnp.where(group == 0, block[2 * at], block[2 * at + 1]) for at in range(2)]
        parts.append(jnp.where(side == 0, sides[0], sides[1]))
    return jnp.concatenate(parts, axis=1)


def pack_body(*refs, weights):
    tokens, bias, gain = refs[:3]
    message, with_raw, raw, qkv_both, out_own, bias_here, gain_here, rows, sems = refs[-9:]
    count = tokens.shape[0]
    heads, bias_width = bias.shape
    core = lax.axis_index("lon")
    half = rows.shape[0]
    copies = [(gain, gain_here), (bias, bias_here), (tokens, raw)]
    if weights:
        w_qkv, w_out = refs[3:5]
        picked = pl.ds(pl.multiple_of(core * half, half), half)
        copies += [(w_qkv.at[picked, :], rows), (w_out.at[picked, :], out_own)]
    fetches = [
        pltpu.make_async_copy(source, target, sems.at[at])
        for at, (source, target) in enumerate(copies)
    ]
    for fetch in fetches:
        fetch.start()
    message[count:, :] = jnp.zeros((message.shape[0] - count, tokens.shape[1]), BF16)
    for fetch in fetches[:3]:
        fetch.wait()
    message[count : count + heads, :bias_width] = bias_here[...]
    message[:count, :] = norm_rows(raw[...].astype(F32), gain_here[...][None])
    with_raw[: count + 16, :] = message[...]
    with_raw[count + 16 :, :] = raw[...]
    for fetch in fetches[3:]:
        fetch.wait()
    if weights:
        side = lax.rem(lax.axis_index("lat"), 2)
        columns = qkv_both.shape[1] // 2
        qkv_both[:, :columns] = pick_columns(rows, side, columns // 3)
        qkv_both[:, columns:] = pick_columns(rows, 1 - side, columns // 3)


def arrived_body(
    own, level1, level2, level3, by_x, by_y, out_own, gains, mine, cross, x_block, raw_x, outs
):
    del by_y, gains
    columns = mine.shape[2]
    rows = x_block.shape[0]
    for at, block in enumerate((own, level1, level2, level3)):
        mine[at] = block[:, :columns]
        cross[at] = block[:, columns:]
    x_block[...] = by_x[:rows, :]
    raw_x[...] = by_x[rows:, :]
    outs[...] = out_own[...]


def complete_body(
    mine, crossed, message, x_block, by_y, by_xy, own, level1, level2, level3, weights, near, outs
):
    weights[0] = mine[...]
    weights[1] = crossed[...]
    for at, block in enumerate((message, x_block, by_y, by_xy)):
        near[at] = block[...]
    for at, block in enumerate((own, level1, level2, level3)):
        outs[at] = block[...]


def pair_body(mine, crossed, after, both):
    del after
    both[0] = mine[...]
    both[1] = crossed[...]


def pair_away(flip):
    pair = lax.rem(lax.axis_index("lat") // 2, 4)
    high, low = pair // 2, pair % 2
    high = 1 - high if flip // 2 else high
    low = 1 - low if flip % 2 else low
    return 2 * high + low


def join_bundles(mine, other, joined):
    core = lax.axis_index("lon")
    half = mine.shape[2]
    for flip in range(4):
        for block, at in ((mine, core), (other, 1 - core)):
            for row in range(2):
                first = pl.multiple_of(((pair_away(flip) * 2 + row) * 2 + at) * half, half)
                joined[pl.ds(first, half), :] = block[flip, row]


def join_columns(mine, other, joined):
    core, side = lax.axis_index("lon"), lax.rem(lax.axis_index("lat"), 2)
    half = mine.shape[2]
    for flip in range(4):
        for block, at in ((mine, core), (other, 1 - core)):
            for cross, row in enumerate((side, 1 - side)):
                first = pl.multiple_of(((pair_away(flip) * 2 + row) * 2 + at) * half, half)
                joined[pl.ds(first, half), :] = block[cross, flip]


def attend_body(join, *refs):
    near, far, mine, other = refs[:4]
    pieces, (weights, bias_rows, near_rows, far_rows) = refs[4:8], refs[8:]
    group, side = lax.axis_index("groups"), lax.rem(lax.axis_index("lat"), 2)
    _, count, quarter = pieces[0].shape
    heads = 3
    head_dim = quarter // heads
    join(mine, other, weights)
    for slot in range(4):
        near_rows[slot * count : (slot + 1) * count, :] = near[slot, :count, :]
        far_rows[slot * count : (slot + 1) * count, :] = far[slot, :count, :]
    for flip in range(2):
        for at, block in enumerate((near, far)):
            bias_rows[flip, :, at * count : (at + 1) * count] = block[flip, count:, :count].astype(
                F32
            )
    first_head = (2 * side + group) * heads
    here = jnp.dot(near_rows[...], weights[...], preferred_element_type=F32).astype(BF16)
    there = jnp.dot(far_rows[...], weights[:, quarter:], preferred_element_type=F32).astype(BF16)
    for slot in range(4):
        flip, sample = slot % 2, slot // 2
        low_row, high_row = slot * count, (slot + 1) * count
        outs = []
        for head in range(heads):
            low = head * head_dim
            queries = here[low_row:high_row, low : low + head_dim]
            keys, values = (
                jnp.concatenate(
                    [
                        here[low_row:high_row, (kind + 1) * quarter + low :][:, :head_dim],
                        there[low_row:high_row, kind * quarter + low :][:, :head_dim],
                    ]
                )
                for kind in range(2)
            )
            scores = lax.dot_general(
                queries, keys, (((1,), (1,)), ((), ())), preferred_element_type=F32
            ) * (head_dim**-0.5)
            scores = scores + bias_rows[flip, pl.ds(first_head + head, 1), :]
            expd = jnp.exp(scores - jnp.max(scores, axis=-1, keepdims=True))
            totals = jnp.sum(expd, axis=-1, keepdims=True)
            weighted = jnp.dot(expd.astype(BF16), values, preferred_element_type=F32)
            outs.append((weighted / totals).astype(BF16))
        attended = jnp.concatenate(outs, axis=1)
        pieces[2 * sample + flip][0] = attended
        pieces[2 * sample + 1 - flip][1] = attended


def project_out(which, pieces, weights, tokens, gain):
    group, side = lax.axis_index("groups"), lax.rem(lax.axis_index("lat"), 2)
    summed = tokens.astype(F32)
    for slot, piece in enumerate(pieces):
        flip, sample = slot % 2, slot // 2
        quarter = piece.shape[2]
        owner = 2 * (side + flip - 2 * side * flip) + (group + sample - 2 * group * sample)
        rows = pl.ds(pl.multiple_of(owner * quarter, quarter), quarter)
        summed = summed + jnp.dot(piece[which], weights[rows, :], preferred_element_type=F32)
    middle = summed.astype(BF16)
    return middle, norm_rows(middle.astype(F32), gain)


def other_body(gain, piece0, piece1, piece2, piece3, weights, tokens, other_in):
    pieces = (piece0, piece1, piece2, piece3)
    other_in[...] = project_out(1, pieces, weights, tokens[...], gain[...])[1]


def tent_pair(row_count, first_col, col_count, half_width):
    rows = lax.broadcasted_iota(jnp.int32, (row_count, col_count), 0)
    cols = lax.broadcasted_iota(jnp.int32, (row_count, col_count), 1) + first_col
    offset = ((cols - rows + row_count // 2) & (row_count - 1)) - row_count // 2
    distance = jnp.abs(offset).astype(F32)
    span_plus = (half_width + 1).astype(F32)
    tent = jnp.where(
        distance <= half_width.astype(F32), (1.0 - distance / span_plus) / span_plus, 0.0
    )
    odd = tent * offset.astype(F32) / span_plus
    return tent.astype(BF16), odd.astype(BF16)


def mix(lines, blocks, basis):
    size = blocks.shape[2]
    return jnp.concatenate(
        [
            jnp.dot(
                lines[:, tile * size : (tile + 1) * size],
                blocks[basis, tile],
                preferred_element_type=F32,
            ).astype(BF16)
            for tile in range(blocks.shape[1])
        ],
        axis=1,
    )


def plan_body(
    lat_count, lon_half, lat_half, quad_off, taps, w_conv, message, blocks, coeffs, gains
):
    del message
    lat_row, core = lax.axis_index("lat"), lax.axis_index("lon")
    side = lax.rem(lat_row, 2)
    for basis in range(2):
        below, centre, above = (taps[quad_off[0] + row, basis] for row in range(3))
        below = jnp.where(lat_half[0] >= 1, below, 0.0)
        above = jnp.where(lat_half[0] >= 1, above, 0.0)
        other = jnp.where(side == 0, above, below)
        halo = jnp.where(side == 0, below, above)
        pole = jnp.where(lat_row == 0, below, 0.0) + jnp.where(
            lat_row == lat_count - 1, above, 0.0
        )
        for at, value in enumerate((other, centre, halo, pole)):
            gains[4 * basis + at : 4 * basis + at + 1, :] = jnp.full((1, 128), value, F32)
    rows, count = coeffs.shape[0], coeffs.shape[1] // 4
    direct = tent_pair(rows, core * count, count, lon_half[0])
    rolled = tent_pair(rows, core * count + count, count, lon_half[0])
    for at, part in enumerate((direct[0], direct[1], rolled[0], rolled[1])):
        coeffs[:, at * count : (at + 1) * count] = part
    size = w_conv.shape[2]
    blocks[...] = jnp.zeros(blocks.shape, BF16)
    per_block = blocks.shape[2] // size
    for basis in range(blocks.shape[0]):
        for tile in range(blocks.shape[1]):
            for at in range(per_block):
                first = (tile * per_block + at) * size
                low, high = at * size, (at + 1) * size
                blocks[basis, tile, low:high, low:high] = w_conv[basis, first : first + size, :]


def own_body(
    gains,
    gain,
    piece0,
    piece1,
    piece2,
    piece3,
    weights,
    tokens,
    other_in,
    blocks,
    coeffs,
    middle,
    partial,
):
    count = tokens.shape[0]
    pieces = (piece0, piece1, piece2, piece3)
    own_middle, own_in = project_out(0, pieces, weights, tokens[...], gain[...])
    middle[...] = own_middle
    own = own_in.astype(F32)
    neighbour = other_in[...].astype(F32)
    direct, rolled = [], []
    for basis in range(2):
        other, centre, _, pole = (gains[4 * basis + at : 4 * basis + at + 1, :1] for at in range(4))
        lines = jnp.concatenate(
            [(other * neighbour + centre * own).astype(BF16), (pole * own).astype(BF16)]
        )
        mixed = mix(lines, blocks, basis)
        direct.append(mixed[:count])
        rolled.append(mixed[count:])
    partial[...] = jnp.dot(
        coeffs[...], jnp.concatenate(direct + rolled), preferred_element_type=F32
    )


def halo_body(gains, halo, blocks, coeffs, middle, partial, kept, sent, total):
    core = lax.axis_index("lon")
    count = halo.shape[0]
    values = halo[...].astype(F32)
    mixed = [
        mix((gains[4 * basis + 2 : 4 * basis + 3, :1] * values).astype(BF16), blocks, basis)
        for basis in range(2)
    ]
    total[...] = partial[...] + jnp.dot(
        coeffs[:, : 2 * count], jnp.concatenate(mixed), preferred_element_type=F32
    )
    here = pl.multiple_of(core * count, count)
    there = pl.multiple_of((1 - core) * count, count)
    kept[...] = middle[...].astype(F32) + total[pl.ds(here, count), :]
    sent[...] = total[pl.ds(there, count), :].astype(BF16)


def pack_plain(weights, columns):
    core, lat_count = lax.axis_index("lon"), lax.axis_size("lat")
    half, width = weights.shape[0] // 2, weights.shape[1]
    rows = lax.dynamic_slice_in_dim(weights, core * half, half, 0)
    if columns == width:
        return jnp.broadcast_to(rows[None], (lat_count, half, columns))
    rows = rows.reshape(half, 3, 2, 2, columns // 3)
    rows = lax.dynamic_index_in_dim(rows, lax.axis_index("groups"), 3, keepdims=False)
    rows = rows.transpose(2, 0, 1, 3).reshape(2, half, columns)
    rows = jnp.broadcast_to(rows[None], (lat_count // 2, 2, half, columns))
    return rows.reshape(lat_count, half, columns)


def gather_plain(weights, columns):
    core = lax.axis_index("lon")
    mine = lax.all_to_all(pack_plain(weights, columns), "lat", 0, 0)
    other = swap_cores(mine)
    both = jnp.where(core == 0, jnp.stack([mine, other], 1), jnp.stack([other, mine], 1))
    whole = both.reshape(4, 2, 2, -1, columns)
    pair = lax.rem(lax.axis_index("lat") // 2, 4)
    whole = jnp.stack(
        [lax.dynamic_index_in_dim(whole, pair ^ flip, 0, keepdims=False) for flip in range(4)]
    )
    return [
        lax.dynamic_index_in_dim(whole, at, 2, keepdims=False) for at in (core, 1 - core)
    ]


def flip_levels(bundle):
    return [move(bundle, lambda g, l, c: (g, l ^ (2 * flip), c)) for flip in (1, 2, 3)]


def per_device(
    tokens,
    gain_attn,
    w_qkv,
    key_bias,
    w_out,
    gain_conv,
    w_conv,
    lat_taps,
    lon_half,
    lat_half,
    quad_off,
):
    own_tokens = tokens[0]
    count, width = own_tokens.shape
    quarter = width // 4
    lat_count = lax.axis_size("lat")
    half = w_qkv.shape[0] // 2
    gain_conv = gain_conv[None]

    direct = half % 16 == 0 and lat_count == 8
    rows = count + 16
    message, with_raw, raw_tokens, qkv_both, out_own = call(
        functools.partial(pack_body, weights=direct),
        [
            ((rows, width), BF16),
            ((rows + count, width), BF16),
            ((count, width), BF16),
            ((half, 6 * quarter), BF16),
            ((half, width), BF16),
        ],
        [HBM] * (5 if direct else 3),
        (own_tokens, key_bias[0], gain_attn) + ((w_qkv, w_out) if direct else ()),
        10 * count * width,
        [
            pltpu.VMEM(key_bias.shape[1:], BF16),
            pltpu.VMEM((width,), F32),
            pltpu.VMEM((half, 3 * width), BF16),
            pltpu.SemaphoreType.DMA((5,)),
        ],
        limit=56,
    )

    size = 4 * w_conv.shape[2]
    diagonal, coeffs, gains = call(
        functools.partial(plan_body, lat_count),
        [
            ((2, width // size, size, size), BF16),
            ((2 * count, 4 * count), BF16),
            ((8, 128), F32),
        ],
        [SMEM] * 4 + [VMEM, ANY],
        (lon_half, lat_half, quad_off, lat_taps, w_conv, message),
        0,
    )
    by_x, by_y = flip_chips(with_raw, 1, 0), flip_chips(message, 0, 1)
    if direct:
        mine, cross, x_block, other_tokens, outs = call(
            arrived_body,
            [
                ((4, half, 3 * quarter), BF16),
                ((4, half, 3 * quarter), BF16),
                ((rows, width), BF16),
                ((count, width), BF16),
                ((half, width), BF16),
            ],
            [VMEM] * 8,
            (qkv_both, *flip_levels(qkv_both), by_x, by_y, out_own, gains),
            0,
        )
        qkv_mine, near, outs = call(
            complete_body,
            [
                ((2, 4, half, 3 * quarter), BF16),
                ((4, rows, width), BF16),
                ((4, half, width), BF16),
            ],
            [VMEM] * 10,
            (
                mine,
                flip_chips(cross, 1, 0),
                message,
                x_block,
                by_y,
                flip_chips(x_block, 0, 1),
                outs,
                *flip_levels(outs),
            ),
            0,
        )
        qkv_other = swap_cores(qkv_mine)
        join = join_columns
    else:
        x_block, other_tokens = by_x[:rows], by_x[rows:]
        near = jnp.stack([message, x_block, by_y, flip_chips(x_block, 0, 1)])
        qkv_mine, qkv_other = gather_plain(w_qkv, 3 * quarter)
        outs, out_other = gather_plain(w_out, width)
        join = join_bundles
    far = swap_cores(near)

    pieces = call(
        functools.partial(attend_body, join),
        [((2, count, quarter), BF16)] * 4,
        [VMEM] * 4,
        (near, far, qkv_mine, qkv_other),
        2 * 1024 * width * 3 * quarter,
        [
            pltpu.VMEM((width, 3 * quarter), BF16),
            pltpu.VMEM((2, 16, 2 * count), F32),
            pltpu.VMEM((4 * count, width), BF16),
            pltpu.VMEM((4 * count, width), BF16),
        ],
    )
    back = [pieces[0]] + [
        flip_chips(piece, flip, sample) for piece, (flip, sample) in zip(pieces[1:], FLIPS)
    ]
    if direct:
        (outs,) = call(
            pair_body,
            [((2, 4, half, width), BF16)],
            [VMEM] * 3,
            (outs, flip_chips(outs, 1, 0), pieces[0]),
            0,
        )
        out_other = swap_cores(outs)
    (full_out,) = call(join, [((width, width), BF16)], [VMEM] * 2, (outs, out_other), 0)
    (other_in,) = call(
        other_body,
        [((count, width), BF16)],
        [VMEM] * 7,
        (gain_conv, *back, full_out, other_tokens),
        2 * count * width * width,
    )
    halo = move(other_in, lambda g, l, c: (g, l + 2 - 4 * (l % 2), c))
    middle, partial = call(
        own_body,
        [((count, width), BF16), ((2 * count, width), F32)],
        [VMEM] * 11,
        (gains, gain_conv, *back, full_out, raw_tokens, other_in, diagonal, coeffs),
        2 * count * width * width * 3,
    )
    kept, sent = call(
        halo_body,
        [((count, width), F32), ((count, width), BF16)],
        [VMEM] * 6,
        (gains, halo, diagonal, coeffs, middle, partial),
        2 * 256 * 256 * width,
        [pltpu.VMEM((2 * count, width), F32)],
    )
    received = swap_cores(sent)
    return (kept + received.astype(F32)).astype(BF16)[None]


def solution(mesh):
    return jax.shard_map(
        per_device,
        mesh=mesh,
        in_specs=(
            P(("groups", "lat"), "lon", None),
            P(),
            P("lat", None),
            P("lat", None, "lon"),
            P("lat", None),
            P(),
            P(),
            P(),
            P("lat"),
            P("lat"),
            P("lat"),
        ),
        out_specs=P(("groups", "lat"), "lon", None),
        check_vma=False,
    )
```

```python
import functools

import jax
import jax.numpy as jnp
from jax import lax
from jax.experimental import pallas as pl
from jax.experimental.pallas import tpu as pltpu
from jax.sharding import PartitionSpec as P

AXES = ("groups", "lat", "lon")
VMEM = pl.BlockSpec(memory_space=pltpu.VMEM)
ANY = pl.BlockSpec(memory_space=pl.ANY)
HBM = pl.BlockSpec(memory_space=pltpu.HBM)
FLIPS = ((1, 0), (0, 1), (1, 1))
SMEM = pl.BlockSpec(memory_space=pltpu.SMEM)
BF16 = jnp.bfloat16
F32 = jnp.float32


def call(body, outs, specs, args, flops, scratch=(), limit=32):
    outs = tuple(jax.ShapeDtypeStruct(shape, dtype) for shape, dtype in outs)
    moved = sum(a.size * a.dtype.itemsize for a in args)
    return pl.pallas_call(
        body,
        out_shape=outs,
        in_specs=specs,
        out_specs=tuple(VMEM for _ in outs),
        scratch_shapes=list(scratch),
        compiler_params=pltpu.CompilerParams(vmem_limit_bytes=limit * 1024 * 1024),
        cost_estimate=pl.CostEstimate(flops=flops, bytes_accessed=moved, transcendentals=0),
    )(*args)


def copy_body(*refs):
    refs[-1][...] = refs[0][...]


def gate(value, *after):
    specs = [VMEM] * (1 + len(after))
    return call(copy_body, [(value.shape, value.dtype)], specs, (value, *after), 0)[0]


def device_pairs(target):
    lat_count = lax.axis_size("lat")
    pairs = []
    for group in range(2):
        for row in range(lat_count):
            for core in range(2):
                to = target(group, row, core)
                if 0 <= to[1] < lat_count:
                    source = (group * lat_count + row) * 2 + core
                    pairs.append((source, (to[0] * lat_count + to[1]) * 2 + to[2]))
    return pairs


def move(values, target):
    return lax.ppermute(values, AXES, device_pairs(target))


def swap_cores(values):
    return lax.ppermute(values, "lon", [(0, 1), (1, 0)])


def flip_chips(values, flip, sample):
    return move(values, lambda g, l, c: (g ^ sample, l ^ flip, c))


def norm_rows(values, gain):
    average = jnp.mean(values, axis=-1, keepdims=True)
    centered = values - average
    variance = jnp.mean(centered * centered, axis=-1, keepdims=True)
    return (centered * lax.rsqrt(variance + 1e-05) * gain).astype(BF16)


def pick_columns(rows, side, quarter):
    group = lax.axis_index("groups")
    parts = []
    for kind in range(3):
        low = 4 * kind * quarter
        block = [rows[:, low + at * quarter : low + (at + 1) * quarter] for at in range(4)]
        sides = [jnp.where(group == 0, block[2 * at], block[2 * at + 1]) for at in range(2)]
        parts.append(jnp.where(side == 0, sides[0], sides[1]))
    return jnp.concatenate(parts, axis=1)


def pack_body(*refs, weights):
    tokens, bias, gain = refs[:3]
    message, raw, out_own, bias_here, gain_here, rows, sems = refs[-7:]
    count = tokens.shape[0]
    heads, bias_width = bias.shape
    core = lax.axis_index("lon")
    half = rows.shape[0]
    copies = [(gain, gain_here), (bias, bias_here), (tokens, raw)]
    if weights:
        w_qkv, w_out = refs[3:5]
        picked = pl.ds(pl.multiple_of(core * half, half), half)
        copies += [(w_qkv.at[picked, :], rows), (w_out.at[picked, :], out_own)]
    fetches = [
        pltpu.make_async_copy(source, target, sems.at[at])
        for at, (source, target) in enumerate(copies)
    ]
    for fetch in fetches:
        fetch.start()
    message[count:, :] = jnp.zeros((message.shape[0] - count, tokens.shape[1]), BF16)
    for fetch in fetches[:3]:
        fetch.wait()
    message[count : count + heads, :bias_width] = bias_here[...]
    message[:count, :] = norm_rows(raw[...].astype(F32), gain_here[...][None])
    for fetch in fetches[3:]:
        fetch.wait()
    if weights:
        side = lax.rem(lax.axis_index("lat"), 2)
        cross = pick_columns(rows, 1 - side, tokens.shape[1] // 4)
        message[count + 16 :, : cross.shape[1]] = cross


def columns_body(w_qkv, w_out, own, out_own):
    half = own.shape[0]
    start = pl.multiple_of(lax.axis_index("lon") * half, half)
    rows = w_qkv[pl.ds(start, half), :]
    own[...] = pick_columns(rows, lax.rem(lax.axis_index("lat"), 2), own.shape[1] // 3)
    out_own[...] = w_out[pl.ds(start, half), :]


def arrived_body(
    own, by_x, by_y, out_own, out1, out2, out3, bundle, x_block, outs
):
    del by_y
    side = lax.rem(lax.axis_index("lat"), 2)
    rows, width = x_block.shape[0], own.shape[1]
    bundle[side] = own[...]
    bundle[1 - side] = by_x[rows:, :width]
    x_block[...] = by_x[:rows, :]
    for at, block in enumerate((out_own, out1, out2, out3)):
        outs[at] = block[...]


def complete_body(
    bundle, level1, level2, level3, message, x_block, by_y, by_xy, outs, crossed, gains, *results
):
    del gains
    weights, near, both = results
    rows = x_block.shape[0]
    for at, block in enumerate((bundle, level1, level2, level3)):
        weights[at] = block[...]
    for at, block in enumerate((message, x_block, by_y, by_xy)):
        near[at] = block[:rows, :]
    both[0] = outs[...]
    both[1] = crossed[...]


def pair_away(flip):
    pair = lax.rem(lax.axis_index("lat") // 2, 4)
    high, low = pair // 2, pair % 2
    high = 1 - high if flip // 2 else high
    low = 1 - low if flip % 2 else low
    return 2 * high + low


def join_bundles(mine, other, joined):
    core = lax.axis_index("lon")
    half = mine.shape[2]
    for flip in range(4):
        for block, at in ((mine, core), (other, 1 - core)):
            for row in range(2):
                first = pl.multiple_of(((pair_away(flip) * 2 + row) * 2 + at) * half, half)
                joined[pl.ds(first, half), :] = block[flip, row]


def join_columns(mine, other, joined):
    core, side = lax.axis_index("lon"), lax.rem(lax.axis_index("lat"), 2)
    half = mine.shape[2]
    for flip in range(4):
        for block, at in ((mine, core), (other, 1 - core)):
            for cross, row in enumerate((side, 1 - side)):
                first = pl.multiple_of(((pair_away(flip) * 2 + row) * 2 + at) * half, half)
                joined[pl.ds(first, half), :] = block[cross, flip]


def attend_body(*refs):
    (near, far, mine, other), pieces = refs[:4], refs[4:8]
    weights, bias_rows, near_rows, far_rows = refs[8:]
    group, side = lax.axis_index("groups"), lax.rem(lax.axis_index("lat"), 2)
    _, count, quarter = pieces[0].shape
    heads = 3
    head_dim = quarter // heads
    join_bundles(mine, other, weights)
    for slot in range(4):
        near_rows[slot * count : (slot + 1) * count, :] = near[slot, :count, :]
        far_rows[slot * count : (slot + 1) * count, :] = far[slot, :count, :]
    for flip in range(2):
        for at, block in enumerate((near, far)):
            bias_rows[flip, :, at * count : (at + 1) * count] = block[flip, count:, :count].astype(
                F32
            )
    first_head = (2 * side + group) * heads
    here = jnp.dot(near_rows[...], weights[...], preferred_element_type=F32).astype(BF16)
    there = jnp.dot(far_rows[...], weights[:, quarter:], preferred_element_type=F32).astype(BF16)
    for slot in range(4):
        flip, sample = slot % 2, slot // 2
        low_row, high_row = slot * count, (slot + 1) * count
        outs = []
        for head in range(heads):
            low = head * head_dim
            queries = here[low_row:high_row, low : low + head_dim]
            keys, values = (
                jnp.concatenate(
                    [
                        here[low_row:high_row, (kind + 1) * quarter + low :][:, :head_dim],
                        there[low_row:high_row, kind * quarter + low :][:, :head_dim],
                    ]
                )
                for kind in range(2)
            )
            scores = lax.dot_general(
                queries, keys, (((1,), (1,)), ((), ())), preferred_element_type=F32
            ) * (head_dim**-0.5)
            scores = scores + bias_rows[flip, pl.ds(first_head + head, 1), :]
            expd = jnp.exp(scores - jnp.max(scores, axis=-1, keepdims=True))
            totals = jnp.sum(expd, axis=-1, keepdims=True)
            weighted = jnp.dot(expd.astype(BF16), values, preferred_element_type=F32)
            outs.append((weighted / totals).astype(BF16))
        attended = jnp.concatenate(outs, axis=1)
        pieces[2 * sample + flip][0] = attended
        pieces[2 * sample + 1 - flip][1] = attended


def project_out(which, pieces, weights, tokens, gain):
    group, side = lax.axis_index("groups"), lax.rem(lax.axis_index("lat"), 2)
    summed = tokens.astype(F32)
    for slot, piece in enumerate(pieces):
        flip, sample = slot % 2, slot // 2
        quarter = piece.shape[2]
        owner = 2 * (side + flip - 2 * side * flip) + (group + sample - 2 * group * sample)
        rows = pl.ds(pl.multiple_of(owner * quarter, quarter), quarter)
        summed = summed + jnp.dot(piece[which], weights[rows, :], preferred_element_type=F32)
    middle = summed.astype(BF16)
    return middle, norm_rows(middle.astype(F32), gain)


def other_body(gain, piece0, piece1, piece2, piece3, weights, tokens, other_in):
    pieces = (piece0, piece1, piece2, piece3)
    other_in[...] = project_out(1, pieces, weights, tokens[...], gain[...])[1]


def tent_pair(row_count, first_col, col_count, half_width):
    rows = lax.broadcasted_iota(jnp.int32, (row_count, col_count), 0)
    cols = lax.broadcasted_iota(jnp.int32, (row_count, col_count), 1) + first_col
    offset = ((cols - rows + row_count // 2) & (row_count - 1)) - row_count // 2
    distance = jnp.abs(offset).astype(F32)
    span_plus = (half_width + 1).astype(F32)
    tent = jnp.where(
        distance <= half_width.astype(F32), (1.0 - distance / span_plus) / span_plus, 0.0
    )
    odd = tent * offset.astype(F32) / span_plus
    return tent.astype(BF16), odd.astype(BF16)


def mix(lines, blocks, basis):
    size = blocks.shape[2]
    return jnp.concatenate(
        [
            jnp.dot(
                lines[:, tile * size : (tile + 1) * size],
                blocks[basis, tile],
                preferred_element_type=F32,
            ).astype(BF16)
            for tile in range(blocks.shape[1])
        ],
        axis=1,
    )


def plan_body(
    lat_count, lon_half, lat_half, quad_off, taps, w_conv, message, blocks, coeffs, gains
):
    del message
    lat_row, core = lax.axis_index("lat"), lax.axis_index("lon")
    side = lax.rem(lat_row, 2)
    for basis in range(2):
        below, centre, above = (taps[quad_off[0] + row, basis] for row in range(3))
        below = jnp.where(lat_half[0] >= 1, below, 0.0)
        above = jnp.where(lat_half[0] >= 1, above, 0.0)
        other = jnp.where(side == 0, above, below)
        halo = jnp.where(side == 0, below, above)
        pole = jnp.where(lat_row == 0, below, 0.0) + jnp.where(
            lat_row == lat_count - 1, above, 0.0
        )
        for at, value in enumerate((other, centre, halo, pole)):
            gains[4 * basis + at : 4 * basis + at + 1, :] = jnp.full((1, 128), value, F32)
    rows, count = coeffs.shape[0], coeffs.shape[1] // 4
    direct = tent_pair(rows, core * count, count, lon_half[0])
    rolled = tent_pair(rows, core * count + count, count, lon_half[0])
    for at, part in enumerate((direct[0], direct[1], rolled[0], rolled[1])):
        coeffs[:, at * count : (at + 1) * count] = part
    size = w_conv.shape[2]
    blocks[...] = jnp.zeros(blocks.shape, BF16)
    per_block = blocks.shape[2] // size
    for basis in range(blocks.shape[0]):
        for tile in range(blocks.shape[1]):
            for at in range(per_block):
                first = (tile * per_block + at) * size
                low, high = at * size, (at + 1) * size
                blocks[basis, tile, low:high, low:high] = w_conv[basis, first : first + size, :]


def own_body(
    gains,
    gain,
    piece0,
    piece1,
    piece2,
    piece3,
    weights,
    tokens,
    other_in,
    blocks,
    coeffs,
    middle,
    partial,
):
    count = tokens.shape[0]
    pieces = (piece0, piece1, piece2, piece3)
    own_middle, own_in = project_out(0, pieces, weights, tokens[...], gain[...])
    middle[...] = own_middle
    own = own_in.astype(F32)
    neighbour = other_in[...].astype(F32)
    direct, rolled = [], []
    for basis in range(2):
        other, centre, _, pole = (gains[4 * basis + at : 4 * basis + at + 1, :1] for at in range(4))
        lines = jnp.concatenate(
            [(other * neighbour + centre * own).astype(BF16), (pole * own).astype(BF16)]
        )
        mixed = mix(lines, blocks, basis)
        direct.append(mixed[:count])
        rolled.append(mixed[count:])
    partial[...] = jnp.dot(
        coeffs[...], jnp.concatenate(direct + rolled), preferred_element_type=F32
    )


def halo_body(gains, halo, blocks, coeffs, middle, partial, kept, sent, total):
    core = lax.axis_index("lon")
    count = halo.shape[0]
    values = halo[...].astype(F32)
    mixed = [
        mix((gains[4 * basis + 2 : 4 * basis + 3, :1] * values).astype(BF16), blocks, basis)
        for basis in range(2)
    ]
    total[...] = partial[...] + jnp.dot(
        coeffs[:, : 2 * count], jnp.concatenate(mixed), preferred_element_type=F32
    )
    here = pl.multiple_of(core * count, count)
    there = pl.multiple_of((1 - core) * count, count)
    kept[...] = middle[...].astype(F32) + total[pl.ds(here, count), :]
    sent[...] = total[pl.ds(there, count), :].astype(BF16)


def pack_plain(weights, columns):
    core, lat_count = lax.axis_index("lon"), lax.axis_size("lat")
    half, width = weights.shape[0] // 2, weights.shape[1]
    rows = lax.dynamic_slice_in_dim(weights, core * half, half, 0)
    if columns == width:
        return jnp.broadcast_to(rows[None], (lat_count, half, columns))
    rows = rows.reshape(half, 3, 2, 2, columns // 3)
    rows = lax.dynamic_index_in_dim(rows, lax.axis_index("groups"), 3, keepdims=False)
    rows = rows.transpose(2, 0, 1, 3).reshape(2, half, columns)
    rows = jnp.broadcast_to(rows[None], (lat_count // 2, 2, half, columns))
    return rows.reshape(lat_count, half, columns)


def gather_plain(weights, columns):
    core = lax.axis_index("lon")
    mine = lax.all_to_all(pack_plain(weights, columns), "lat", 0, 0)
    other = swap_cores(mine)
    both = jnp.where(core == 0, jnp.stack([mine, other], 1), jnp.stack([other, mine], 1))
    whole = both.reshape(4, 2, 2, -1, columns)
    pair = lax.rem(lax.axis_index("lat") // 2, 4)
    whole = jnp.stack(
        [lax.dynamic_index_in_dim(whole, pair ^ flip, 0, keepdims=False) for flip in range(4)]
    )
    return [
        lax.dynamic_index_in_dim(whole, at, 2, keepdims=False) for at in (core, 1 - core)
    ]


def flip_levels(bundle):
    return [move(bundle, lambda g, l, c: (g, l ^ (2 * flip), c)) for flip in (1, 2, 3)]


def per_device(
    tokens,
    gain_attn,
    w_qkv,
    key_bias,
    w_out,
    gain_conv,
    w_conv,
    lat_taps,
    lon_half,
    lat_half,
    quad_off,
):
    own_tokens = tokens[0]
    count, width = own_tokens.shape
    quarter = width // 4
    lat_count = lax.axis_size("lat")
    half = w_qkv.shape[0] // 2
    gain_conv = gain_conv[None]

    direct = half % 16 == 0 and lat_count == 8
    rows = count + 16
    message, raw_tokens, out_own = call(
        functools.partial(pack_body, weights=direct),
        [
            ((rows + (half if direct else 0), width), BF16),
            ((count, width), BF16),
            ((half, width), BF16),
        ],
        [HBM] * (5 if direct else 3),
        (own_tokens, key_bias[0], gain_attn) + ((w_qkv, w_out) if direct else ()),
        10 * count * width,
        [
            pltpu.VMEM(key_bias.shape[1:], BF16),
            pltpu.VMEM((width,), F32),
            pltpu.VMEM((half, 3 * width), BF16),
            pltpu.SemaphoreType.DMA((5,)),
        ],
        limit=56,
    )

    by_x, by_y = flip_chips(message, 1, 0), flip_chips(message, 0, 1)
    x_block = by_x
    if direct:
        levels = flip_levels(out_own)
        qkv_own, out_own = call(
            columns_body,
            [((half, 3 * quarter), BF16), ((half, width), BF16)],
            [VMEM] * 2,
            (w_qkv, w_out),
            0,
        )
        bundle, x_block, outs = call(
            arrived_body,
            [
                ((2, half, 3 * quarter), BF16),
                ((rows, width), BF16),
                ((4, half, width), BF16),
            ],
            [VMEM] * 7,
            (qkv_own, by_x, by_y, out_own, *levels),
            0,
        )
    size = 4 * w_conv.shape[2]
    diagonal, coeffs, gains = call(
        functools.partial(plan_body, lat_count),
        [
            ((2, width // size, size, size), BF16),
            ((2 * count, 4 * count), BF16),
            ((8, 128), F32),
        ],
        [SMEM] * 4 + [VMEM, ANY],
        (lon_half, lat_half, quad_off, lat_taps, w_conv, x_block),
        0,
    )
    if direct:
        qkv_mine, near, out_mine = call(
            complete_body,
            [
                ((4, 2, half, 3 * quarter), BF16),
                ((4, rows, width), BF16),
                ((2, 4, half, width), BF16),
            ],
            [VMEM] * 11,
            (
                bundle,
                *flip_levels(bundle),
                message,
                x_block,
                by_y,
                flip_chips(x_block, 0, 1),
                outs,
                flip_chips(outs, 1, 0),
                gains,
            ),
            0,
        )
        qkv_other, out_other = swap_cores(qkv_mine), swap_cores(out_mine)
        join = join_columns
    else:
        near = jnp.stack([message, by_x, by_y, flip_chips(by_x, 0, 1)])
        qkv_mine, qkv_other = gather_plain(w_qkv, 3 * quarter)
        out_mine, out_other = gather_plain(w_out, width)
        join = join_bundles
    far = swap_cores(near)
    raw_tokens = gate(raw_tokens, qkv_mine)
    other_tokens = flip_chips(raw_tokens, 1, 0)

    pieces = call(
        attend_body,
        [((2, count, quarter), BF16)] * 4,
        [VMEM] * 4,
        (near, far, qkv_mine, qkv_other),
        2 * 1024 * width * 3 * quarter,
        [
            pltpu.VMEM((width, 3 * quarter), BF16),
            pltpu.VMEM((2, 16, 2 * count), F32),
            pltpu.VMEM((4 * count, width), BF16),
            pltpu.VMEM((4 * count, width), BF16),
        ],
    )
    back = [pieces[0]] + [
        flip_chips(piece, flip, sample) for piece, (flip, sample) in zip(pieces[1:], FLIPS)
    ]
    (full_out,) = call(
        join, [((width, width), BF16)], [VMEM] * 2, (out_mine, out_other), 0
    )
    (other_in,) = call(
        other_body,
        [((count, width), BF16)],
        [VMEM] * 7,
        (gain_conv, *back, full_out, other_tokens),
        2 * count * width * width,
    )
    halo = move(other_in, lambda g, l, c: (g, l + 2 - 4 * (l % 2), c))
    middle, partial = call(
        own_body,
        [((count, width), BF16), ((2 * count, width), F32)],
        [VMEM] * 11,
        (gains, gain_conv, *back, full_out, raw_tokens, other_in, diagonal, coeffs),
        2 * count * width * width * 3,
    )
    kept, sent = call(
        halo_body,
        [((count, width), F32), ((count, width), BF16)],
        [VMEM] * 6,
        (gains, halo, diagonal, coeffs, middle, partial),
        2 * 256 * 256 * width,
        [pltpu.VMEM((2 * count, width), F32)],
    )
    received = swap_cores(sent)
    return (kept + received.astype(F32)).astype(BF16)[None]


def solution(mesh):
    return jax.shard_map(
        per_device,
        mesh=mesh,
        in_specs=(
            P(("groups", "lat"), "lon", None),
            P(),
            P("lat", None),
            P("lat", None, "lon"),
            P("lat", None),
            P(),
            P(),
            P(),
            P("lat"),
            P("lat"),
            P("lat"),
        ),
        out_specs=P(("groups", "lat"), "lon", None),
        check_vma=False,
    )
```

```python
import functools

import jax
import jax.numpy as jnp
from jax import lax
from jax.experimental import pallas as pl
from jax.experimental.pallas import tpu as pltpu
from jax.sharding import PartitionSpec as P

AXES = ("groups", "lat", "lon")
VMEM = pl.BlockSpec(memory_space=pltpu.VMEM)
ANY = pl.BlockSpec(memory_space=pl.ANY)
HBM = pl.BlockSpec(memory_space=pltpu.HBM)
FLIPS = ((1, 0), (0, 1), (1, 1))
SMEM = pl.BlockSpec(memory_space=pltpu.SMEM)
BF16 = jnp.bfloat16
F32 = jnp.float32


def call(body, outs, specs, args, flops, scratch=(), limit=32):
    outs = tuple(jax.ShapeDtypeStruct(shape, dtype) for shape, dtype in outs)
    moved = sum(a.size * a.dtype.itemsize for a in args)
    return pl.pallas_call(
        body,
        out_shape=outs,
        in_specs=specs,
        out_specs=tuple(VMEM for _ in outs),
        scratch_shapes=list(scratch),
        compiler_params=pltpu.CompilerParams(vmem_limit_bytes=limit * 1024 * 1024),
        cost_estimate=pl.CostEstimate(flops=flops, bytes_accessed=moved, transcendentals=0),
    )(*args)


def copy_body(*refs):
    refs[-1][...] = refs[0][...]


def gate(value, *after):
    specs = [VMEM] * (1 + len(after))
    return call(copy_body, [(value.shape, value.dtype)], specs, (value, *after), 0)[0]


def device_pairs(target):
    lat_count = lax.axis_size("lat")
    pairs = []
    for group in range(2):
        for row in range(lat_count):
            for core in range(2):
                to = target(group, row, core)
                if 0 <= to[1] < lat_count:
                    source = (group * lat_count + row) * 2 + core
                    pairs.append((source, (to[0] * lat_count + to[1]) * 2 + to[2]))
    return pairs


def move(values, target):
    return lax.ppermute(values, AXES, device_pairs(target))


def swap_cores(values):
    return lax.ppermute(values, "lon", [(0, 1), (1, 0)])


def flip_chips(values, flip, sample):
    return move(values, lambda g, l, c: (g ^ sample, l ^ flip, c))


def norm_rows(values, gain):
    average = jnp.mean(values, axis=-1, keepdims=True)
    centered = values - average
    variance = jnp.mean(centered * centered, axis=-1, keepdims=True)
    return (centered * lax.rsqrt(variance + 1e-05) * gain).astype(BF16)


def pick_columns(rows, side, quarter):
    group = lax.axis_index("groups")
    parts = []
    for kind in range(3):
        low = 4 * kind * quarter
        block = [rows[:, low + at * quarter : low + (at + 1) * quarter] for at in range(4)]
        sides = [jnp.where(group == 0, block[2 * at], block[2 * at + 1]) for at in range(2)]
        parts.append(jnp.where(side == 0, sides[0], sides[1]))
    return jnp.concatenate(parts, axis=1)


def pack_body(*refs, weights):
    tokens, bias, gain = refs[:3]
    message, raw, out_own, bias_here, gain_here, rows, sems = refs[-7:]
    count = tokens.shape[0]
    heads, bias_width = bias.shape
    core = lax.axis_index("lon")
    half = rows.shape[0]
    copies = [(gain, gain_here), (bias, bias_here), (tokens, raw)]
    if weights:
        w_qkv, w_out = refs[3:5]
        picked = pl.ds(pl.multiple_of(core * half, half), half)
        copies += [(w_qkv.at[picked, :], rows), (w_out.at[picked, :], out_own)]
    fetches = [
        pltpu.make_async_copy(source, target, sems.at[at])
        for at, (source, target) in enumerate(copies)
    ]
    for fetch in fetches:
        fetch.start()
    message[count:, :] = jnp.zeros((message.shape[0] - count, tokens.shape[1]), BF16)
    for fetch in fetches[:3]:
        fetch.wait()
    message[count : count + heads, :bias_width] = bias_here[...]
    message[:count, :] = norm_rows(raw[...].astype(F32), gain_here[...][None])
    for fetch in fetches[3:]:
        fetch.wait()
    if weights:
        side = lax.rem(lax.axis_index("lat"), 2)
        cross = pick_columns(rows, 1 - side, tokens.shape[1] // 4)
        message[count + 16 :, : cross.shape[1]] = cross


def columns_body(w_qkv, w_out, own, out_own):
    half = own.shape[0]
    start = pl.multiple_of(lax.axis_index("lon") * half, half)
    rows = w_qkv[pl.ds(start, half), :]
    own[...] = pick_columns(rows, lax.rem(lax.axis_index("lat"), 2), own.shape[1] // 3)
    out_own[...] = w_out[pl.ds(start, half), :]


def arrived_body(
    own, by_x, by_y, out_own, out1, out2, out3, bundle, x_block, outs
):
    del by_y
    side = lax.rem(lax.axis_index("lat"), 2)
    rows, width = x_block.shape[0], own.shape[1]
    bundle[side] = own[...]
    bundle[1 - side] = by_x[rows:, :width]
    x_block[...] = by_x[:rows, :]
    for at, block in enumerate((out_own, out1, out2, out3)):
        outs[at] = block[...]


def complete_body(
    bundle, level1, level2, level3, message, x_block, by_y, by_xy, outs, crossed, gains, *results
):
    del gains
    weights, near, both = results
    rows = x_block.shape[0]
    for at, block in enumerate((bundle, level1, level2, level3)):
        weights[at] = block[...]
    for at, block in enumerate((message, x_block, by_y, by_xy)):
        near[at] = block[:rows, :]
    both[0] = outs[...]
    both[1] = crossed[...]


def pair_away(flip):
    pair = lax.rem(lax.axis_index("lat") // 2, 4)
    high, low = pair // 2, pair % 2
    high = 1 - high if flip // 2 else high
    low = 1 - low if flip % 2 else low
    return 2 * high + low


def join_bundles(mine, other, joined):
    core = lax.axis_index("lon")
    half = mine.shape[2]
    for flip in range(4):
        for block, at in ((mine, core), (other, 1 - core)):
            for row in range(2):
                first = pl.multiple_of(((pair_away(flip) * 2 + row) * 2 + at) * half, half)
                joined[pl.ds(first, half), :] = block[flip, row]


def join_columns(mine, other, joined):
    core, side = lax.axis_index("lon"), lax.rem(lax.axis_index("lat"), 2)
    half = mine.shape[2]
    for flip in range(4):
        for block, at in ((mine, core), (other, 1 - core)):
            for cross, row in enumerate((side, 1 - side)):
                first = pl.multiple_of(((pair_away(flip) * 2 + row) * 2 + at) * half, half)
                joined[pl.ds(first, half), :] = block[cross, flip]


def attend_body(join, sample, near, far, mine, other, *rest):
    piece0, piece1, *scratch = rest[-6:]
    weights, bias_rows, near_rows, far_rows = scratch
    pieces = (piece0, piece1)
    group, side = lax.axis_index("groups"), lax.rem(lax.axis_index("lat"), 2)
    _, count, quarter = piece0.shape
    heads = 3
    head_dim = quarter // heads
    join(mine, other, weights)
    for flip in range(2):
        rows = slice(flip * count, (flip + 1) * count)
        near_rows[rows, :] = near[2 * sample + flip, :count, :]
        far_rows[rows, :] = far[2 * sample + flip, :count, :]
        for at, block in enumerate((near, far)):
            bias_rows[flip, :, at * count : (at + 1) * count] = block[flip, count:, :count].astype(
                F32
            )
    first_head = (2 * side + group) * heads
    here = jnp.dot(near_rows[...], weights[...], preferred_element_type=F32).astype(BF16)
    there = jnp.dot(far_rows[...], weights[:, quarter:], preferred_element_type=F32).astype(BF16)
    for flip in range(2):
        low_row, high_row = flip * count, (flip + 1) * count
        outs = []
        for head in range(heads):
            low = head * head_dim
            queries = here[low_row:high_row, low : low + head_dim]
            keys, values = (
                jnp.concatenate(
                    [
                        here[low_row:high_row, (kind + 1) * quarter + low :][:, :head_dim],
                        there[low_row:high_row, kind * quarter + low :][:, :head_dim],
                    ]
                )
                for kind in range(2)
            )
            scores = lax.dot_general(
                queries, keys, (((1,), (1,)), ((), ())), preferred_element_type=F32
            ) * (head_dim**-0.5)
            scores = scores + bias_rows[flip, pl.ds(first_head + head, 1), :]
            expd = jnp.exp(scores - jnp.max(scores, axis=-1, keepdims=True))
            totals = jnp.sum(expd, axis=-1, keepdims=True)
            weighted = jnp.dot(expd.astype(BF16), values, preferred_element_type=F32)
            outs.append((weighted / totals).astype(BF16))
        attended = jnp.concatenate(outs, axis=1)
        pieces[flip][0] = attended
        pieces[1 - flip][1] = attended


def project_out(which, pieces, weights, tokens, gain):
    group, side = lax.axis_index("groups"), lax.rem(lax.axis_index("lat"), 2)
    summed = tokens.astype(F32)
    for slot, piece in enumerate(pieces):
        flip, sample = slot % 2, slot // 2
        quarter = piece.shape[2]
        owner = 2 * (side + flip - 2 * side * flip) + (group + sample - 2 * group * sample)
        rows = pl.ds(pl.multiple_of(owner * quarter, quarter), quarter)
        summed = summed + jnp.dot(piece[which], weights[rows, :], preferred_element_type=F32)
    middle = summed.astype(BF16)
    return middle, norm_rows(middle.astype(F32), gain)


def other_body(gain, piece0, piece1, piece2, piece3, weights, tokens, other_in):
    pieces = (piece0, piece1, piece2, piece3)
    other_in[...] = project_out(1, pieces, weights, tokens[...], gain[...])[1]


def tent_pair(row_count, first_col, col_count, half_width):
    rows = lax.broadcasted_iota(jnp.int32, (row_count, col_count), 0)
    cols = lax.broadcasted_iota(jnp.int32, (row_count, col_count), 1) + first_col
    offset = ((cols - rows + row_count // 2) & (row_count - 1)) - row_count // 2
    distance = jnp.abs(offset).astype(F32)
    span_plus = (half_width + 1).astype(F32)
    tent = jnp.where(
        distance <= half_width.astype(F32), (1.0 - distance / span_plus) / span_plus, 0.0
    )
    odd = tent * offset.astype(F32) / span_plus
    return tent.astype(BF16), odd.astype(BF16)


def mix(lines, blocks, basis):
    size = blocks.shape[2]
    return jnp.concatenate(
        [
            jnp.dot(
                lines[:, tile * size : (tile + 1) * size],
                blocks[basis, tile],
                preferred_element_type=F32,
            ).astype(BF16)
            for tile in range(blocks.shape[1])
        ],
        axis=1,
    )


def plan_body(
    lat_count, lon_half, lat_half, quad_off, taps, w_conv, message, blocks, coeffs, gains
):
    del message
    lat_row, core = lax.axis_index("lat"), lax.axis_index("lon")
    side = lax.rem(lat_row, 2)
    for basis in range(2):
        below, centre, above = (taps[quad_off[0] + row, basis] for row in range(3))
        below = jnp.where(lat_half[0] >= 1, below, 0.0)
        above = jnp.where(lat_half[0] >= 1, above, 0.0)
        other = jnp.where(side == 0, above, below)
        halo = jnp.where(side == 0, below, above)
        pole = jnp.where(lat_row == 0, below, 0.0) + jnp.where(
            lat_row == lat_count - 1, above, 0.0
        )
        for at, value in enumerate((other, centre, halo, pole)):
            gains[4 * basis + at : 4 * basis + at + 1, :] = jnp.full((1, 128), value, F32)
    rows, count = coeffs.shape[0], coeffs.shape[1] // 4
    direct = tent_pair(rows, core * count, count, lon_half[0])
    rolled = tent_pair(rows, core * count + count, count, lon_half[0])
    for at, part in enumerate((direct[0], direct[1], rolled[0], rolled[1])):
        coeffs[:, at * count : (at + 1) * count] = part
    size = w_conv.shape[2]
    blocks[...] = jnp.zeros(blocks.shape, BF16)
    per_block = blocks.shape[2] // size
    for basis in range(blocks.shape[0]):
        for tile in range(blocks.shape[1]):
            for at in range(per_block):
                first = (tile * per_block + at) * size
                low, high = at * size, (at + 1) * size
                blocks[basis, tile, low:high, low:high] = w_conv[basis, first : first + size, :]


def own_body(
    gains,
    gain,
    piece0,
    piece1,
    piece2,
    piece3,
    weights,
    tokens,
    other_in,
    blocks,
    coeffs,
    middle,
    partial,
):
    count = tokens.shape[0]
    pieces = (piece0, piece1, piece2, piece3)
    own_middle, own_in = project_out(0, pieces, weights, tokens[...], gain[...])
    middle[...] = own_middle
    own = own_in.astype(F32)
    neighbour = other_in[...].astype(F32)
    direct, rolled = [], []
    for basis in range(2):
        other, centre, _, pole = (gains[4 * basis + at : 4 * basis + at + 1, :1] for at in range(4))
        lines = jnp.concatenate(
            [(other * neighbour + centre * own).astype(BF16), (pole * own).astype(BF16)]
        )
        mixed = mix(lines, blocks, basis)
        direct.append(mixed[:count])
        rolled.append(mixed[count:])
    partial[...] = jnp.dot(
        coeffs[...], jnp.concatenate(direct + rolled), preferred_element_type=F32
    )


def halo_body(gains, halo, blocks, coeffs, middle, partial, kept, sent, total):
    core = lax.axis_index("lon")
    count = halo.shape[0]
    values = halo[...].astype(F32)
    mixed = [
        mix((gains[4 * basis + 2 : 4 * basis + 3, :1] * values).astype(BF16), blocks, basis)
        for basis in range(2)
    ]
    total[...] = partial[...] + jnp.dot(
        coeffs[:, : 2 * count], jnp.concatenate(mixed), preferred_element_type=F32
    )
    here = pl.multiple_of(core * count, count)
    there = pl.multiple_of((1 - core) * count, count)
    kept[...] = middle[...].astype(F32) + total[pl.ds(here, count), :]
    sent[...] = total[pl.ds(there, count), :].astype(BF16)


def pack_plain(weights, columns):
    core, lat_count = lax.axis_index("lon"), lax.axis_size("lat")
    half, width = weights.shape[0] // 2, weights.shape[1]
    rows = lax.dynamic_slice_in_dim(weights, core * half, half, 0)
    if columns == width:
        return jnp.broadcast_to(rows[None], (lat_count, half, columns))
    rows = rows.reshape(half, 3, 2, 2, columns // 3)
    rows = lax.dynamic_index_in_dim(rows, lax.axis_index("groups"), 3, keepdims=False)
    rows = rows.transpose(2, 0, 1, 3).reshape(2, half, columns)
    rows = jnp.broadcast_to(rows[None], (lat_count // 2, 2, half, columns))
    return rows.reshape(lat_count, half, columns)


def gather_plain(weights, columns):
    core = lax.axis_index("lon")
    mine = lax.all_to_all(pack_plain(weights, columns), "lat", 0, 0)
    other = swap_cores(mine)
    both = jnp.where(core == 0, jnp.stack([mine, other], 1), jnp.stack([other, mine], 1))
    whole = both.reshape(4, 2, 2, -1, columns)
    pair = lax.rem(lax.axis_index("lat") // 2, 4)
    whole = jnp.stack(
        [lax.dynamic_index_in_dim(whole, pair ^ flip, 0, keepdims=False) for flip in range(4)]
    )
    return [
        lax.dynamic_index_in_dim(whole, at, 2, keepdims=False) for at in (core, 1 - core)
    ]


def flip_levels(bundle):
    return [move(bundle, lambda g, l, c: (g, l ^ (2 * flip), c)) for flip in (1, 2, 3)]


def per_device(
    tokens,
    gain_attn,
    w_qkv,
    key_bias,
    w_out,
    gain_conv,
    w_conv,
    lat_taps,
    lon_half,
    lat_half,
    quad_off,
):
    own_tokens = tokens[0]
    count, width = own_tokens.shape
    quarter = width // 4
    lat_count = lax.axis_size("lat")
    half = w_qkv.shape[0] // 2
    gain_conv = gain_conv[None]

    direct = half % 16 == 0 and lat_count == 8
    rows = count + 16
    message, raw_tokens, out_own = call(
        functools.partial(pack_body, weights=direct),
        [
            ((rows + (half if direct else 0), width), BF16),
            ((count, width), BF16),
            ((half, width), BF16),
        ],
        [HBM] * (5 if direct else 3),
        (own_tokens, key_bias[0], gain_attn) + ((w_qkv, w_out) if direct else ()),
        10 * count * width,
        [
            pltpu.VMEM(key_bias.shape[1:], BF16),
            pltpu.VMEM((width,), F32),
            pltpu.VMEM((half, 3 * width), BF16),
            pltpu.SemaphoreType.DMA((5,)),
        ],
        limit=56,
    )

    by_x, by_y = flip_chips(message, 1, 0), flip_chips(message, 0, 1)
    x_block = by_x
    if direct:
        levels = flip_levels(out_own)
        qkv_own, out_own = call(
            columns_body,
            [((half, 3 * quarter), BF16), ((half, width), BF16)],
            [VMEM] * 2,
            (w_qkv, w_out),
            0,
        )
        bundle, x_block, outs = call(
            arrived_body,
            [
                ((2, half, 3 * quarter), BF16),
                ((rows, width), BF16),
                ((4, half, width), BF16),
            ],
            [VMEM] * 7,
            (qkv_own, by_x, by_y, out_own, *levels),
            0,
        )
    size = 4 * w_conv.shape[2]
    diagonal, coeffs, gains = call(
        functools.partial(plan_body, lat_count),
        [
            ((2, width // size, size, size), BF16),
            ((2 * count, 4 * count), BF16),
            ((8, 128), F32),
        ],
        [SMEM] * 4 + [VMEM, ANY],
        (lon_half, lat_half, quad_off, lat_taps, w_conv, x_block),
        0,
    )
    if direct:
        qkv_mine, near, out_mine = call(
            complete_body,
            [
                ((4, 2, half, 3 * quarter), BF16),
                ((4, rows, width), BF16),
                ((2, 4, half, width), BF16),
            ],
            [VMEM] * 11,
            (
                bundle,
                *flip_levels(bundle),
                message,
                x_block,
                by_y,
                flip_chips(x_block, 0, 1),
                outs,
                flip_chips(outs, 1, 0),
                gains,
            ),
            0,
        )
        qkv_other, out_other = swap_cores(qkv_mine), swap_cores(out_mine)
        join = join_columns
    else:
        near = jnp.stack([message, by_x, by_y, flip_chips(by_x, 0, 1)])
        qkv_mine, qkv_other = gather_plain(w_qkv, 3 * quarter)
        out_mine, out_other = gather_plain(w_out, width)
        join = join_bundles
    far = swap_cores(near)
    raw_tokens = gate(raw_tokens, qkv_mine)
    other_tokens = flip_chips(raw_tokens, 1, 0)

    pieces = ()
    for sample in (1, 0):
        after = pieces[:1]
        pieces = (
            *call(
                functools.partial(attend_body, join_bundles, sample),
                [((2, count, quarter), BF16)] * 2,
                [VMEM] * (4 + len(after)),
                (near, far, qkv_mine, qkv_other, *after),
                512 * width * 3 * quarter,
                [
                    pltpu.VMEM((width, 3 * quarter), BF16),
                    pltpu.VMEM((2, 16, 2 * count), F32),
                    pltpu.VMEM((2 * count, width), BF16),
                    pltpu.VMEM((2 * count, width), BF16),
                ],
            ),
            *pieces,
        )
    back = [pieces[0]] + [
        flip_chips(piece, flip, sample) for piece, (flip, sample) in zip(pieces[1:], FLIPS)
    ]
    (full_out,) = call(
        join, [((width, width), BF16)], [VMEM] * 2, (out_mine, out_other), 0
    )
    (other_in,) = call(
        other_body,
        [((count, width), BF16)],
        [VMEM] * 7,
        (gain_conv, *back, full_out, other_tokens),
        2 * count * width * width,
    )
    halo = move(other_in, lambda g, l, c: (g, l + 2 - 4 * (l % 2), c))
    middle, partial = call(
        own_body,
        [((count, width), BF16), ((2 * count, width), F32)],
        [VMEM] * 11,
        (gains, gain_conv, *back, full_out, raw_tokens, other_in, diagonal, coeffs),
        2 * count * width * width * 3,
    )
    kept, sent = call(
        halo_body,
        [((count, width), F32), ((count, width), BF16)],
        [VMEM] * 6,
        (gains, halo, diagonal, coeffs, middle, partial),
        2 * 256 * 256 * width,
        [pltpu.VMEM((2 * count, width), F32)],
    )
    received = swap_cores(sent)
    return (kept + received.astype(F32)).astype(BF16)[None]


def solution(mesh):
    return jax.shard_map(
        per_device,
        mesh=mesh,
        in_specs=(
            P(("groups", "lat"), "lon", None),
            P(),
            P("lat", None),
            P("lat", None, "lon"),
            P("lat", None),
            P(),
            P(),
            P(),
            P("lat"),
            P("lat"),
            P("lat"),
        ),
        out_specs=P(("groups", "lat"), "lon", None),
        check_vma=False,
    )
```

```python
import functools

import jax
import jax.numpy as jnp
from jax import lax
from jax.experimental import pallas as pl
from jax.experimental.pallas import tpu as pltpu
from jax.sharding import PartitionSpec as P

AXES = ("groups", "lat", "lon")
VMEM = pl.BlockSpec(memory_space=pltpu.VMEM)
ANY = pl.BlockSpec(memory_space=pl.ANY)
HBM = pl.BlockSpec(memory_space=pltpu.HBM)
FLIPS = ((1, 0), (0, 1), (1, 1))
SMEM = pl.BlockSpec(memory_space=pltpu.SMEM)
BF16 = jnp.bfloat16
F32 = jnp.float32


def call(body, outs, specs, args, flops, scratch=(), limit=32):
    outs = tuple(jax.ShapeDtypeStruct(shape, dtype) for shape, dtype in outs)
    moved = sum(a.size * a.dtype.itemsize for a in args)
    return pl.pallas_call(
        body,
        out_shape=outs,
        in_specs=specs,
        out_specs=tuple(VMEM for _ in outs),
        scratch_shapes=list(scratch),
        compiler_params=pltpu.CompilerParams(vmem_limit_bytes=limit * 1024 * 1024),
        cost_estimate=pl.CostEstimate(flops=flops, bytes_accessed=moved, transcendentals=0),
    )(*args)


def device_pairs(target):
    lat_count = lax.axis_size("lat")
    pairs = []
    for group in range(2):
        for row in range(lat_count):
            for core in range(2):
                to = target(group, row, core)
                if 0 <= to[1] < lat_count:
                    source = (group * lat_count + row) * 2 + core
                    pairs.append((source, (to[0] * lat_count + to[1]) * 2 + to[2]))
    return pairs


def move(values, target):
    return lax.ppermute(values, AXES, device_pairs(target))


def swap_cores(values):
    return lax.ppermute(values, "lon", [(0, 1), (1, 0)])


def flip_chips(values, flip, sample):
    return move(values, lambda g, l, c: (g ^ sample, l ^ flip, c))


def norm_rows(values, gain):
    average = jnp.mean(values, axis=-1, keepdims=True)
    centered = values - average
    variance = jnp.mean(centered * centered, axis=-1, keepdims=True)
    return (centered * lax.rsqrt(variance + 1e-05) * gain).astype(BF16)


def pick_columns(rows, side, quarter):
    group = lax.axis_index("groups")
    parts = []
    for kind in range(3):
        low = 4 * kind * quarter
        block = [rows[:, low + at * quarter : low + (at + 1) * quarter] for at in range(4)]
        sides = [jnp.where(group == 0, block[2 * at], block[2 * at + 1]) for at in range(2)]
        parts.append(jnp.where(side == 0, sides[0], sides[1]))
    return jnp.concatenate(parts, axis=1)


def pack_body(*refs, weights):
    tokens, bias, gain = refs[:3]
    message, wide, raw, out_own, bias_here, gain_here, rows, sems = refs[-8:]
    count = tokens.shape[0]
    heads, bias_width = bias.shape
    core = lax.axis_index("lon")
    half = rows.shape[0]
    copies = [(gain, gain_here), (bias, bias_here), (tokens, raw)]
    if weights:
        w_qkv, w_out = refs[3:5]
        picked = pl.ds(pl.multiple_of(core * half, half), half)
        copies += [(w_qkv.at[picked, :], rows), (w_out.at[picked, :], out_own)]
    fetches = [
        pltpu.make_async_copy(source, target, sems.at[at])
        for at, (source, target) in enumerate(copies)
    ]
    for fetch in fetches:
        fetch.start()
    message[count:, :] = jnp.zeros((message.shape[0] - count, tokens.shape[1]), BF16)
    for fetch in fetches[:3]:
        fetch.wait()
    message[count : count + heads, :bias_width] = bias_here[...]
    message[:count, :] = norm_rows(raw[...].astype(F32), gain_here[...][None])
    wide[: count + 16, :] = message[...]
    wide[count + 16 : 2 * count + 16, :] = raw[...]
    for fetch in fetches[3:]:
        fetch.wait()
    if weights:
        side = lax.rem(lax.axis_index("lat"), 2)
        cross = pick_columns(rows, 1 - side, tokens.shape[1] // 4)
        wide[2 * count + 16 :, : cross.shape[1]] = cross
        wide[2 * count + 16 :, cross.shape[1] :] = jnp.zeros(
            (rows.shape[0], tokens.shape[1] - cross.shape[1]), BF16
        )


def columns_body(w_qkv, w_out, own, out_own):
    half = own.shape[0]
    start = pl.multiple_of(lax.axis_index("lon") * half, half)
    rows = w_qkv[pl.ds(start, half), :]
    own[...] = pick_columns(rows, lax.rem(lax.axis_index("lat"), 2), own.shape[1] // 3)
    out_own[...] = w_out[pl.ds(start, half), :]


def arrived_body(
    own, by_x, by_y, out_own, out1, out2, out3, bundle, x_block, raw_x, outs
):
    del by_y
    side = lax.rem(lax.axis_index("lat"), 2)
    rows, width = x_block.shape[0], own.shape[1]
    bundle[side] = own[...]
    count = raw_x.shape[0]
    bundle[1 - side] = by_x[rows + count :, :width]
    raw_x[...] = by_x[rows : rows + count, :]
    x_block[...] = by_x[:rows, :]
    for at, block in enumerate((out_own, out1, out2, out3)):
        outs[at] = block[...]


def complete_body(
    bundle, level1, level2, level3, message, x_block, by_y, by_xy, crossed, gains, *results
):
    del crossed, gains
    weights, near = results
    rows = x_block.shape[0]
    for at, block in enumerate((bundle, level1, level2, level3)):
        weights[at] = block[...]
    for at, block in enumerate((message, x_block, by_y, by_xy)):
        near[at] = block[:rows, :]


def pair_body(mine, crossed, after, both):
    del after
    both[0] = mine[...]
    both[1] = crossed[...]


def pair_away(flip):
    pair = lax.rem(lax.axis_index("lat") // 2, 4)
    high, low = pair // 2, pair % 2
    high = 1 - high if flip // 2 else high
    low = 1 - low if flip % 2 else low
    return 2 * high + low


def join_bundles(mine, other, joined):
    core = lax.axis_index("lon")
    half = mine.shape[2]
    for flip in range(4):
        for block, at in ((mine, core), (other, 1 - core)):
            for row in range(2):
                first = pl.multiple_of(((pair_away(flip) * 2 + row) * 2 + at) * half, half)
                joined[pl.ds(first, half), :] = block[flip, row]


def join_columns(mine, other, joined):
    core, side = lax.axis_index("lon"), lax.rem(lax.axis_index("lat"), 2)
    half = mine.shape[2]
    for flip in range(4):
        for block, at in ((mine, core), (other, 1 - core)):
            for cross, row in enumerate((side, 1 - side)):
                first = pl.multiple_of(((pair_away(flip) * 2 + row) * 2 + at) * half, half)
                joined[pl.ds(first, half), :] = block[cross, flip]


def attend_body(*refs):
    (near, far, mine, other), pieces = refs[:4], refs[4:8]
    weights, bias_rows, near_rows, far_rows = refs[8:]
    group, side = lax.axis_index("groups"), lax.rem(lax.axis_index("lat"), 2)
    _, count, quarter = pieces[0].shape
    heads = 3
    head_dim = quarter // heads
    join_bundles(mine, other, weights)
    for slot in range(4):
        near_rows[slot * count : (slot + 1) * count, :] = near[slot, :count, :]
        far_rows[slot * count : (slot + 1) * count, :] = far[slot, :count, :]
    for flip in range(2):
        for at, block in enumerate((near, far)):
            bias_rows[flip, :, at * count : (at + 1) * count] = block[flip, count:, :count].astype(
                F32
            )
    first_head = (2 * side + group) * heads
    here = jnp.dot(near_rows[...], weights[...], preferred_element_type=F32).astype(BF16)
    there = jnp.dot(far_rows[...], weights[:, quarter:], preferred_element_type=F32).astype(BF16)
    for slot in range(4):
        flip, sample = slot % 2, slot // 2
        low_row, high_row = slot * count, (slot + 1) * count
        outs = []
        for head in range(heads):
            low = head * head_dim
            queries = here[low_row:high_row, low : low + head_dim]
            keys, values = (
                jnp.concatenate(
                    [
                        here[low_row:high_row, (kind + 1) * quarter + low :][:, :head_dim],
                        there[low_row:high_row, kind * quarter + low :][:, :head_dim],
                    ]
                )
                for kind in range(2)
            )
            scores = lax.dot_general(
                queries, keys, (((1,), (1,)), ((), ())), preferred_element_type=F32
            ) * (head_dim**-0.5)
            scores = scores + bias_rows[flip, pl.ds(first_head + head, 1), :]
            expd = jnp.exp(scores - jnp.max(scores, axis=-1, keepdims=True))
            totals = jnp.sum(expd, axis=-1, keepdims=True)
            weighted = jnp.dot(expd.astype(BF16), values, preferred_element_type=F32)
            outs.append((weighted / totals).astype(BF16))
        attended = jnp.concatenate(outs, axis=1)
        pieces[2 * sample + flip][0] = attended
        pieces[2 * sample + 1 - flip][1] = attended


def project_out(which, pieces, weights, tokens, gain):
    group, side = lax.axis_index("groups"), lax.rem(lax.axis_index("lat"), 2)
    summed = tokens.astype(F32)
    for slot, piece in enumerate(pieces):
        flip, sample = slot % 2, slot // 2
        quarter = piece.shape[2]
        owner = 2 * (side + flip - 2 * side * flip) + (group + sample - 2 * group * sample)
        rows = pl.ds(pl.multiple_of(owner * quarter, quarter), quarter)
        summed = summed + jnp.dot(piece[which], weights[rows, :], preferred_element_type=F32)
    middle = summed.astype(BF16)
    return middle, norm_rows(middle.astype(F32), gain)


def other_body(gain, piece0, piece1, piece2, piece3, weights, tokens, other_in):
    pieces = (piece0, piece1, piece2, piece3)
    other_in[...] = project_out(1, pieces, weights, tokens[...], gain[...])[1]


def tent_pair(row_count, first_col, col_count, half_width):
    rows = lax.broadcasted_iota(jnp.int32, (row_count, col_count), 0)
    cols = lax.broadcasted_iota(jnp.int32, (row_count, col_count), 1) + first_col
    offset = ((cols - rows + row_count // 2) & (row_count - 1)) - row_count // 2
    distance = jnp.abs(offset).astype(F32)
    span_plus = (half_width + 1).astype(F32)
    tent = jnp.where(
        distance <= half_width.astype(F32), (1.0 - distance / span_plus) / span_plus, 0.0
    )
    odd = tent * offset.astype(F32) / span_plus
    return tent.astype(BF16), odd.astype(BF16)


def mix(lines, blocks, basis):
    size = blocks.shape[2]
    return jnp.concatenate(
        [
            jnp.dot(
                lines[:, tile * size : (tile + 1) * size],
                blocks[basis, tile],
                preferred_element_type=F32,
            ).astype(BF16)
            for tile in range(blocks.shape[1])
        ],
        axis=1,
    )


def plan_body(
    lat_count, lon_half, lat_half, quad_off, taps, w_conv, message, blocks, coeffs, gains
):
    del message
    lat_row, core = lax.axis_index("lat"), lax.axis_index("lon")
    side = lax.rem(lat_row, 2)
    for basis in range(2):
        below, centre, above = (taps[quad_off[0] + row, basis] for row in range(3))
        below = jnp.where(lat_half[0] >= 1, below, 0.0)
        above = jnp.where(lat_half[0] >= 1, above, 0.0)
        other = jnp.where(side == 0, above, below)
        halo = jnp.where(side == 0, below, above)
        pole = jnp.where(lat_row == 0, below, 0.0) + jnp.where(
            lat_row == lat_count - 1, above, 0.0
        )
        for at, value in enumerate((other, centre, halo, pole)):
            gains[4 * basis + at : 4 * basis + at + 1, :] = jnp.full((1, 128), value, F32)
    rows, count = coeffs.shape[0], coeffs.shape[1] // 4
    direct = tent_pair(rows, core * count, count, lon_half[0])
    rolled = tent_pair(rows, core * count + count, count, lon_half[0])
    for at, part in enumerate((direct[0], direct[1], rolled[0], rolled[1])):
        coeffs[:, at * count : (at + 1) * count] = part
    size = w_conv.shape[2]
    blocks[...] = jnp.zeros(blocks.shape, BF16)
    per_block = blocks.shape[2] // size
    for basis in range(blocks.shape[0]):
        for tile in range(blocks.shape[1]):
            for at in range(per_block):
                first = (tile * per_block + at) * size
                low, high = at * size, (at + 1) * size
                blocks[basis, tile, low:high, low:high] = w_conv[basis, first : first + size, :]


def own_body(
    gains,
    gain,
    piece0,
    piece1,
    piece2,
    piece3,
    weights,
    tokens,
    other_in,
    blocks,
    coeffs,
    middle,
    partial,
):
    count = tokens.shape[0]
    pieces = (piece0, piece1, piece2, piece3)
    own_middle, own_in = project_out(0, pieces, weights, tokens[...], gain[...])
    middle[...] = own_middle
    own = own_in.astype(F32)
    neighbour = other_in[...].astype(F32)
    direct, rolled = [], []
    for basis in range(2):
        other, centre, _, pole = (gains[4 * basis + at : 4 * basis + at + 1, :1] for at in range(4))
        lines = jnp.concatenate(
            [(other * neighbour + centre * own).astype(BF16), (pole * own).astype(BF16)]
        )
        mixed = mix(lines, blocks, basis)
        direct.append(mixed[:count])
        rolled.append(mixed[count:])
    partial[...] = jnp.dot(
        coeffs[...], jnp.concatenate(direct + rolled), preferred_element_type=F32
    )


def halo_body(gains, halo, blocks, coeffs, middle, partial, kept, sent, total):
    core = lax.axis_index("lon")
    count = halo.shape[0]
    values = halo[...].astype(F32)
    mixed = [
        mix((gains[4 * basis + 2 : 4 * basis + 3, :1] * values).astype(BF16), blocks, basis)
        for basis in range(2)
    ]
    total[...] = partial[...] + jnp.dot(
        coeffs[:, : 2 * count], jnp.concatenate(mixed), preferred_element_type=F32
    )
    here = pl.multiple_of(core * count, count)
    there = pl.multiple_of((1 - core) * count, count)
    kept[...] = middle[...].astype(F32) + total[pl.ds(here, count), :]
    sent[...] = total[pl.ds(there, count), :].astype(BF16)


def pack_plain(weights, columns):
    core, lat_count = lax.axis_index("lon"), lax.axis_size("lat")
    half, width = weights.shape[0] // 2, weights.shape[1]
    rows = lax.dynamic_slice_in_dim(weights, core * half, half, 0)
    if columns == width:
        return jnp.broadcast_to(rows[None], (lat_count, half, columns))
    rows = rows.reshape(half, 3, 2, 2, columns // 3)
    rows = lax.dynamic_index_in_dim(rows, lax.axis_index("groups"), 3, keepdims=False)
    rows = rows.transpose(2, 0, 1, 3).reshape(2, half, columns)
    rows = jnp.broadcast_to(rows[None], (lat_count // 2, 2, half, columns))
    return rows.reshape(lat_count, half, columns)


def gather_plain(weights, columns):
    core = lax.axis_index("lon")
    mine = lax.all_to_all(pack_plain(weights, columns), "lat", 0, 0)
    other = swap_cores(mine)
    both = jnp.where(core == 0, jnp.stack([mine, other], 1), jnp.stack([other, mine], 1))
    whole = both.reshape(4, 2, 2, -1, columns)
    pair = lax.rem(lax.axis_index("lat") // 2, 4)
    whole = jnp.stack(
        [lax.dynamic_index_in_dim(whole, pair ^ flip, 0, keepdims=False) for flip in range(4)]
    )
    return [
        lax.dynamic_index_in_dim(whole, at, 2, keepdims=False) for at in (core, 1 - core)
    ]


def flip_levels(bundle):
    return [move(bundle, lambda g, l, c: (g, l ^ (2 * flip), c)) for flip in (1, 2, 3)]


def per_device(
    tokens,
    gain_attn,
    w_qkv,
    key_bias,
    w_out,
    gain_conv,
    w_conv,
    lat_taps,
    lon_half,
    lat_half,
    quad_off,
):
    own_tokens = tokens[0]
    count, width = own_tokens.shape
    quarter = width // 4
    lat_count = lax.axis_size("lat")
    half = w_qkv.shape[0] // 2
    gain_conv = gain_conv[None]

    direct = half % 16 == 0 and lat_count == 8
    rows = count + 16
    message, wide, raw_tokens, out_own = call(
        functools.partial(pack_body, weights=direct),
        [
            ((rows, width), BF16),
            ((rows + count + (half if direct else 0), width), BF16),
            ((count, width), BF16),
            ((half, width), BF16),
        ],
        [HBM] * (5 if direct else 3),
        (own_tokens, key_bias[0], gain_attn) + ((w_qkv, w_out) if direct else ()),
        10 * count * width,
        [
            pltpu.VMEM(key_bias.shape[1:], BF16),
            pltpu.VMEM((width,), F32),
            pltpu.VMEM((half, 3 * width), BF16),
            pltpu.SemaphoreType.DMA((5,)),
        ],
        limit=56,
    )

    by_x, by_y = flip_chips(wide, 1, 0), flip_chips(message, 0, 1)
    x_block, other_tokens = by_x[:rows], by_x[rows : rows + count]
    if direct:
        levels = flip_levels(out_own)
        qkv_own, out_own = call(
            columns_body,
            [((half, 3 * quarter), BF16), ((half, width), BF16)],
            [VMEM] * 2,
            (w_qkv, w_out),
            0,
        )
        bundle, x_block, other_tokens, outs = call(
            arrived_body,
            [
                ((2, half, 3 * quarter), BF16),
                ((rows, width), BF16),
                ((count, width), BF16),
                ((4, half, width), BF16),
            ],
            [VMEM] * 7,
            (qkv_own, by_x, by_y, out_own, *levels),
            0,
        )
    size = 4 * w_conv.shape[2]
    diagonal, coeffs, gains = call(
        functools.partial(plan_body, lat_count),
        [
            ((2, width // size, size, size), BF16),
            ((2 * count, 4 * count), BF16),
            ((8, 128), F32),
        ],
        [SMEM] * 4 + [VMEM, ANY],
        (lon_half, lat_half, quad_off, lat_taps, w_conv, x_block),
        0,
    )
    if direct:
        crossed = flip_chips(outs, 1, 0)
        qkv_mine, near = call(
            complete_body,
            [
                ((4, 2, half, 3 * quarter), BF16),
                ((4, rows, width), BF16),
            ],
            [VMEM] * 10,
            (
                bundle,
                *flip_levels(bundle),
                message,
                x_block,
                by_y,
                flip_chips(x_block, 0, 1),
                crossed,
                gains,
            ),
            0,
        )
        qkv_other = swap_cores(qkv_mine)
        join = join_columns
    else:
        near = jnp.stack([message, x_block, by_y, flip_chips(x_block, 0, 1)])
        qkv_mine, qkv_other = gather_plain(w_qkv, 3 * quarter)
        out_mine, out_other = gather_plain(w_out, width)
        join = join_bundles
    far = swap_cores(near)

    pieces = call(
        attend_body,
        [((2, count, quarter), BF16)] * 4,
        [VMEM] * 4,
        (near, far, qkv_mine, qkv_other),
        2 * 1024 * width * 3 * quarter,
        [
            pltpu.VMEM((width, 3 * quarter), BF16),
            pltpu.VMEM((2, 16, 2 * count), F32),
            pltpu.VMEM((4 * count, width), BF16),
            pltpu.VMEM((4 * count, width), BF16),
        ],
    )
    back = [pieces[0]] + [
        flip_chips(piece, flip, sample) for piece, (flip, sample) in zip(pieces[1:], FLIPS)
    ]
    if direct:
        (out_mine,) = call(
            pair_body,
            [((2, 4, half, width), BF16)],
            [VMEM] * 3,
            (outs, crossed, pieces[0]),
            0,
        )
        out_other = swap_cores(out_mine)
    (full_out,) = call(
        join, [((width, width), BF16)], [VMEM] * 2, (out_mine, out_other), 0
    )
    (other_in,) = call(
        other_body,
        [((count, width), BF16)],
        [VMEM] * 7,
        (gain_conv, *back, full_out, other_tokens),
        2 * count * width * width,
    )
    halo = move(other_in, lambda g, l, c: (g, l + 2 - 4 * (l % 2), c))
    middle, partial = call(
        own_body,
        [((count, width), BF16), ((2 * count, width), F32)],
        [VMEM] * 11,
        (gains, gain_conv, *back, full_out, raw_tokens, other_in, diagonal, coeffs),
        2 * count * width * width * 3,
    )
    kept, sent = call(
        halo_body,
        [((count, width), F32), ((count, width), BF16)],
        [VMEM] * 6,
        (gains, halo, diagonal, coeffs, middle, partial),
        2 * 256 * 256 * width,
        [pltpu.VMEM((2 * count, width), F32)],
    )
    received = swap_cores(sent)
    return (kept + received.astype(F32)).astype(BF16)[None]


def solution(mesh):
    return jax.shard_map(
        per_device,
        mesh=mesh,
        in_specs=(
            P(("groups", "lat"), "lon", None),
            P(),
            P("lat", None),
            P("lat", None, "lon"),
            P("lat", None),
            P(),
            P(),
            P(),
            P("lat"),
            P("lat"),
            P("lat"),
        ),
        out_specs=P(("groups", "lat"), "lon", None),
        check_vma=False,
    )
```

```python
import functools

import jax
import jax.numpy as jnp
from jax import lax
from jax.experimental import pallas as pl
from jax.experimental.pallas import tpu as pltpu
from jax.sharding import PartitionSpec as P

AXES = ("groups", "lat", "lon")
VMEM = pl.BlockSpec(memory_space=pltpu.VMEM)
ANY = pl.BlockSpec(memory_space=pl.ANY)
HBM = pl.BlockSpec(memory_space=pltpu.HBM)
FLIPS = ((1, 0), (0, 1), (1, 1))
SMEM = pl.BlockSpec(memory_space=pltpu.SMEM)
BF16 = jnp.bfloat16
F32 = jnp.float32


def call(body, outs, specs, args, flops, scratch=(), limit=32):
    outs = tuple(jax.ShapeDtypeStruct(shape, dtype) for shape, dtype in outs)
    moved = sum(a.size * a.dtype.itemsize for a in args)
    return pl.pallas_call(
        body,
        out_shape=outs,
        in_specs=specs,
        out_specs=tuple(VMEM for _ in outs),
        scratch_shapes=list(scratch),
        compiler_params=pltpu.CompilerParams(vmem_limit_bytes=limit * 1024 * 1024),
        cost_estimate=pl.CostEstimate(flops=flops, bytes_accessed=moved, transcendentals=0),
    )(*args)


def copy_body(*refs):
    refs[-1][...] = refs[0][...]


def gate(value, *after):
    specs = [VMEM] * (1 + len(after))
    return call(copy_body, [(value.shape, value.dtype)], specs, (value, *after), 0)[0]


def device_pairs(target):
    lat_count = lax.axis_size("lat")
    pairs = []
    for group in range(2):
        for row in range(lat_count):
            for core in range(2):
                to = target(group, row, core)
                if 0 <= to[1] < lat_count:
                    source = (group * lat_count + row) * 2 + core
                    pairs.append((source, (to[0] * lat_count + to[1]) * 2 + to[2]))
    return pairs


def move(values, target):
    return lax.ppermute(values, AXES, device_pairs(target))


def swap_cores(values):
    return lax.ppermute(values, "lon", [(0, 1), (1, 0)])


def flip_chips(values, flip, sample):
    return move(values, lambda g, l, c: (g ^ sample, l ^ flip, c))


def norm_rows(values, gain):
    average = jnp.mean(values, axis=-1, keepdims=True)
    centered = values - average
    variance = jnp.mean(centered * centered, axis=-1, keepdims=True)
    return (centered * lax.rsqrt(variance + 1e-05) * gain).astype(BF16)


def pick_columns(rows, side, quarter):
    group = lax.axis_index("groups")
    parts = []
    for kind in range(3):
        low = 4 * kind * quarter
        block = [rows[:, low + at * quarter : low + (at + 1) * quarter] for at in range(4)]
        sides = [jnp.where(group == 0, block[2 * at], block[2 * at + 1]) for at in range(2)]
        parts.append(jnp.where(side == 0, sides[0], sides[1]))
    return jnp.concatenate(parts, axis=1)


def pack_body(*refs, weights):
    tokens, bias, gain = refs[:3]
    message, raw, out_own, bias_here, gain_here, rows, sems = refs[-7:]
    count = tokens.shape[0]
    heads, bias_width = bias.shape
    core = lax.axis_index("lon")
    half = rows.shape[0]
    copies = [(gain, gain_here), (bias, bias_here), (tokens, raw)]
    if weights:
        w_qkv, w_out = refs[3:5]
        picked = pl.ds(pl.multiple_of(core * half, half), half)
        copies += [(w_qkv.at[picked, :], rows), (w_out.at[picked, :], out_own)]
    fetches = [
        pltpu.make_async_copy(source, target, sems.at[at])
        for at, (source, target) in enumerate(copies)
    ]
    for fetch in fetches:
        fetch.start()
    message[count:, :] = jnp.zeros((message.shape[0] - count, tokens.shape[1]), BF16)
    for fetch in fetches[:3]:
        fetch.wait()
    message[count : count + heads, :bias_width] = bias_here[...]
    message[:count, :] = norm_rows(raw[...].astype(F32), gain_here[...][None])
    for fetch in fetches[3:]:
        fetch.wait()
    if weights:
        side = lax.rem(lax.axis_index("lat"), 2)
        cross = pick_columns(rows, 1 - side, tokens.shape[1] // 4)
        message[count + 16 :, : cross.shape[1]] = cross


def columns_body(w_qkv, w_out, own, out_own):
    half = own.shape[0]
    start = pl.multiple_of(lax.axis_index("lon") * half, half)
    rows = w_qkv[pl.ds(start, half), :]
    own[...] = pick_columns(rows, lax.rem(lax.axis_index("lat"), 2), own.shape[1] // 3)
    out_own[...] = w_out[pl.ds(start, half), :]


def arrived_body(
    own, by_x, by_y, out_own, out3, out2, out1, bundle, x_block, outs
):
    del by_y
    side = lax.rem(lax.axis_index("lat"), 2)
    rows, width = x_block.shape[0], own.shape[1]
    bundle[side] = own[...]
    bundle[1 - side] = by_x[rows:, :width]
    x_block[...] = by_x[:rows, :]
    for at, block in enumerate((out_own, out1, out2, out3)):
        outs[at] = block[...]


def complete_body(
    bundle, level3, level2, level1, message, x_block, by_y, by_xy, outs, crossed, gains, *results
):
    del gains
    weights, near, both = results
    rows = x_block.shape[0]
    for at, block in enumerate((bundle, level1, level2, level3)):
        weights[at] = block[...]
    for at, block in enumerate((message, x_block, by_y, by_xy)):
        near[at] = block[:rows, :]
    both[0] = outs[...]
    both[1] = crossed[...]


def pair_away(flip):
    pair = lax.rem(lax.axis_index("lat") // 2, 4)
    high, low = pair // 2, pair % 2
    high = 1 - high if flip // 2 else high
    low = 1 - low if flip % 2 else low
    return 2 * high + low


def join_bundles(mine, other, joined):
    core = lax.axis_index("lon")
    half = mine.shape[2]
    for flip in range(4):
        for block, at in ((mine, core), (other, 1 - core)):
            for row in range(2):
                first = pl.multiple_of(((pair_away(flip) * 2 + row) * 2 + at) * half, half)
                joined[pl.ds(first, half), :] = block[flip, row]


def join_columns(mine, other, joined):
    core, side = lax.axis_index("lon"), lax.rem(lax.axis_index("lat"), 2)
    half = mine.shape[2]
    for flip in range(4):
        for block, at in ((mine, core), (other, 1 - core)):
            for cross, row in enumerate((side, 1 - side)):
                first = pl.multiple_of(((pair_away(flip) * 2 + row) * 2 + at) * half, half)
                joined[pl.ds(first, half), :] = block[cross, flip]


def attend_body(*refs):
    (near, far, mine, other), pieces = refs[:4], refs[4:8]
    weights, bias_rows, near_rows, far_rows = refs[8:]
    group, side = lax.axis_index("groups"), lax.rem(lax.axis_index("lat"), 2)
    _, count, quarter = pieces[0].shape
    heads = 3
    head_dim = quarter // heads
    join_bundles(mine, other, weights)
    for slot in range(4):
        near_rows[slot * count : (slot + 1) * count, :] = near[slot, :count, :]
        far_rows[slot * count : (slot + 1) * count, :] = far[slot, :count, :]
    for flip in range(2):
        for at, block in enumerate((near, far)):
            bias_rows[flip, :, at * count : (at + 1) * count] = block[flip, count:, :count].astype(
                F32
            )
    first_head = (2 * side + group) * heads
    here = jnp.dot(near_rows[...], weights[...], preferred_element_type=F32).astype(BF16)
    there = jnp.dot(far_rows[...], weights[:, quarter:], preferred_element_type=F32).astype(BF16)
    for slot in range(4):
        flip, sample = slot % 2, slot // 2
        low_row, high_row = slot * count, (slot + 1) * count
        outs = []
        for head in range(heads):
            low = head * head_dim
            queries = here[low_row:high_row, low : low + head_dim]
            keys, values = (
                jnp.concatenate(
                    [
                        here[low_row:high_row, (kind + 1) * quarter + low :][:, :head_dim],
                        there[low_row:high_row, kind * quarter + low :][:, :head_dim],
                    ]
                )
                for kind in range(2)
            )
            scores = lax.dot_general(
                queries, keys, (((1,), (1,)), ((), ())), preferred_element_type=F32
            ) * (head_dim**-0.5)
            scores = scores + bias_rows[flip, pl.ds(first_head + head, 1), :]
            expd = jnp.exp(scores - jnp.max(scores, axis=-1, keepdims=True))
            totals = jnp.sum(expd, axis=-1, keepdims=True)
            weighted = jnp.dot(expd.astype(BF16), values, preferred_element_type=F32)
            outs.append((weighted / totals).astype(BF16))
        attended = jnp.concatenate(outs, axis=1)
        pieces[2 * sample + flip][0] = attended
        pieces[2 * sample + 1 - flip][1] = attended


def project_out(which, pieces, weights, tokens, gain):
    group, side = lax.axis_index("groups"), lax.rem(lax.axis_index("lat"), 2)
    summed = tokens.astype(F32)
    for slot, piece in enumerate(pieces):
        flip, sample = slot % 2, slot // 2
        quarter = piece.shape[2]
        owner = 2 * (side + flip - 2 * side * flip) + (group + sample - 2 * group * sample)
        rows = pl.ds(pl.multiple_of(owner * quarter, quarter), quarter)
        summed = summed + jnp.dot(piece[which], weights[rows, :], preferred_element_type=F32)
    middle = summed.astype(BF16)
    return middle, norm_rows(middle.astype(F32), gain)


def other_body(gain, piece3, piece2, piece1, piece0, weights, tokens, other_in):
    pieces = (piece0, piece1, piece2, piece3)
    other_in[...] = project_out(1, pieces, weights, tokens[...], gain[...])[1]


def tent_pair(row_count, first_col, col_count, half_width):
    rows = lax.broadcasted_iota(jnp.int32, (row_count, col_count), 0)
    cols = lax.broadcasted_iota(jnp.int32, (row_count, col_count), 1) + first_col
    offset = ((cols - rows + row_count // 2) & (row_count - 1)) - row_count // 2
    distance = jnp.abs(offset).astype(F32)
    span_plus = (half_width + 1).astype(F32)
    tent = jnp.where(
        distance <= half_width.astype(F32), (1.0 - distance / span_plus) / span_plus, 0.0
    )
    odd = tent * offset.astype(F32) / span_plus
    return tent.astype(BF16), odd.astype(BF16)


def mix(lines, blocks, basis):
    size = blocks.shape[2]
    return jnp.concatenate(
        [
            jnp.dot(
                lines[:, tile * size : (tile + 1) * size],
                blocks[basis, tile],
                preferred_element_type=F32,
            ).astype(BF16)
            for tile in range(blocks.shape[1])
        ],
        axis=1,
    )


def plan_body(
    lat_count, lon_half, lat_half, quad_off, taps, w_conv, message, blocks, coeffs, gains
):
    del message
    lat_row, core = lax.axis_index("lat"), lax.axis_index("lon")
    side = lax.rem(lat_row, 2)
    for basis in range(2):
        below, centre, above = (taps[quad_off[0] + row, basis] for row in range(3))
        below = jnp.where(lat_half[0] >= 1, below, 0.0)
        above = jnp.where(lat_half[0] >= 1, above, 0.0)
        other = jnp.where(side == 0, above, below)
        halo = jnp.where(side == 0, below, above)
        pole = jnp.where(lat_row == 0, below, 0.0) + jnp.where(
            lat_row == lat_count - 1, above, 0.0
        )
        for at, value in enumerate((other, centre, halo, pole)):
            gains[4 * basis + at : 4 * basis + at + 1, :] = jnp.full((1, 128), value, F32)
    rows, count = coeffs.shape[0], coeffs.shape[1] // 4
    direct = tent_pair(rows, core * count, count, lon_half[0])
    rolled = tent_pair(rows, core * count + count, count, lon_half[0])
    for at, part in enumerate((direct[0], direct[1], rolled[0], rolled[1])):
        coeffs[:, at * count : (at + 1) * count] = part
    size = w_conv.shape[2]
    blocks[...] = jnp.zeros(blocks.shape, BF16)
    per_block = blocks.shape[2] // size
    for basis in range(blocks.shape[0]):
        for tile in range(blocks.shape[1]):
            for at in range(per_block):
                first = (tile * per_block + at) * size
                low, high = at * size, (at + 1) * size
                blocks[basis, tile, low:high, low:high] = w_conv[basis, first : first + size, :]


def own_body(
    gains,
    gain,
    piece3,
    piece2,
    piece1,
    piece0,
    weights,
    tokens,
    other_in,
    blocks,
    coeffs,
    middle,
    partial,
):
    count = tokens.shape[0]
    pieces = (piece0, piece1, piece2, piece3)
    own_middle, own_in = project_out(0, pieces, weights, tokens[...], gain[...])
    middle[...] = own_middle
    own = own_in.astype(F32)
    neighbour = other_in[...].astype(F32)
    direct, rolled = [], []
    for basis in range(2):
        other, centre, _, pole = (gains[4 * basis + at : 4 * basis + at + 1, :1] for at in range(4))
        lines = jnp.concatenate(
            [(other * neighbour + centre * own).astype(BF16), (pole * own).astype(BF16)]
        )
        mixed = mix(lines, blocks, basis)
        direct.append(mixed[:count])
        rolled.append(mixed[count:])
    partial[...] = jnp.dot(
        coeffs[...], jnp.concatenate(direct + rolled), preferred_element_type=F32
    )


def halo_body(gains, halo, blocks, coeffs, middle, partial, kept, sent, total):
    core = lax.axis_index("lon")
    count = halo.shape[0]
    values = halo[...].astype(F32)
    mixed = [
        mix((gains[4 * basis + 2 : 4 * basis + 3, :1] * values).astype(BF16), blocks, basis)
        for basis in range(2)
    ]
    total[...] = partial[...] + jnp.dot(
        coeffs[:, : 2 * count], jnp.concatenate(mixed), preferred_element_type=F32
    )
    here = pl.multiple_of(core * count, count)
    there = pl.multiple_of((1 - core) * count, count)
    kept[...] = middle[...].astype(F32) + total[pl.ds(here, count), :]
    sent[...] = total[pl.ds(there, count), :].astype(BF16)


def pack_plain(weights, columns):
    core, lat_count = lax.axis_index("lon"), lax.axis_size("lat")
    half, width = weights.shape[0] // 2, weights.shape[1]
    rows = lax.dynamic_slice_in_dim(weights, core * half, half, 0)
    if columns == width:
        return jnp.broadcast_to(rows[None], (lat_count, half, columns))
    rows = rows.reshape(half, 3, 2, 2, columns // 3)
    rows = lax.dynamic_index_in_dim(rows, lax.axis_index("groups"), 3, keepdims=False)
    rows = rows.transpose(2, 0, 1, 3).reshape(2, half, columns)
    rows = jnp.broadcast_to(rows[None], (lat_count // 2, 2, half, columns))
    return rows.reshape(lat_count, half, columns)


def gather_plain(weights, columns):
    core = lax.axis_index("lon")
    mine = lax.all_to_all(pack_plain(weights, columns), "lat", 0, 0)
    other = swap_cores(mine)
    both = jnp.where(core == 0, jnp.stack([mine, other], 1), jnp.stack([other, mine], 1))
    whole = both.reshape(4, 2, 2, -1, columns)
    pair = lax.rem(lax.axis_index("lat") // 2, 4)
    whole = jnp.stack(
        [lax.dynamic_index_in_dim(whole, pair ^ flip, 0, keepdims=False) for flip in range(4)]
    )
    return [
        lax.dynamic_index_in_dim(whole, at, 2, keepdims=False) for at in (core, 1 - core)
    ]


def flip_levels(bundle):
    moved = [move(bundle, lambda g, l, c: (g, l ^ (2 * flip), c)) for flip in (3, 2, 1)]
    return moved[::-1]


def per_device(
    tokens,
    gain_attn,
    w_qkv,
    key_bias,
    w_out,
    gain_conv,
    w_conv,
    lat_taps,
    lon_half,
    lat_half,
    quad_off,
):
    own_tokens = tokens[0]
    count, width = own_tokens.shape
    quarter = width // 4
    lat_count = lax.axis_size("lat")
    half = w_qkv.shape[0] // 2
    gain_conv = gain_conv[None]

    direct = half % 16 == 0 and lat_count == 8
    rows = count + 16
    message, raw_tokens, out_own = call(
        functools.partial(pack_body, weights=direct),
        [
            ((rows + (half if direct else 0), width), BF16),
            ((count, width), BF16),
            ((half, width), BF16),
        ],
        [HBM] * (5 if direct else 3),
        (own_tokens, key_bias[0], gain_attn) + ((w_qkv, w_out) if direct else ()),
        10 * count * width,
        [
            pltpu.VMEM(key_bias.shape[1:], BF16),
            pltpu.VMEM((width,), F32),
            pltpu.VMEM((half, 3 * width), BF16),
            pltpu.SemaphoreType.DMA((5,)),
        ],
        limit=56,
    )

    by_x, by_y = flip_chips(message, 1, 0), flip_chips(message, 0, 1)
    x_block = by_x
    if direct:
        levels = flip_levels(out_own)
        qkv_own, out_own = call(
            columns_body,
            [((half, 3 * quarter), BF16), ((half, width), BF16)],
            [VMEM] * 2,
            (w_qkv, w_out),
            0,
        )
        bundle, x_block, outs = call(
            arrived_body,
            [
                ((2, half, 3 * quarter), BF16),
                ((rows, width), BF16),
                ((4, half, width), BF16),
            ],
            [VMEM] * 7,
            (qkv_own, by_x, by_y, out_own, *levels[::-1]),
            0,
        )
    size = 4 * w_conv.shape[2]
    diagonal, coeffs, gains = call(
        functools.partial(plan_body, lat_count),
        [
            ((2, width // size, size, size), BF16),
            ((2 * count, 4 * count), BF16),
            ((8, 128), F32),
        ],
        [SMEM] * 4 + [VMEM, ANY],
        (lon_half, lat_half, quad_off, lat_taps, w_conv, x_block),
        0,
    )
    if direct:
        qkv_mine, near, out_mine = call(
            complete_body,
            [
                ((4, 2, half, 3 * quarter), BF16),
                ((4, rows, width), BF16),
                ((2, 4, half, width), BF16),
            ],
            [VMEM] * 11,
            (
                bundle,
                *flip_levels(bundle)[::-1],
                message,
                x_block,
                by_y,
                flip_chips(x_block, 0, 1),
                outs,
                flip_chips(outs, 1, 0),
                gains,
            ),
            0,
        )
        qkv_other, out_other = swap_cores(qkv_mine), swap_cores(out_mine)
        join = join_columns
    else:
        near = jnp.stack([message, by_x, by_y, flip_chips(by_x, 0, 1)])
        qkv_mine, qkv_other = gather_plain(w_qkv, 3 * quarter)
        out_mine, out_other = gather_plain(w_out, width)
        join = join_bundles
    far = swap_cores(near)
    raw_tokens = gate(raw_tokens, qkv_mine)
    other_tokens = flip_chips(raw_tokens, 1, 0)

    pieces = call(
        attend_body,
        [((2, count, quarter), BF16)] * 4,
        [VMEM] * 4,
        (near, far, qkv_mine, qkv_other),
        2 * 1024 * width * 3 * quarter,
        [
            pltpu.VMEM((width, 3 * quarter), BF16),
            pltpu.VMEM((2, 16, 2 * count), F32),
            pltpu.VMEM((4 * count, width), BF16),
            pltpu.VMEM((4 * count, width), BF16),
        ],
    )
    back = [
        flip_chips(piece, flip, sample) for piece, (flip, sample) in zip(pieces[:0:-1], FLIPS[::-1])
    ]
    back = [pieces[0]] + back[::-1]
    (full_out,) = call(
        join, [((width, width), BF16)], [VMEM] * 2, (out_mine, out_other), 0
    )
    (other_in,) = call(
        other_body,
        [((count, width), BF16)],
        [VMEM] * 7,
        (gain_conv, *back[::-1], full_out, other_tokens),
        2 * count * width * width,
    )
    halo = move(other_in, lambda g, l, c: (g, l + 2 - 4 * (l % 2), c))
    middle, partial = call(
        own_body,
        [((count, width), BF16), ((2 * count, width), F32)],
        [VMEM] * 11,
        (gains, gain_conv, *back[::-1], full_out, raw_tokens, other_in, diagonal, coeffs),
        2 * count * width * width * 3,
    )
    kept, sent = call(
        halo_body,
        [((count, width), F32), ((count, width), BF16)],
        [VMEM] * 6,
        (gains, halo, diagonal, coeffs, middle, partial),
        2 * 256 * 256 * width,
        [pltpu.VMEM((2 * count, width), F32)],
    )
    received = swap_cores(sent)
    return (kept + received.astype(F32)).astype(BF16)[None]


def solution(mesh):
    return jax.shard_map(
        per_device,
        mesh=mesh,
        in_specs=(
            P(("groups", "lat"), "lon", None),
            P(),
            P("lat", None),
            P("lat", None, "lon"),
            P("lat", None),
            P(),
            P(),
            P(),
            P("lat"),
            P("lat"),
            P("lat"),
        ),
        out_specs=P(("groups", "lat"), "lon", None),
        check_vma=False,
    )
```

```python
import functools

import jax
import jax.numpy as jnp
from jax import lax
from jax.experimental import pallas as pl
from jax.experimental.pallas import tpu as pltpu
from jax.sharding import PartitionSpec as P

AXES = ("groups", "lat", "lon")
VMEM = pl.BlockSpec(memory_space=pltpu.VMEM)
ANY = pl.BlockSpec(memory_space=pl.ANY)
HBM = pl.BlockSpec(memory_space=pltpu.HBM)
FLIPS = ((1, 0), (0, 1), (1, 1))
SMEM = pl.BlockSpec(memory_space=pltpu.SMEM)
BF16 = jnp.bfloat16
F32 = jnp.float32


def call(body, outs, specs, args, flops, scratch=(), limit=32):
    outs = tuple(jax.ShapeDtypeStruct(shape, dtype) for shape, dtype in outs)
    moved = sum(a.size * a.dtype.itemsize for a in args)
    return pl.pallas_call(
        body,
        out_shape=outs,
        in_specs=specs,
        out_specs=tuple(VMEM for _ in outs),
        scratch_shapes=list(scratch),
        compiler_params=pltpu.CompilerParams(vmem_limit_bytes=limit * 1024 * 1024),
        cost_estimate=pl.CostEstimate(flops=flops, bytes_accessed=moved, transcendentals=0),
    )(*args)


def device_pairs(target):
    lat_count = lax.axis_size("lat")
    pairs = []
    for group in range(2):
        for row in range(lat_count):
            for core in range(2):
                to = target(group, row, core)
                if 0 <= to[1] < lat_count:
                    source = (group * lat_count + row) * 2 + core
                    pairs.append((source, (to[0] * lat_count + to[1]) * 2 + to[2]))
    return pairs


def move(values, target):
    return lax.ppermute(values, AXES, device_pairs(target))


def swap_cores(values):
    return lax.ppermute(values, "lon", [(0, 1), (1, 0)])


def flip_chips(values, flip, sample):
    return move(values, lambda g, l, c: (g ^ sample, l ^ flip, c))


def norm_rows(values, gain):
    average = jnp.mean(values, axis=-1, keepdims=True)
    centered = values - average
    variance = jnp.mean(centered * centered, axis=-1, keepdims=True)
    return (centered * lax.rsqrt(variance + 1e-05) * gain).astype(BF16)


def pick_columns(rows, side, quarter):
    group = lax.axis_index("groups")
    parts = []
    for kind in range(3):
        low = 4 * kind * quarter
        block = [rows[:, low + at * quarter : low + (at + 1) * quarter] for at in range(4)]
        sides = [jnp.where(group == 0, block[2 * at], block[2 * at + 1]) for at in range(2)]
        parts.append(jnp.where(side == 0, sides[0], sides[1]))
    return jnp.concatenate(parts, axis=1)


def pack_body(*refs, weights):
    tokens, bias, gain = refs[:3]
    message, raw, out_own, bias_here, gain_here, rows, sems = refs[-7:]
    count = tokens.shape[0]
    heads, bias_width = bias.shape
    core = lax.axis_index("lon")
    half = rows.shape[0]
    copies = [(gain, gain_here), (bias, bias_here), (tokens, raw)]
    if weights:
        w_qkv, w_out = refs[3:5]
        picked = pl.ds(pl.multiple_of(core * half, half), half)
        copies += [(w_qkv.at[picked, :], rows), (w_out.at[picked, :], out_own)]
    fetches = [
        pltpu.make_async_copy(source, target, sems.at[at])
        for at, (source, target) in enumerate(copies)
    ]
    for fetch in fetches:
        fetch.start()
    message[count:, :] = jnp.zeros((message.shape[0] - count, tokens.shape[1]), BF16)
    for fetch in fetches[:3]:
        fetch.wait()
    message[count : count + heads, :bias_width] = bias_here[...]
    message[:count, :] = norm_rows(raw[...].astype(F32), gain_here[...][None])
    for fetch in fetches[3:]:
        fetch.wait()
    if weights:
        side = lax.rem(lax.axis_index("lat"), 2)
        cross = pick_columns(rows, 1 - side, tokens.shape[1] // 4)
        message[count + 16 :, : cross.shape[1]] = cross


def columns_body(w_qkv, w_out, own, out_own):
    half = own.shape[0]
    start = pl.multiple_of(lax.axis_index("lon") * half, half)
    rows = w_qkv[pl.ds(start, half), :]
    own[...] = pick_columns(rows, lax.rem(lax.axis_index("lat"), 2), own.shape[1] // 3)
    out_own[...] = w_out[pl.ds(start, half), :]


def arrived_body(
    own, by_x, by_y, out_own, out3, out2, out1, raw, bundle, x_block, cargo
):
    del by_y
    side = lax.rem(lax.axis_index("lat"), 2)
    rows, width = x_block.shape[0], own.shape[1]
    bundle[side] = own[...]
    bundle[1 - side] = by_x[rows:, :width]
    x_block[...] = by_x[:rows, :]
    half = out_own.shape[0]
    for at, block in enumerate((out_own, out1, out2, out3)):
        cargo[at * half : (at + 1) * half, :] = block[...]
    cargo[4 * half :, :] = raw[...]


def complete_body(
    bundle, level3, level2, level1, message, x_block, by_y, by_xy, cargo, crossed, gains, *results
):
    del gains
    weights, near, both, raw_x = results
    rows = x_block.shape[0]
    for at, block in enumerate((bundle, level1, level2, level3)):
        weights[at] = block[...]
    for at, block in enumerate((message, x_block, by_y, by_xy)):
        near[at] = block[:rows, :]
    half = both.shape[2]
    for at in range(4):
        both[0, at] = cargo[at * half : (at + 1) * half, :]
        both[1, at] = crossed[at * half : (at + 1) * half, :]
    raw_x[...] = crossed[4 * half :, :]


def pair_away(flip):
    pair = lax.rem(lax.axis_index("lat") // 2, 4)
    high, low = pair // 2, pair % 2
    high = 1 - high if flip // 2 else high
    low = 1 - low if flip % 2 else low
    return 2 * high + low


def join_bundles(mine, other, joined):
    core = lax.axis_index("lon")
    half = mine.shape[2]
    for flip in range(4):
        for block, at in ((mine, core), (other, 1 - core)):
            for row in range(2):
                first = pl.multiple_of(((pair_away(flip) * 2 + row) * 2 + at) * half, half)
                joined[pl.ds(first, half), :] = block[flip, row]


def join_columns(mine, other, joined):
    core, side = lax.axis_index("lon"), lax.rem(lax.axis_index("lat"), 2)
    half = mine.shape[2]
    for flip in range(4):
        for block, at in ((mine, core), (other, 1 - core)):
            for cross, row in enumerate((side, 1 - side)):
                first = pl.multiple_of(((pair_away(flip) * 2 + row) * 2 + at) * half, half)
                joined[pl.ds(first, half), :] = block[cross, flip]


def attend_body(*refs):
    (near, far, mine, other), pieces = refs[:4], refs[4:8]
    weights, bias_rows, near_rows, far_rows = refs[8:]
    group, side = lax.axis_index("groups"), lax.rem(lax.axis_index("lat"), 2)
    _, count, quarter = pieces[0].shape
    heads = 3
    head_dim = quarter // heads
    join_bundles(mine, other, weights)
    for slot in range(4):
        near_rows[slot * count : (slot + 1) * count, :] = near[slot, :count, :]
        far_rows[slot * count : (slot + 1) * count, :] = far[slot, :count, :]
    for flip in range(2):
        for at, block in enumerate((near, far)):
            bias_rows[flip, :, at * count : (at + 1) * count] = block[flip, count:, :count].astype(
                F32
            )
    first_head = (2 * side + group) * heads
    here = jnp.dot(near_rows[...], weights[...], preferred_element_type=F32).astype(BF16)
    there = jnp.dot(far_rows[...], weights[:, quarter:], preferred_element_type=F32).astype(BF16)
    for slot in range(4):
        flip, sample = slot % 2, slot // 2
        low_row, high_row = slot * count, (slot + 1) * count
        outs = []
        for head in range(heads):
            low = head * head_dim
            queries = here[low_row:high_row, low : low + head_dim]
            keys, values = (
                jnp.concatenate(
                    [
                        here[low_row:high_row, (kind + 1) * quarter + low :][:, :head_dim],
                        there[low_row:high_row, kind * quarter + low :][:, :head_dim],
                    ]
                )
                for kind in range(2)
            )
            scores = lax.dot_general(
                queries, keys, (((1,), (1,)), ((), ())), preferred_element_type=F32
            ) * (head_dim**-0.5)
            scores = scores + bias_rows[flip, pl.ds(first_head + head, 1), :]
            expd = jnp.exp(scores - jnp.max(scores, axis=-1, keepdims=True))
            totals = jnp.sum(expd, axis=-1, keepdims=True)
            weighted = jnp.dot(expd.astype(BF16), values, preferred_element_type=F32)
            outs.append((weighted / totals).astype(BF16))
        attended = jnp.concatenate(outs, axis=1)
        pieces[2 * sample + flip][0] = attended
        pieces[2 * sample + 1 - flip][1] = attended


def project_out(which, pieces, weights, tokens, gain):
    group, side = lax.axis_index("groups"), lax.rem(lax.axis_index("lat"), 2)
    summed = tokens.astype(F32)
    for slot, piece in enumerate(pieces):
        flip, sample = slot % 2, slot // 2
        quarter = piece.shape[2]
        owner = 2 * (side + flip - 2 * side * flip) + (group + sample - 2 * group * sample)
        rows = pl.ds(pl.multiple_of(owner * quarter, quarter), quarter)
        summed = summed + jnp.dot(piece[which], weights[rows, :], preferred_element_type=F32)
    middle = summed.astype(BF16)
    return middle, norm_rows(middle.astype(F32), gain)


def other_body(gain, piece3, piece2, piece1, piece0, weights, tokens, other_in):
    pieces = (piece0, piece1, piece2, piece3)
    other_in[...] = project_out(1, pieces, weights, tokens[...], gain[...])[1]


def tent_pair(row_count, first_col, col_count, half_width):
    rows = lax.broadcasted_iota(jnp.int32, (row_count, col_count), 0)
    cols = lax.broadcasted_iota(jnp.int32, (row_count, col_count), 1) + first_col
    offset = ((cols - rows + row_count // 2) & (row_count - 1)) - row_count // 2
    distance = jnp.abs(offset).astype(F32)
    span_plus = (half_width + 1).astype(F32)
    tent = jnp.where(
        distance <= half_width.astype(F32), (1.0 - distance / span_plus) / span_plus, 0.0
    )
    odd = tent * offset.astype(F32) / span_plus
    return tent.astype(BF16), odd.astype(BF16)


def mix(lines, blocks, basis):
    size = blocks.shape[2]
    return jnp.concatenate(
        [
            jnp.dot(
                lines[:, tile * size : (tile + 1) * size],
                blocks[basis, tile],
                preferred_element_type=F32,
            ).astype(BF16)
            for tile in range(blocks.shape[1])
        ],
        axis=1,
    )


def plan_body(
    lat_count, lon_half, lat_half, quad_off, taps, w_conv, message, blocks, coeffs, gains
):
    del message
    lat_row, core = lax.axis_index("lat"), lax.axis_index("lon")
    side = lax.rem(lat_row, 2)
    for basis in range(2):
        below, centre, above = (taps[quad_off[0] + row, basis] for row in range(3))
        below = jnp.where(lat_half[0] >= 1, below, 0.0)
        above = jnp.where(lat_half[0] >= 1, above, 0.0)
        other = jnp.where(side == 0, above, below)
        halo = jnp.where(side == 0, below, above)
        pole = jnp.where(lat_row == 0, below, 0.0) + jnp.where(
            lat_row == lat_count - 1, above, 0.0
        )
        for at, value in enumerate((other, centre, halo, pole)):
            gains[4 * basis + at : 4 * basis + at + 1, :] = jnp.full((1, 128), value, F32)
    rows, count = coeffs.shape[0], coeffs.shape[1] // 4
    direct = tent_pair(rows, core * count, count, lon_half[0])
    rolled = tent_pair(rows, core * count + count, count, lon_half[0])
    for at, part in enumerate((direct[0], direct[1], rolled[0], rolled[1])):
        coeffs[:, at * count : (at + 1) * count] = part
    size = w_conv.shape[2]
    blocks[...] = jnp.zeros(blocks.shape, BF16)
    per_block = blocks.shape[2] // size
    for basis in range(blocks.shape[0]):
        for tile in range(blocks.shape[1]):
            for at in range(per_block):
                first = (tile * per_block + at) * size
                low, high = at * size, (at + 1) * size
                blocks[basis, tile, low:high, low:high] = w_conv[basis, first : first + size, :]


def own_body(
    gains,
    gain,
    piece3,
    piece2,
    piece1,
    piece0,
    weights,
    tokens,
    other_in,
    blocks,
    coeffs,
    middle,
    partial,
):
    count = tokens.shape[0]
    pieces = (piece0, piece1, piece2, piece3)
    own_middle, own_in = project_out(0, pieces, weights, tokens[...], gain[...])
    middle[...] = own_middle
    own = own_in.astype(F32)
    neighbour = other_in[...].astype(F32)
    direct, rolled = [], []
    for basis in range(2):
        other, centre, _, pole = (gains[4 * basis + at : 4 * basis + at + 1, :1] for at in range(4))
        lines = jnp.concatenate(
            [(other * neighbour + centre * own).astype(BF16), (pole * own).astype(BF16)]
        )
        mixed = mix(lines, blocks, basis)
        direct.append(mixed[:count])
        rolled.append(mixed[count:])
    partial[...] = jnp.dot(
        coeffs[...], jnp.concatenate(direct + rolled), preferred_element_type=F32
    )


def halo_body(gains, halo, blocks, coeffs, middle, partial, kept, sent, total):
    core = lax.axis_index("lon")
    count = halo.shape[0]
    values = halo[...].astype(F32)
    mixed = [
        mix((gains[4 * basis + 2 : 4 * basis + 3, :1] * values).astype(BF16), blocks, basis)
        for basis in range(2)
    ]
    total[...] = partial[...] + jnp.dot(
        coeffs[:, : 2 * count], jnp.concatenate(mixed), preferred_element_type=F32
    )
    here = pl.multiple_of(core * count, count)
    there = pl.multiple_of((1 - core) * count, count)
    kept[...] = middle[...].astype(F32) + total[pl.ds(here, count), :]
    sent[...] = total[pl.ds(there, count), :].astype(BF16)


def pack_plain(weights, columns):
    core, lat_count = lax.axis_index("lon"), lax.axis_size("lat")
    half, width = weights.shape[0] // 2, weights.shape[1]
    rows = lax.dynamic_slice_in_dim(weights, core * half, half, 0)
    if columns == width:
        return jnp.broadcast_to(rows[None], (lat_count, half, columns))
    rows = rows.reshape(half, 3, 2, 2, columns // 3)
    rows = lax.dynamic_index_in_dim(rows, lax.axis_index("groups"), 3, keepdims=False)
    rows = rows.transpose(2, 0, 1, 3).reshape(2, half, columns)
    rows = jnp.broadcast_to(rows[None], (lat_count // 2, 2, half, columns))
    return rows.reshape(lat_count, half, columns)


def gather_plain(weights, columns):
    core = lax.axis_index("lon")
    mine = lax.all_to_all(pack_plain(weights, columns), "lat", 0, 0)
    other = swap_cores(mine)
    both = jnp.where(core == 0, jnp.stack([mine, other], 1), jnp.stack([other, mine], 1))
    whole = both.reshape(4, 2, 2, -1, columns)
    pair = lax.rem(lax.axis_index("lat") // 2, 4)
    whole = jnp.stack(
        [lax.dynamic_index_in_dim(whole, pair ^ flip, 0, keepdims=False) for flip in range(4)]
    )
    return [
        lax.dynamic_index_in_dim(whole, at, 2, keepdims=False) for at in (core, 1 - core)
    ]


def flip_levels(bundle):
    moved = [move(bundle, lambda g, l, c: (g, l ^ (2 * flip), c)) for flip in (3, 2, 1)]
    return moved[::-1]


def per_device(
    tokens,
    gain_attn,
    w_qkv,
    key_bias,
    w_out,
    gain_conv,
    w_conv,
    lat_taps,
    lon_half,
    lat_half,
    quad_off,
):
    own_tokens = tokens[0]
    count, width = own_tokens.shape
    quarter = width // 4
    lat_count = lax.axis_size("lat")
    half = w_qkv.shape[0] // 2
    gain_conv = gain_conv[None]

    direct = half % 16 == 0 and lat_count == 8
    rows = count + 16
    message, raw_tokens, out_own = call(
        functools.partial(pack_body, weights=direct),
        [
            ((rows + (half if direct else 0), width), BF16),
            ((count, width), BF16),
            ((half, width), BF16),
        ],
        [HBM] * (5 if direct else 3),
        (own_tokens, key_bias[0], gain_attn) + ((w_qkv, w_out) if direct else ()),
        10 * count * width,
        [
            pltpu.VMEM(key_bias.shape[1:], BF16),
            pltpu.VMEM((width,), F32),
            pltpu.VMEM((half, 3 * width), BF16),
            pltpu.SemaphoreType.DMA((5,)),
        ],
        limit=56,
    )

    by_x, by_y = flip_chips(message, 1, 0), flip_chips(message, 0, 1)
    x_block = by_x
    if direct:
        levels = flip_levels(out_own)
        qkv_own, out_own = call(
            columns_body,
            [((half, 3 * quarter), BF16), ((half, width), BF16)],
            [VMEM] * 2,
            (w_qkv, w_out),
            0,
        )
        bundle, x_block, cargo = call(
            arrived_body,
            [
                ((2, half, 3 * quarter), BF16),
                ((rows, width), BF16),
                ((4 * half + count, width), BF16),
            ],
            [VMEM] * 8,
            (qkv_own, by_x, by_y, out_own, *levels[::-1], raw_tokens),
            0,
        )
    size = 4 * w_conv.shape[2]
    diagonal, coeffs, gains = call(
        functools.partial(plan_body, lat_count),
        [
            ((2, width // size, size, size), BF16),
            ((2 * count, 4 * count), BF16),
            ((8, 128), F32),
        ],
        [SMEM] * 4 + [VMEM, ANY],
        (lon_half, lat_half, quad_off, lat_taps, w_conv, x_block),
        0,
    )
    if direct:
        qkv_mine, near, out_mine, other_tokens = call(
            complete_body,
            [
                ((4, 2, half, 3 * quarter), BF16),
                ((4, rows, width), BF16),
                ((2, 4, half, width), BF16),
                ((count, width), BF16),
            ],
            [VMEM] * 11,
            (
                bundle,
                *flip_levels(bundle)[::-1],
                message,
                x_block,
                by_y,
                flip_chips(x_block, 0, 1),
                cargo,
                flip_chips(cargo, 1, 0),
                gains,
            ),
            0,
        )
        qkv_other, out_other = swap_cores(qkv_mine), swap_cores(out_mine)
        join = join_columns
    else:
        near = jnp.stack([message, by_x, by_y, flip_chips(by_x, 0, 1)])
        other_tokens = flip_chips(raw_tokens, 1, 0)
        qkv_mine, qkv_other = gather_plain(w_qkv, 3 * quarter)
        out_mine, out_other = gather_plain(w_out, width)
        join = join_bundles
    far = swap_cores(near)

    pieces = call(
        attend_body,
        [((2, count, quarter), BF16)] * 4,
        [VMEM] * 4,
        (near, far, qkv_mine, qkv_other),
        2 * 1024 * width * 3 * quarter,
        [
            pltpu.VMEM((width, 3 * quarter), BF16),
            pltpu.VMEM((2, 16, 2 * count), F32),
            pltpu.VMEM((4 * count, width), BF16),
            pltpu.VMEM((4 * count, width), BF16),
        ],
    )
    back = [
        flip_chips(piece, flip, sample) for piece, (flip, sample) in zip(pieces[:0:-1], FLIPS[::-1])
    ]
    back = [pieces[0]] + back[::-1]
    (full_out,) = call(
        join, [((width, width), BF16)], [VMEM] * 2, (out_mine, out_other), 0
    )
    (other_in,) = call(
        other_body,
        [((count, width), BF16)],
        [VMEM] * 7,
        (gain_conv, *back[::-1], full_out, other_tokens),
        2 * count * width * width,
    )
    halo = move(other_in, lambda g, l, c: (g, l + 2 - 4 * (l % 2), c))
    middle, partial = call(
        own_body,
        [((count, width), BF16), ((2 * count, width), F32)],
        [VMEM] * 11,
        (gains, gain_conv, *back[::-1], full_out, raw_tokens, other_in, diagonal, coeffs),
        2 * count * width * width * 3,
    )
    kept, sent = call(
        halo_body,
        [((count, width), F32), ((count, width), BF16)],
        [VMEM] * 6,
        (gains, halo, diagonal, coeffs, middle, partial),
        2 * 256 * 256 * width,
        [pltpu.VMEM((2 * count, width), F32)],
    )
    received = swap_cores(sent)
    return (kept + received.astype(F32)).astype(BF16)[None]


def solution(mesh):
    return jax.shard_map(
        per_device,
        mesh=mesh,
        in_specs=(
            P(("groups", "lat"), "lon", None),
            P(),
            P("lat", None),
            P("lat", None, "lon"),
            P("lat", None),
            P(),
            P(),
            P(),
            P("lat"),
            P("lat"),
            P("lat"),
        ),
        out_specs=P(("groups", "lat"), "lon", None),
        check_vma=False,
    )
```

```python
import functools

import jax
import jax.numpy as jnp
from jax import lax
from jax.experimental import pallas as pl
from jax.experimental.pallas import tpu as pltpu
from jax.sharding import PartitionSpec as P

AXES = ("groups", "lat", "lon")
VMEM = pl.BlockSpec(memory_space=pltpu.VMEM)
ANY = pl.BlockSpec(memory_space=pl.ANY)
HBM = pl.BlockSpec(memory_space=pltpu.HBM)
FLIPS = ((1, 0), (0, 1), (1, 1))
SMEM = pl.BlockSpec(memory_space=pltpu.SMEM)
BF16 = jnp.bfloat16
F32 = jnp.float32


def call(body, outs, specs, args, flops, scratch=(), limit=32):
    outs = tuple(jax.ShapeDtypeStruct(shape, dtype) for shape, dtype in outs)
    moved = sum(a.size * a.dtype.itemsize for a in args)
    return pl.pallas_call(
        body,
        out_shape=outs,
        in_specs=specs,
        out_specs=tuple(VMEM for _ in outs),
        scratch_shapes=list(scratch),
        compiler_params=pltpu.CompilerParams(vmem_limit_bytes=limit * 1024 * 1024),
        cost_estimate=pl.CostEstimate(flops=flops, bytes_accessed=moved, transcendentals=0),
    )(*args)


def copy_body(*refs):
    refs[-1][...] = refs[0][...]


def gate(value, *after):
    specs = [VMEM] * (1 + len(after))
    return call(copy_body, [(value.shape, value.dtype)], specs, (value, *after), 0)[0]


def device_pairs(target):
    lat_count = lax.axis_size("lat")
    pairs = []
    for group in range(2):
        for row in range(lat_count):
            for core in range(2):
                to = target(group, row, core)
                if 0 <= to[1] < lat_count:
                    source = (group * lat_count + row) * 2 + core
                    pairs.append((source, (to[0] * lat_count + to[1]) * 2 + to[2]))
    return pairs


def move(values, target):
    return lax.ppermute(values, AXES, device_pairs(target))


def swap_cores(values):
    return lax.ppermute(values, "lon", [(0, 1), (1, 0)])


def flip_chips(values, flip, sample):
    return move(values, lambda g, l, c: (g ^ sample, l ^ flip, c))


def norm_rows(values, gain):
    average = jnp.mean(values, axis=-1, keepdims=True)
    centered = values - average
    variance = jnp.mean(centered * centered, axis=-1, keepdims=True)
    return (centered * lax.rsqrt(variance + 1e-05) * gain).astype(BF16)


def pick_columns(rows, side, quarter):
    group = lax.axis_index("groups")
    parts = []
    for kind in range(3):
        low = 4 * kind * quarter
        block = [rows[:, low + at * quarter : low + (at + 1) * quarter] for at in range(4)]
        sides = [jnp.where(group == 0, block[2 * at], block[2 * at + 1]) for at in range(2)]
        parts.append(jnp.where(side == 0, sides[0], sides[1]))
    return jnp.concatenate(parts, axis=1)


def pack_body(*refs, weights):
    tokens, bias, gain = refs[:3]
    message, raw, out_own, bias_here, gain_here, rows, sems = refs[-7:]
    count = tokens.shape[0]
    heads, bias_width = bias.shape
    core = lax.axis_index("lon")
    half = rows.shape[0]
    copies = [(gain, gain_here), (bias, bias_here), (tokens, raw)]
    if weights:
        w_qkv, w_out = refs[3:5]
        picked = pl.ds(pl.multiple_of(core * half, half), half)
        copies += [(w_qkv.at[picked, :], rows), (w_out.at[picked, :], out_own)]
    fetches = [
        pltpu.make_async_copy(source, target, sems.at[at])
        for at, (source, target) in enumerate(copies)
    ]
    for fetch in fetches:
        fetch.start()
    message[count:, :] = jnp.zeros((message.shape[0] - count, tokens.shape[1]), BF16)
    for fetch in fetches[:3]:
        fetch.wait()
    message[count : count + heads, :bias_width] = bias_here[...]
    message[:count, :] = norm_rows(raw[...].astype(F32), gain_here[...][None])
    for fetch in fetches[3:]:
        fetch.wait()
    if weights:
        side = lax.rem(lax.axis_index("lat"), 2)
        cross = pick_columns(rows, 1 - side, tokens.shape[1] // 4)
        message[count + 16 :, : cross.shape[1]] = cross


def columns_body(w_qkv, w_out, own, out_own):
    half = own.shape[0]
    start = pl.multiple_of(lax.axis_index("lon") * half, half)
    rows = w_qkv[pl.ds(start, half), :]
    own[...] = pick_columns(rows, lax.rem(lax.axis_index("lat"), 2), own.shape[1] // 3)
    out_own[...] = w_out[pl.ds(start, half), :]


def arrived_body(
    own, by_x, by_y, out_own, out3, out2, out1, bundle, x_block, outs
):
    del by_y
    side = lax.rem(lax.axis_index("lat"), 2)
    rows, width = x_block.shape[0], own.shape[1]
    bundle[side] = own[...]
    bundle[1 - side] = by_x[rows:, :width]
    x_block[...] = by_x[:rows, :]
    for at, block in enumerate((out_own, out1, out2, out3)):
        outs[at] = block[...]


def complete_body(
    bundle, level3, level2, level1, message, x_block, by_y, by_xy, outs, crossed, gains, *results
):
    del gains
    weights, near, both = results
    rows = x_block.shape[0]
    for at, block in enumerate((bundle, level1, level2, level3)):
        weights[at] = block[...]
    for at, block in enumerate((message, x_block, by_y, by_xy)):
        near[at] = block[:rows, :]
    both[0] = outs[...]
    both[1] = crossed[...]


def pair_away(flip):
    pair = lax.rem(lax.axis_index("lat") // 2, 4)
    high, low = pair // 2, pair % 2
    high = 1 - high if flip // 2 else high
    low = 1 - low if flip % 2 else low
    return 2 * high + low


def join_bundles(mine, other, joined):
    core = lax.axis_index("lon")
    half = mine.shape[2]
    for flip in range(4):
        for block, at in ((mine, core), (other, 1 - core)):
            for row in range(2):
                first = pl.multiple_of(((pair_away(flip) * 2 + row) * 2 + at) * half, half)
                joined[pl.ds(first, half), :] = block[flip, row]


def join_columns(mine, other, joined):
    core, side = lax.axis_index("lon"), lax.rem(lax.axis_index("lat"), 2)
    half = mine.shape[2]
    for flip in range(4):
        for block, at in ((mine, core), (other, 1 - core)):
            for cross, row in enumerate((side, 1 - side)):
                first = pl.multiple_of(((pair_away(flip) * 2 + row) * 2 + at) * half, half)
                joined[pl.ds(first, half), :] = block[cross, flip]


def attend_body(*refs):
    (near, far, mine, other), pieces = refs[:4], refs[4:8]
    weights, bias_rows, near_rows, far_rows = refs[8:]
    group, side = lax.axis_index("groups"), lax.rem(lax.axis_index("lat"), 2)
    _, count, quarter = pieces[0].shape
    heads = 3
    head_dim = quarter // heads
    join_bundles(mine, other, weights)
    for slot in range(4):
        near_rows[slot * count : (slot + 1) * count, :] = near[slot, :count, :]
        far_rows[slot * count : (slot + 1) * count, :] = far[slot, :count, :]
    for flip in range(2):
        for at, block in enumerate((near, far)):
            bias_rows[flip, :, at * count : (at + 1) * count] = block[flip, count:, :count].astype(
                F32
            )
    first_head = (2 * side + group) * heads
    here = jnp.dot(near_rows[...], weights[...], preferred_element_type=F32).astype(BF16)
    there = jnp.dot(far_rows[...], weights[:, quarter:], preferred_element_type=F32).astype(BF16)
    for slot in range(4):
        flip, sample = slot % 2, slot // 2
        low_row, high_row = slot * count, (slot + 1) * count
        outs = []
        for head in range(heads):
            low = head * head_dim
            queries = here[low_row:high_row, low : low + head_dim]
            keys, values = (
                jnp.concatenate(
                    [
                        here[low_row:high_row, (kind + 1) * quarter + low :][:, :head_dim],
                        there[low_row:high_row, kind * quarter + low :][:, :head_dim],
                    ]
                )
                for kind in range(2)
            )
            scores = lax.dot_general(
                queries, keys, (((1,), (1,)), ((), ())), preferred_element_type=F32
            ) * (head_dim**-0.5)
            scores = scores + bias_rows[flip, pl.ds(first_head + head, 1), :]
            expd = jnp.exp(scores - jnp.max(scores, axis=-1, keepdims=True))
            totals = jnp.sum(expd, axis=-1, keepdims=True)
            weighted = jnp.dot(expd.astype(BF16), values, preferred_element_type=F32)
            outs.append((weighted / totals).astype(BF16))
        attended = jnp.concatenate(outs, axis=1)
        pieces[2 * sample + flip][0] = attended
        pieces[2 * sample + 1 - flip][1] = attended


def project_out(which, pieces, weights, tokens, gain):
    group, side = lax.axis_index("groups"), lax.rem(lax.axis_index("lat"), 2)
    summed = tokens.astype(F32)
    for slot, piece in enumerate(pieces):
        flip, sample = slot % 2, slot // 2
        quarter = piece.shape[2]
        owner = 2 * (side + flip - 2 * side * flip) + (group + sample - 2 * group * sample)
        rows = pl.ds(pl.multiple_of(owner * quarter, quarter), quarter)
        summed = summed + jnp.dot(piece[which], weights[rows, :], preferred_element_type=F32)
    middle = summed.astype(BF16)
    return middle, norm_rows(middle.astype(F32), gain)


def other_body(gain, piece3, piece2, piece1, piece0, weights, tokens, other_in):
    pieces = (piece0, piece1, piece2, piece3)
    other_in[...] = project_out(1, pieces, weights, tokens[...], gain[...])[1]


def tent_pair(row_count, first_col, col_count, half_width):
    rows = lax.broadcasted_iota(jnp.int32, (row_count, col_count), 0)
    cols = lax.broadcasted_iota(jnp.int32, (row_count, col_count), 1) + first_col
    offset = ((cols - rows + row_count // 2) & (row_count - 1)) - row_count // 2
    distance = jnp.abs(offset).astype(F32)
    span_plus = (half_width + 1).astype(F32)
    tent = jnp.where(
        distance <= half_width.astype(F32), (1.0 - distance / span_plus) / span_plus, 0.0
    )
    odd = tent * offset.astype(F32) / span_plus
    return tent.astype(BF16), odd.astype(BF16)


def mix(lines, blocks, basis):
    size = blocks.shape[2]
    return jnp.concatenate(
        [
            jnp.dot(
                lines[:, tile * size : (tile + 1) * size],
                blocks[basis, tile],
                preferred_element_type=F32,
            ).astype(BF16)
            for tile in range(blocks.shape[1])
        ],
        axis=1,
    )


def plan_body(
    lat_count, lon_half, lat_half, quad_off, taps, w_conv, message, blocks, coeffs, gains
):
    del message
    lat_row, core = lax.axis_index("lat"), lax.axis_index("lon")
    side = lax.rem(lat_row, 2)
    for basis in range(2):
        below, centre, above = (taps[quad_off[0] + row, basis] for row in range(3))
        below = jnp.where(lat_half[0] >= 1, below, 0.0)
        above = jnp.where(lat_half[0] >= 1, above, 0.0)
        other = jnp.where(side == 0, above, below)
        halo = jnp.where(side == 0, below, above)
        pole = jnp.where(lat_row == 0, below, 0.0) + jnp.where(
            lat_row == lat_count - 1, above, 0.0
        )
        for at, value in enumerate((other, centre, halo, pole)):
            gains[4 * basis + at : 4 * basis + at + 1, :] = jnp.full((1, 128), value, F32)
    rows, count = coeffs.shape[0], coeffs.shape[1] // 4
    direct = tent_pair(rows, core * count, count, lon_half[0])
    rolled = tent_pair(rows, core * count + count, count, lon_half[0])
    for at, part in enumerate((direct[0], direct[1], rolled[0], rolled[1])):
        coeffs[:, at * count : (at + 1) * count] = part
    size = w_conv.shape[2]
    blocks[...] = jnp.zeros(blocks.shape, BF16)
    per_block = blocks.shape[2] // size
    for basis in range(blocks.shape[0]):
        for tile in range(blocks.shape[1]):
            for at in range(per_block):
                first = (tile * per_block + at) * size
                low, high = at * size, (at + 1) * size
                blocks[basis, tile, low:high, low:high] = w_conv[basis, first : first + size, :]


def own_body(
    gains,
    gain,
    piece3,
    piece2,
    piece1,
    piece0,
    weights,
    tokens,
    other_in,
    blocks,
    coeffs,
    middle,
    partial,
):
    count = tokens.shape[0]
    pieces = (piece0, piece1, piece2, piece3)
    own_middle, own_in = project_out(0, pieces, weights, tokens[...], gain[...])
    middle[...] = own_middle
    own = own_in.astype(F32)
    neighbour = other_in[...].astype(F32)
    direct, rolled = [], []
    for basis in range(2):
        other, centre, _, pole = (gains[4 * basis + at : 4 * basis + at + 1, :1] for at in range(4))
        lines = jnp.concatenate(
            [(other * neighbour + centre * own).astype(BF16), (pole * own).astype(BF16)]
        )
        mixed = mix(lines, blocks, basis)
        direct.append(mixed[:count])
        rolled.append(mixed[count:])
    partial[...] = jnp.dot(
        coeffs[...], jnp.concatenate(direct + rolled), preferred_element_type=F32
    )


def halo_body(gains, halo, blocks, coeffs, middle, partial, kept, sent, total):
    core = lax.axis_index("lon")
    count = halo.shape[0]
    values = halo[...].astype(F32)
    mixed = [
        mix((gains[4 * basis + 2 : 4 * basis + 3, :1] * values).astype(BF16), blocks, basis)
        for basis in range(2)
    ]
    total[...] = partial[...] + jnp.dot(
        coeffs[:, : 2 * count], jnp.concatenate(mixed), preferred_element_type=F32
    )
    here = pl.multiple_of(core * count, count)
    there = pl.multiple_of((1 - core) * count, count)
    kept[...] = middle[...].astype(F32) + total[pl.ds(here, count), :]
    sent[...] = total[pl.ds(there, count), :].astype(BF16)


def pack_plain(weights, columns):
    core, lat_count = lax.axis_index("lon"), lax.axis_size("lat")
    half, width = weights.shape[0] // 2, weights.shape[1]
    rows = lax.dynamic_slice_in_dim(weights, core * half, half, 0)
    if columns == width:
        return jnp.broadcast_to(rows[None], (lat_count, half, columns))
    rows = rows.reshape(half, 3, 2, 2, columns // 3)
    rows = lax.dynamic_index_in_dim(rows, lax.axis_index("groups"), 3, keepdims=False)
    rows = rows.transpose(2, 0, 1, 3).reshape(2, half, columns)
    rows = jnp.broadcast_to(rows[None], (lat_count // 2, 2, half, columns))
    return rows.reshape(lat_count, half, columns)


def gather_plain(weights, columns):
    core = lax.axis_index("lon")
    mine = lax.all_to_all(pack_plain(weights, columns), "lat", 0, 0)
    other = swap_cores(mine)
    both = jnp.where(core == 0, jnp.stack([mine, other], 1), jnp.stack([other, mine], 1))
    whole = both.reshape(4, 2, 2, -1, columns)
    pair = lax.rem(lax.axis_index("lat") // 2, 4)
    whole = jnp.stack(
        [lax.dynamic_index_in_dim(whole, pair ^ flip, 0, keepdims=False) for flip in range(4)]
    )
    return [
        lax.dynamic_index_in_dim(whole, at, 2, keepdims=False) for at in (core, 1 - core)
    ]


def flip_levels(bundle):
    moved = [move(bundle, lambda g, l, c: (g, l ^ (2 * flip), c)) for flip in (3, 2, 1)]
    return moved[::-1]


def per_device(
    tokens,
    gain_attn,
    w_qkv,
    key_bias,
    w_out,
    gain_conv,
    w_conv,
    lat_taps,
    lon_half,
    lat_half,
    quad_off,
):
    own_tokens = tokens[0]
    count, width = own_tokens.shape
    quarter = width // 4
    lat_count = lax.axis_size("lat")
    half = w_qkv.shape[0] // 2
    gain_conv = gain_conv[None]

    direct = half % 16 == 0 and lat_count == 8
    rows = count + 16
    message, raw_tokens, out_own = call(
        functools.partial(pack_body, weights=direct),
        [
            ((rows + (half if direct else 0), width), BF16),
            ((count, width), BF16),
            ((half, width), BF16),
        ],
        [HBM] * (5 if direct else 3),
        (own_tokens, key_bias[0], gain_attn) + ((w_qkv, w_out) if direct else ()),
        10 * count * width,
        [
            pltpu.VMEM(key_bias.shape[1:], BF16),
            pltpu.VMEM((width,), F32),
            pltpu.VMEM((half, 3 * width), BF16),
            pltpu.SemaphoreType.DMA((5,)),
        ],
        limit=56,
    )

    by_x, by_y = flip_chips(message, 1, 0), flip_chips(message, 0, 1)
    x_block = by_x
    if direct:
        levels = flip_levels(out_own)
        qkv_own, out_own = call(
            columns_body,
            [((half, 3 * quarter), BF16), ((half, width), BF16)],
            [VMEM] * 2,
            (w_qkv, w_out),
            0,
        )
        bundle, x_block, outs = call(
            arrived_body,
            [
                ((2, half, 3 * quarter), BF16),
                ((rows, width), BF16),
                ((4, half, width), BF16),
            ],
            [VMEM] * 7,
            (qkv_own, by_x, by_y, out_own, *levels[::-1]),
            0,
        )
    size = 4 * w_conv.shape[2]
    diagonal, coeffs, gains = call(
        functools.partial(plan_body, lat_count),
        [
            ((2, width // size, size, size), BF16),
            ((2 * count, 4 * count), BF16),
            ((8, 128), F32),
        ],
        [SMEM] * 4 + [VMEM, ANY],
        (lon_half, lat_half, quad_off, lat_taps, w_conv, x_block),
        0,
    )
    if direct:
        qkv_mine, near, out_mine = call(
            complete_body,
            [
                ((4, 2, half, 3 * quarter), BF16),
                ((4, rows, width), BF16),
                ((2, 4, half, width), BF16),
            ],
            [VMEM] * 11,
            (
                bundle,
                *flip_levels(bundle)[::-1],
                message,
                x_block,
                by_y,
                flip_chips(x_block, 0, 1),
                outs,
                flip_chips(outs, 1, 0),
                gains,
            ),
            0,
        )
        qkv_other = swap_cores(qkv_mine)
        join = join_columns
    else:
        near = jnp.stack([message, by_x, by_y, flip_chips(by_x, 0, 1)])
        qkv_mine, qkv_other = gather_plain(w_qkv, 3 * quarter)
        out_mine, out_other = gather_plain(w_out, width)
        join = join_bundles
    far = swap_cores(near)
    raw_tokens = gate(raw_tokens, qkv_mine)
    other_tokens = flip_chips(raw_tokens, 1, 0)

    pieces = call(
        attend_body,
        [((2, count, quarter), BF16)] * 4,
        [VMEM] * 4,
        (near, far, qkv_mine, qkv_other),
        2 * 1024 * width * 3 * quarter,
        [
            pltpu.VMEM((width, 3 * quarter), BF16),
            pltpu.VMEM((2, 16, 2 * count), F32),
            pltpu.VMEM((4 * count, width), BF16),
            pltpu.VMEM((4 * count, width), BF16),
        ],
    )
    back = [
        flip_chips(piece, flip, sample) for piece, (flip, sample) in zip(pieces[:0:-1], FLIPS[::-1])
    ]
    back = [pieces[0]] + back[::-1]
    if direct:
        out_mine = gate(out_mine, pieces[0])
        out_other = swap_cores(out_mine)
    (full_out,) = call(
        join, [((width, width), BF16)], [VMEM] * 2, (out_mine, out_other), 0
    )
    (other_in,) = call(
        other_body,
        [((count, width), BF16)],
        [VMEM] * 7,
        (gain_conv, *back[::-1], full_out, other_tokens),
        2 * count * width * width,
    )
    halo = move(other_in, lambda g, l, c: (g, l + 2 - 4 * (l % 2), c))
    middle, partial = call(
        own_body,
        [((count, width), BF16), ((2 * count, width), F32)],
        [VMEM] * 11,
        (gains, gain_conv, *back[::-1], full_out, raw_tokens, other_in, diagonal, coeffs),
        2 * count * width * width * 3,
    )
    kept, sent = call(
        halo_body,
        [((count, width), F32), ((count, width), BF16)],
        [VMEM] * 6,
        (gains, halo, diagonal, coeffs, middle, partial),
        2 * 256 * 256 * width,
        [pltpu.VMEM((2 * count, width), F32)],
    )
    received = swap_cores(sent)
    return (kept + received.astype(F32)).astype(BF16)[None]


def solution(mesh):
    return jax.shard_map(
        per_device,
        mesh=mesh,
        in_specs=(
            P(("groups", "lat"), "lon", None),
            P(),
            P("lat", None),
            P("lat", None, "lon"),
            P("lat", None),
            P(),
            P(),
            P(),
            P("lat"),
            P("lat"),
            P("lat"),
        ),
        out_specs=P(("groups", "lat"), "lon", None),
        check_vma=False,
    )
```
